32 devices in a mesh: col: 8 (over z, x), row: 4 (over y, core).
Axes of the slice: x: 2, y: 2, z: 4, core: 2. Of those that a mesh axis runs over, the one named last changes fastest.
Arguments:
- trailing: float32 [12288, 4096], P('row', 'col'), may hold values from -6 to 6
- panel_rows: float32 [12288, 512], P(('row', 'col')), may hold values from -6 to 6
- pivot_block: float32 [512, 512], P('col'), as said below
- panel_fill: int32 [48, 2], replicated, may hold values 0 or 1
Outputs:
- updated: float32 [12288, 4096], P('row', 'col')
- panel_factor: float32 [12288, 512], P(('row', 'col'))
The draws below stay inside these ranges and needn't reach their ends.
Inputs may be any that keep to these rules, and one draw needn't show every extreme that they name: `pivot_block`: Symmetric; each diagonal entry exceeds the sum of the magnitudes of the other entries of its row by at least 1. `panel_fill`: each entry is 1 with probability 0.15, independently of the others.
All inputs are finite; a program needn't handle non-finite values.
Results may differ from the reference program's by a relative error of at most 0.00008.
Values sent between devices are 32-bit elements; how exact they have to be, the bound alone decides.
No kernel may reach another device: no remote copies, remote signals or barrier semaphores. Data moves between devices by JAX's collectives and lax.ppermute only.
A program may use at most 128 MiB of HBM per device.

```python
import jax
import jax.numpy as jnp
from jax import lax

B = 256
NR = 48
NC = 16


def draw_pivot_block(key, part):
    pivot_order = 2 * B
    first_key, second_key = jax.random.split(jax.random.fold_in(key, 17))
    spread = 8.0
    diag_extra = jax.random.uniform(second_key, (pivot_order,), jnp.float32, 1.0, 2.0)
    magnitudes = jax.random.uniform(first_key, (pivot_order, pivot_order), jnp.float32, 0.6, 1.0) * (spread / pivot_order)
    upper_part = jnp.triu(magnitudes, 1)
    coupling = -(upper_part + upper_part.T)
    identity = jnp.eye(pivot_order, dtype=jnp.float32)
    return coupling + identity * (spread + diag_extra)[None, :]


def set_ends(array, key, least, high):
    index_at = [jax.random.randint(jax.random.fold_in(key, axis), (), 0, length) for axis, length in enumerate(array.shape)]
    main_axis = array.shape.index(max(array.shape))
    next_to = index_at[:main_axis] + [(index_at[main_axis] + 1) % array.shape[main_axis]] + index_at[main_axis + 1:]
    return array.at[tuple(index_at)].set(least).at[tuple(next_to)].set(high)


def block_scale(rng, shape, shards, low, top_value):
    gain, own = 1.0, jax.random.fold_in(rng, 6)
    for dim, shards_of in shards:
        steps = jnp.exp(jax.random.uniform(jax.random.fold_in(own, dim), (shards_of,), jnp.float32, low / len(shards), top_value / len(shards)))
        gain = gain * jnp.repeat(steps, shape[dim] // shards_of).reshape([-1 if axis == dim else 1 for axis in range(len(shape))])
    return gain


def noise(stream_key, dims, scale, reach, shards=(), kind=jnp.bfloat16):
    drawn = jax.random.normal(stream_key, dims, jnp.float32) * scale
    if len(shards) > 0:
        drawn = block_scale(stream_key, dims, shards, -0.22, 0.18) * drawn
    return jnp.clip(drawn, min=-reach, max=reach).astype(kind)


def setup_inputs(seed: int = 0) -> dict:
    arg_keys = jax.random.split(jax.random.key(seed), 5)
    trailing = noise(arg_keys[0], (NR * B, NC * B), 1.0, 6.0, ((0, 4), (1, 8)), jnp.float32)
    panel_rows = noise(arg_keys[1], (NR * B, 2 * B), 1.0, 6.0, ((0, 32),), jnp.float32)
    pivot_block = draw_pivot_block(jax.random.fold_in(arg_keys[4], 71), 0)
    panel_fill = set_ends((jax.random.randint(arg_keys[3], (NR, 2), 0, 20) < 3).astype(jnp.int32), jax.random.fold_in(arg_keys[3], 1), 0, 1)
    return {"trailing": trailing, "panel_rows": panel_rows, "pivot_block": pivot_block, "panel_fill": panel_fill}


def reference(trailing, panel_rows, pivot_block, panel_fill):
    flags = jnp.repeat(panel_fill.astype(jnp.float32), B, axis=0)
    total_rows = panel_rows.shape[0]
    masked = (panel_rows.reshape(total_rows, 2, B) * flags[:, :, None]).reshape(total_rows, 2 * B)
    factor = jnp.linalg.cholesky(pivot_block)
    panel_factor = lax.linalg.triangular_solve(factor, masked, left_side=False, lower=True, transpose_a=True)
    columns = panel_factor[:trailing.shape[1]]
    update = lax.dot_general(panel_factor, columns, (((1,), (1,)), ((), ())), precision=lax.Precision.HIGHEST)
    updated = trailing - update
    return (updated, panel_factor)
```

```python
import functools
import math

import jax
import jax.numpy as jnp
from jax import lax
from jax.experimental import pallas as pl
from jax.experimental.pallas import tpu as pltpu
from jax.sharding import PartitionSpec as P

F32, BF16 = jnp.float32, jnp.bfloat16
VMEM = pl.BlockSpec(memory_space=pltpu.VMEM)
SMEM = pl.BlockSpec(memory_space=pltpu.SMEM)
ANY = pl.BlockSpec(memory_space=pl.ANY)
COARSE_STEPS = 2
FINE_STEPS = 16
RESIDUAL = 5e-4


def halves(value):
    high = value.astype(BF16)
    return high, (value - high.astype(F32)).astype(BF16)


def dot(a, b, dims):
    return lax.dot_general(a, b, (dims, ((), ())), preferred_element_type=F32)


NN, NT, TN = ((1,), (0,)), ((1,), (1,)), ((0,), (0,))


def dot3(a, b, dims):
    (ah, al), (bh, bl) = a, b
    return dot(ah, bh, dims) + (dot(ah, bl, dims) + dot(al, bh, dims))


def inverse_factor_kernel(a_ref, w_ref, s_ref, flag):
    n = a_ref.shape[0]
    rows = lax.broadcasted_iota(jnp.int32, (n, n), 0)
    cols = lax.broadcasted_iota(jnp.int32, (n, n), 1)
    eye = (rows == cols).astype(F32)
    take = jnp.where(rows > cols, 1.0, 0.5 * eye)
    a = a_ref[...]
    diag_row = jnp.sum(a * eye, axis=0, keepdims=True)
    diag_col = jnp.sum(a * eye, axis=1, keepdims=True)
    scale_row, scale_col = lax.rsqrt(diag_row), lax.rsqrt(diag_col)
    scaled = jnp.where(rows == cols, 1.0, a * scale_row * scale_col)
    s_ref[...] = scaled
    scaled_parts = halves(scaled)
    w = eye - take * (scaled - eye)
    for _ in range(COARSE_STEPS):
        wh = w.astype(BF16)
        t = dot(wh, scaled_parts[0], NN).astype(BF16)
        change = take * (dot(t, wh, NT) - eye)
        w = w - dot(change.astype(BF16), wh, NN)
    w_ref[...] = w
    flag[0] = 0

    def fine(state):
        step, _ = state
        w = w_ref[...]
        parts = halves(w)
        t = halves(dot3(parts, halves(s_ref[...]), NN))
        residual = dot3(t, parts, NT) - eye
        w_ref[...] = w - dot((take * residual).astype(BF16), parts[0], NN)
        return step + 1, jnp.sum(residual * residual)

    _, left = lax.while_loop(
        lambda state: jnp.logical_and(state[0] < FINE_STEPS, jnp.logical_not(state[1] < RESIDUAL**2)),
        fine,
        (jnp.int32(0), jnp.float32(1.0)),
    )
    done = left < RESIDUAL**2

    @pl.when(jnp.logical_not(done))
    def _():
        w_ref[...] = eye

        def eliminate(j, carry):
            row = s_ref[pl.ds(j, 1), :]
            pick = lax.broadcasted_iota(jnp.int32, (1, n), 1) == j
            pivot = jnp.sum(jnp.where(pick, row, 0.0), axis=1, keepdims=True)
            column = jnp.sum(jnp.where(pick, s_ref[...], 0.0), axis=1, keepdims=True)
            below = lax.broadcasted_iota(jnp.int32, (n, 1), 0) > j
            ratio = jnp.where(below, column / pivot, 0.0)
            s_ref[...] = s_ref[...] - ratio * row
            w_ref[...] = w_ref[...] - ratio * w_ref[pl.ds(j, 1), :]
            return carry

        lax.fori_loop(0, n, eliminate, 0)
        pivots = jnp.sum(s_ref[...] * eye, axis=1, keepdims=True)
        w_ref[...] = w_ref[...] * lax.rsqrt(pivots)

    w_ref[...] = w_ref[...] * scale_row


def inverse_factor(pivot):
    n = pivot.shape[0]
    return pl.pallas_call(
        inverse_factor_kernel,
        out_shape=jax.ShapeDtypeStruct((n, n), F32),
        in_specs=[VMEM],
        out_specs=VMEM,
        scratch_shapes=[pltpu.VMEM((n, n), F32), pltpu.SMEM((1,), jnp.int32)],
        compiler_params=pltpu.CompilerParams(vmem_limit_bytes=32 * 2**20),
        cost_estimate=pl.CostEstimate(flops=40 * n**3, bytes_accessed=8 * n * n, transcendentals=0),
    )(pivot)


class Sizes:
    def __init__(self, trailing, panel_rows, panel_fill):
        self.cols, self.rows = lax.axis_size("col"), lax.axis_size("row")
        self.block = panel_rows.shape[1] // 2
        self.piece = panel_rows.shape[0]
        self.unit = math.gcd(self.piece, self.block)
        self.per_piece = self.piece // self.unit
        self.per_block = self.block // self.unit
        self.slab = self.piece * self.cols
        self.width = trailing.shape[1]
        self.tiles = self.cols * self.per_piece

    def source(self, c):
        slab = c * self.width // self.slab
        return slab, (c * self.width - slab * self.slab) // self.piece

    def sources(self):
        found = []
        for c in range(self.cols):
            slab, first = self.source(c)
            last = ((c + 1) * self.width - 1 - slab * self.slab) // self.piece
            found.append(last - first + 1)
        return found


def unit_flag(sizes, fill_ref, piece_index, unit, panel):
    block = (piece_index * sizes.per_piece + unit) // sizes.per_block
    return fill_ref[block * 2 + panel]


def pack_kernel(sizes, cap, where_ref, fill_ref, panel_ref, out_ref, sems):
    piece = where_ref[1] * sizes.cols + where_ref[0]
    slot = jnp.int32(0)
    started = []
    for u in range(sizes.per_piece):
        for p in range(2):
            flag = unit_flag(sizes, fill_ref, piece, u, p) != 0
            copy = pltpu.make_async_copy(
                panel_ref.at[pl.ds(u * sizes.unit, sizes.unit), pl.ds(p * sizes.block, sizes.block)],
                out_ref.at[jnp.minimum(slot, cap - 1)],
                sems.at[u * 2 + p],
            )
            keep = jnp.logical_and(flag, slot < cap)
            pl.when(keep)(copy.start)
            started.append((keep, copy))
            slot = slot + flag.astype(jnp.int32)
    for keep, copy in started:
        pl.when(keep)(copy.wait)


def pack(sizes, cap, where, fill, panel):
    return pl.pallas_call(
        functools.partial(pack_kernel, sizes, cap),
        out_shape=jax.ShapeDtypeStruct((cap, sizes.unit, sizes.block), F32),
        in_specs=[SMEM, SMEM, ANY],
        out_specs=ANY,
        scratch_shapes=[pltpu.SemaphoreType.DMA((2 * sizes.per_piece,))],
        cost_estimate=pl.CostEstimate(flops=0, bytes_accessed=2 * panel.size * 4, transcendentals=0),
    )(where, fill, panel)


def apply_factor_kernel(sizes, cap, lists, where_ref, fill_ref, w_ref, panel_ref, *refs):
    list_refs, (x_ref, high_ref, low_ref, masked, column) = refs[:lists], refs[lists:]
    c, r = where_ref[0], where_ref[1]
    own = r * sizes.cols + c
    for u in range(sizes.per_piece):
        for p in range(2):
            at = (pl.ds(u * sizes.unit, sizes.unit), pl.ds(p * sizes.block, sizes.block))
            flag = unit_flag(sizes, fill_ref, own, u, p) != 0
            masked[at] = jnp.where(flag, panel_ref[at], 0.0)
    w = halves(w_ref[...])
    x_ref[...] = dot3(halves(masked[...]), w, NT)
    column[...] = jnp.zeros_like(column)
    slab = c * sizes.width // sizes.slab
    first = (c * sizes.width - slab * sizes.slab) // sizes.piece
    for j, list_ref in enumerate(list_refs):
        piece = slab * sizes.cols + first + j
        inside = first + j < sizes.cols
        piece = jnp.where(inside, piece, 0)
        slot = jnp.int32(0)
        for u in range(sizes.per_piece):
            at_row = (piece * sizes.per_piece + u) * sizes.unit - c * sizes.width
            needed = jnp.logical_and(inside, jnp.logical_and(at_row >= 0, at_row < sizes.width))
            start = pl.multiple_of(jnp.where(needed, at_row, 0), sizes.unit)
            for p in range(2):
                flag = unit_flag(sizes, fill_ref, piece, u, p) != 0

                @pl.when(jnp.logical_and(flag, needed))
                def _(slot=slot, p=p, start=start, list_ref=list_ref):
                    column[pl.ds(start, sizes.unit), pl.ds(p * sizes.block, sizes.block)] = list_ref[
                        jnp.minimum(slot, cap - 1)
                    ]

                slot = slot + flag.astype(jnp.int32)
    solved = dot3(w, halves(column[...]), NT)
    high, low = halves(dot3(w, halves(solved), TN))
    high_ref[...] = high
    low_ref[...] = low


def apply_factor(sizes, cap, where, fill, w, panel, lists):
    n = w.shape[0]
    return pl.pallas_call(
        functools.partial(apply_factor_kernel, sizes, cap, len(lists)),
        out_shape=(
            jax.ShapeDtypeStruct(panel.shape, F32),
            jax.ShapeDtypeStruct((n, sizes.width), BF16),
            jax.ShapeDtypeStruct((n, sizes.width), BF16),
        ),
        in_specs=[SMEM, SMEM] + [VMEM] * (2 + len(lists)),
        out_specs=(VMEM, VMEM, VMEM),
        scratch_shapes=[pltpu.VMEM(panel.shape, F32), pltpu.VMEM((sizes.width, n), F32)],
        compiler_params=pltpu.CompilerParams(vmem_limit_bytes=40 * 2**20),
        cost_estimate=pl.CostEstimate(flops=16 * n**3, bytes_accessed=12 * n * n, transcendentals=0),
    )(where, fill, w, panel, *lists)


def update_kernel(sizes, cap, where_ref, fill_ref, high_ref, low_ref, window_ref, *refs):
    lists, (out_ref, tiles, units, in_sems, unit_sems, out_sems) = refs[: sizes.cols], refs[sizes.cols :]
    c, r = where_ref[0], where_ref[1]

    def place(k):
        return jnp.bitwise_xor(c, k)

    def flags_of(t):
        piece = r * sizes.cols + place(t // sizes.per_piece)
        return [unit_flag(sizes, fill_ref, piece, t % sizes.per_piece, p) != 0 for p in range(2)]

    def rows_of(t):
        start = (place(t // sizes.per_piece) * sizes.per_piece + t % sizes.per_piece) * sizes.unit
        return pl.ds(pl.multiple_of(start, sizes.unit), sizes.unit)

    def tile_in(t):
        return pltpu.make_async_copy(window_ref.at[rows_of(t)], tiles.at[t], in_sems.at[t])

    def tile_out(t):
        return pltpu.make_async_copy(tiles.at[t], out_ref.at[rows_of(t)], out_sems.at[t])

    for k in range(sizes.cols):
        slot = jnp.int32(0)
        for u in range(sizes.per_piece):
            t = k * sizes.per_piece + u
            flags = flags_of(t)
            pl.when(jnp.logical_or(*flags))(tile_in(t).start)
            for p in range(2):
                copy = pltpu.make_async_copy(
                    lists[k].at[jnp.minimum(slot, cap - 1)], units.at[t, p], unit_sems.at[t, p]
                )
                pl.when(flags[p])(copy.start)
                slot = slot + flags[p].astype(jnp.int32)

    @pl.loop(0, sizes.tiles)
    def _(t):
        flags = flags_of(t)

        @pl.when(jnp.logical_or(*flags))
        def _():
            tile_in(t).wait()
            for p in range(2):

                @pl.when(flags[p])
                def _(p=p):
                    pltpu.make_async_copy(lists[0].at[0], units.at[t, p], unit_sems.at[t, p]).wait()
                    at = pl.ds(p * sizes.block, sizes.block)
                    right = (high_ref[at, :], low_ref[at, :])
                    tiles[t] = tiles[t] - dot3(halves(units[t, p]), right, NN)

            tile_out(t).start()

    @pl.loop(0, sizes.tiles)
    def _(t):
        pl.when(jnp.logical_or(*flags_of(t)))(tile_out(t).wait)


def update(sizes, cap, where, fill, high, low, window, lists):
    tiles = sizes.tiles
    return pl.pallas_call(
        functools.partial(update_kernel, sizes, cap),
        out_shape=jax.ShapeDtypeStruct(window.shape, F32),
        in_specs=[SMEM, SMEM, VMEM, VMEM] + [ANY] * (1 + len(lists)),
        out_specs=ANY,
        input_output_aliases={4: 0},
        scratch_shapes=[
            pltpu.VMEM((tiles, sizes.unit, sizes.width), F32),
            pltpu.VMEM((tiles, 2, sizes.unit, sizes.block), F32),
            pltpu.SemaphoreType.DMA((tiles,)),
            pltpu.SemaphoreType.DMA((tiles, 2)),
            pltpu.SemaphoreType.DMA((tiles,)),
        ],
        compiler_params=pltpu.CompilerParams(vmem_limit_bytes=32 * 2**20),
        cost_estimate=pl.CostEstimate(flops=10**9, bytes_accessed=6 * 10**6, transcendentals=0),
    )(where, fill, high, low, window, *lists)


def swap(value, axis, step):
    size = lax.axis_size(axis)
    return lax.ppermute(value, axis, [(i, i ^ step) for i in range(size)])


def doubled(value, axis):
    size, step = lax.axis_size(axis), 1
    index = lax.axis_index(axis)
    while step < size:
        other = swap(value, axis, step)
        second = (index & step) != 0
        value = jnp.where(
            second, jnp.concatenate([other, value], 0), jnp.concatenate([value, other], 0)
        )
        step *= 2
    return value


def gather_pivot(pivot_block):
    share = pivot_block.shape[0] // lax.axis_size("row")
    own = lax.dynamic_slice_in_dim(pivot_block, lax.axis_index("row") * share, share, 0)
    cols, rows = lax.axis_size("col"), lax.axis_size("row")
    by_col = doubled(own[None], "col")
    both = doubled(by_col[None], "row")
    return both.transpose(1, 0, 2, 3).reshape(cols * rows * share, -1)


def gather_lists(own, cols):
    found = [own] + [swap(own, "col", k) for k in range(2, cols, 2)]
    lists = []
    for value in found:
        lists += [value, swap(value, "col", 1)]
    return lists


def gather_column(sizes, own):
    counts = sizes.sources()
    r, c = lax.axis_index("row"), lax.axis_index("col")
    target = c * sizes.width // sizes.slab
    values = []
    for j in range(max(counts)):
        pairs = []
        for at in range(sizes.cols):
            slab, first = sizes.source(at)
            if j < counts[at]:
                pairs.append(((first + j) * sizes.rows + slab, at * sizes.rows + slab))
        values.append(lax.ppermute(own, ("col", "row"), pairs))
    value = jnp.stack(values)
    step = sizes.rows // 2
    while step:
        other = swap(value, "row", step)
        value = jnp.where(((r ^ target) & step) != 0, other, value)
        step //= 2
    return [value[j] for j in range(max(counts))]


def per_device(trailing, panel_rows, pivot_block, panel_fill):
    sizes = Sizes(trailing, panel_rows, panel_fill)
    cap = 2 * sizes.per_piece
    fill = panel_fill.reshape(-1)
    where = jnp.stack([lax.axis_index("col"), lax.axis_index("row")]).astype(jnp.int32)
    own = pack(sizes, cap, where, fill, panel_rows)
    pivot = gather_pivot(pivot_block)
    column = gather_column(sizes, own)
    lists = gather_lists(own, sizes.cols)
    w = inverse_factor(pivot)
    own_factor, high, low = apply_factor(sizes, cap, where, fill, w, panel_rows, column)
    updated = update(sizes, cap, where, fill, high, low, trailing, lists)
    return updated, own_factor


def solution(mesh):
    in_specs = (P("row", "col"), P(("row", "col"), None), P("col", None), P())
    out_specs = (P("row", "col"), P(("row", "col"), None))
    return jax.shard_map(
        per_device, mesh=mesh, in_specs=in_specs, out_specs=out_specs, check_vma=False
    )
```

```python
import functools
import math

import jax
import jax.numpy as jnp
from jax import lax
from jax.experimental import pallas as pl
from jax.experimental.pallas import tpu as pltpu
from jax.sharding import PartitionSpec as P

F32, BF16 = jnp.float32, jnp.bfloat16
VMEM = pl.BlockSpec(memory_space=pltpu.VMEM)
SMEM = pl.BlockSpec(memory_space=pltpu.SMEM)
ANY = pl.BlockSpec(memory_space=pl.ANY)
COARSE_STEPS = 2
FINE_STEPS = 16
RESIDUAL = 5e-4


def halves(value):
    high = value.astype(BF16)
    return high, (value - high.astype(F32)).astype(BF16)


def dot(a, b, dims):
    return lax.dot_general(a, b, (dims, ((), ())), preferred_element_type=F32)


NN, NT, TN = ((1,), (0,)), ((1,), (1,)), ((0,), (0,))


def dot3(a, b, dims):
    (ah, al), (bh, bl) = a, b
    return dot(ah, bh, dims) + (dot(ah, bl, dims) + dot(al, bh, dims))


def inverse_factor_kernel(a_ref, w_ref, s_ref, flag):
    n = a_ref.shape[0]
    rows = lax.broadcasted_iota(jnp.int32, (n, n), 0)
    cols = lax.broadcasted_iota(jnp.int32, (n, n), 1)
    eye = (rows == cols).astype(F32)
    take = jnp.where(rows > cols, 1.0, 0.5 * eye)
    a = a_ref[...]
    diag_row = jnp.sum(a * eye, axis=0, keepdims=True)
    diag_col = jnp.sum(a * eye, axis=1, keepdims=True)
    scale_row, scale_col = lax.rsqrt(diag_row), lax.rsqrt(diag_col)
    scaled = jnp.where(rows == cols, 1.0, a * scale_row * scale_col)
    s_ref[...] = scaled
    scaled_parts = halves(scaled)
    w = eye - take * (scaled - eye)
    for _ in range(COARSE_STEPS):
        wh = w.astype(BF16)
        t = dot(wh, scaled_parts[0], NN).astype(BF16)
        change = take * (dot(t, wh, NT) - eye)
        w = w - dot(change.astype(BF16), wh, NN)
    w_ref[...] = w
    flag[0] = 0

    def fine(state):
        step, _ = state
        w = w_ref[...]
        parts = halves(w)
        t = halves(dot3(parts, halves(s_ref[...]), NN))
        residual = dot3(t, parts, NT) - eye
        w_ref[...] = w - dot((take * residual).astype(BF16), parts[0], NN)
        return step + 1, jnp.sum(residual * residual)

    _, left = lax.while_loop(
        lambda state: jnp.logical_and(state[0] < FINE_STEPS, jnp.logical_not(state[1] < RESIDUAL**2)),
        fine,
        (jnp.int32(0), jnp.float32(1.0)),
    )
    done = left < RESIDUAL**2

    @pl.when(jnp.logical_not(done))
    def _():
        w_ref[...] = eye

        def eliminate(j, carry):
            row = s_ref[pl.ds(j, 1), :]
            pick = lax.broadcasted_iota(jnp.int32, (1, n), 1) == j
            pivot = jnp.sum(jnp.where(pick, row, 0.0), axis=1, keepdims=True)
            column = jnp.sum(jnp.where(pick, s_ref[...], 0.0), axis=1, keepdims=True)
            below = lax.broadcasted_iota(jnp.int32, (n, 1), 0) > j
            ratio = jnp.where(below, column / pivot, 0.0)
            s_ref[...] = s_ref[...] - ratio * row
            w_ref[...] = w_ref[...] - ratio * w_ref[pl.ds(j, 1), :]
            return carry

        lax.fori_loop(0, n, eliminate, 0)
        pivots = jnp.sum(s_ref[...] * eye, axis=1, keepdims=True)
        w_ref[...] = w_ref[...] * lax.rsqrt(pivots)

    w_ref[...] = w_ref[...] * scale_row


def inverse_factor(pivot):
    n = pivot.shape[0]
    return pl.pallas_call(
        inverse_factor_kernel,
        out_shape=jax.ShapeDtypeStruct((n, n), F32),
        in_specs=[VMEM],
        out_specs=VMEM,
        scratch_shapes=[pltpu.VMEM((n, n), F32), pltpu.SMEM((1,), jnp.int32)],
        compiler_params=pltpu.CompilerParams(vmem_limit_bytes=32 * 2**20),
    )(pivot)


class Sizes:
    def __init__(self, trailing, panel_rows, panel_fill):
        self.cols, self.rows = lax.axis_size("col"), lax.axis_size("row")
        self.block = panel_rows.shape[1] // 2
        self.piece = panel_rows.shape[0]
        self.unit = math.gcd(self.piece, self.block)
        self.per_piece = self.piece // self.unit
        self.per_block = self.block // self.unit
        self.slab = self.piece * self.cols
        self.width = trailing.shape[1]
        self.tiles = self.cols * self.per_piece

    def source(self, c):
        slab = c * self.width // self.slab
        return slab, (c * self.width - slab * self.slab) // self.piece

    def sources(self):
        found = []
        for c in range(self.cols):
            slab, first = self.source(c)
            last = ((c + 1) * self.width - 1 - slab * self.slab) // self.piece
            found.append(last - first + 1)
        return found


def unit_flag(sizes, fill_ref, piece_index, unit, panel):
    block = (piece_index * sizes.per_piece + unit) // sizes.per_block
    return fill_ref[block * 2 + panel] != 0


def pool_pieces(sizes, pool_row, pool_col):
    for core in range(2):
        for side in range(2):
            yield core, side, (pool_row * 2 + core) * sizes.cols + pool_col * 2 + side


def fits_kernel(sizes, cap, fill_ref, out_ref):
    most = jnp.int32(0)
    for pool_row in range(sizes.rows // 2):
        for pool_col in range(sizes.cols // 2):
            count = jnp.int32(0)
            for _, _, piece in pool_pieces(sizes, pool_row, pool_col):
                for u in range(sizes.per_piece):
                    for p in range(2):
                        count = count + unit_flag(sizes, fill_ref, piece, u, p).astype(jnp.int32)
            most = jnp.maximum(most, count)
    out_ref[0] = (most <= cap).astype(jnp.int32)


def fits(sizes, cap, fill):
    return pl.pallas_call(
        functools.partial(fits_kernel, sizes, cap),
        out_shape=jax.ShapeDtypeStruct((1,), jnp.int32),
        in_specs=[SMEM],
        out_specs=SMEM,
    )(fill)


def pack_kernel(sizes, cap, where_ref, fill_ref, panel_ref, side_ref, core_ref, out_ref, pool):
    c, r = where_ref[0], where_ref[1]
    side, core = c % 2, r % 2
    half, quarter = sizes.unit // 2, sizes.unit // 4
    own_at = pl.multiple_of(side * half + core * quarter, quarter)
    side_at = pl.multiple_of(core * quarter, quarter)
    for u in range(sizes.per_piece):
        pool[core, side, u] = panel_ref[u, pl.ds(own_at, quarter), :]
        pool[core, 1 - side, u] = side_ref[u, pl.ds(side_at, quarter), :]
        pool[1 - core, side, u] = core_ref[0, u]
        pool[1 - core, 1 - side, u] = core_ref[1, u]
    slot = jnp.int32(0)
    for core_at, side_at, piece in pool_pieces(sizes, r // 2, c // 2):
        for u in range(sizes.per_piece):
            for p in range(2):
                flag = unit_flag(sizes, fill_ref, piece, u, p)

                @pl.when(flag)
                def _(slot=slot, core_at=core_at, side_at=side_at, u=u, p=p):
                    out_ref[jnp.minimum(slot, cap - 1)] = pool[
                        core_at, side_at, u, :, p * sizes.block : (p + 1) * sizes.block
                    ]

                slot = slot + flag.astype(jnp.int32)


def pack(sizes, cap, where, fill, panel, from_side, from_core):
    quarter = sizes.unit // 4
    return pl.pallas_call(
        functools.partial(pack_kernel, sizes, cap),
        out_shape=jax.ShapeDtypeStruct((cap, quarter, sizes.block), F32),
        in_specs=[SMEM, SMEM, VMEM, VMEM, VMEM],
        out_specs=VMEM,
        scratch_shapes=[pltpu.VMEM((2, 2, sizes.per_piece, quarter, 2 * sizes.block), F32)],
        compiler_params=pltpu.CompilerParams(vmem_limit_bytes=16 * 2**20),
    )(where, fill, panel, from_side, from_core)


def apply_factor_kernel(
    sizes, where_ref, fill_ref, w_ref, panel_ref, column_ref, x_ref, high_ref, low_ref, slot_ref, masked, column
):
    c, r = where_ref[0], where_ref[1]

    def mask(source, target, first_unit, count):
        for u in range(count):
            for p in range(2):
                at = (pl.ds(u * sizes.unit, sizes.unit), pl.ds(p * sizes.block, sizes.block))
                flag = fill_ref[(first_unit + u) // sizes.per_block * 2 + p] != 0
                target[at] = jnp.where(flag, source[at], 0.0)

    mask(panel_ref, masked, (r * sizes.cols + c) * sizes.per_piece, sizes.per_piece)
    mask(column_ref, column, c * (sizes.width // sizes.unit), sizes.width // sizes.unit)
    w = halves(w_ref[...])
    x_ref[...] = dot3(halves(masked[...]), w, NT)
    solved = dot3(w, halves(column[...]), NT)
    high_ref[...], low_ref[...] = halves(dot3(w, halves(solved), TN))

    @pl.loop(0, sizes.cols // 2)
    def _(group):
        pool_col = jnp.bitwise_xor(c // 2, group)
        slot = jnp.int32(0)
        for core, side, piece in pool_pieces(sizes, r // 2, pool_col):
            for u in range(sizes.per_piece):
                for p in range(2):
                    flag = unit_flag(sizes, fill_ref, piece, u, p)

                    @pl.when(core == r % 2)
                    def _(slot=slot, flag=flag, side=side, u=u, p=p):
                        at = ((group * 2 + side) * sizes.per_piece + u) * 2 + p
                        slot_ref[at] = jnp.where(flag, slot, -1)

                    slot = slot + flag.astype(jnp.int32)


def apply_factor(sizes, where, fill, w, panel, column):
    n = w.shape[0]
    return pl.pallas_call(
        functools.partial(apply_factor_kernel, sizes),
        out_shape=(
            jax.ShapeDtypeStruct(panel.shape, F32),
            jax.ShapeDtypeStruct((n, sizes.width), BF16),
            jax.ShapeDtypeStruct((n, sizes.width), BF16),
            jax.ShapeDtypeStruct((2 * sizes.tiles,), jnp.int32),
        ),
        in_specs=[SMEM, SMEM, VMEM, VMEM, VMEM],
        out_specs=(VMEM, VMEM, VMEM, SMEM),
        scratch_shapes=[pltpu.VMEM(panel.shape, F32), pltpu.VMEM((sizes.width, n), F32)],
        compiler_params=pltpu.CompilerParams(vmem_limit_bytes=32 * 2**20),
    )(where, fill, w, panel, column)


def update_kernel(sizes, where_ref, slot_ref, high_ref, low_ref, window_ref, *refs):
    groups = sizes.cols // 2
    lists, (out_ref, tiles, unit_data, in_sems, out_sems) = refs[: 4 * groups], refs[4 * groups :]
    c, r = where_ref[0], where_ref[1]
    side, core = c % 2, r % 2
    per_group = 2 * sizes.per_piece
    quarter = sizes.unit // 4

    def rows_of(t):
        group = jnp.bitwise_xor(c // 2, t // per_group)
        return pl.ds(pl.multiple_of((group * per_group + t % per_group) * sizes.unit, sizes.unit), sizes.unit)

    def tile_in(t):
        return pltpu.make_async_copy(window_ref.at[rows_of(t)], tiles.at[t], in_sems.at[t])

    def tile_out(t):
        return pltpu.make_async_copy(tiles.at[t], out_ref.at[rows_of(t)], out_sems.at[t])

    def active(t):
        return jnp.logical_or(slot_ref[2 * t] >= 0, slot_ref[2 * t + 1] >= 0)

    @pl.loop(0, sizes.tiles)
    def _(t):
        pl.when(active(t))(tile_in(t).start)

    for group in range(groups):

        @pl.loop(group * per_group, (group + 1) * per_group)
        def _(t, group=group):
            @pl.when(active(t))
            def _():
                tile_in(t).wait()
                for p in range(2):
                    slot = slot_ref[2 * t + p]

                    @pl.when(slot >= 0)
                    def _(p=p, slot=slot):
                        for flip in range(4):
                            from_side = jnp.bitwise_xor(side, flip // 2)
                            from_core = jnp.bitwise_xor(core, flip % 2)
                            at = pl.multiple_of((from_side * 2 + from_core) * quarter, quarter)
                            unit_data[pl.ds(at, quarter), :] = lists[4 * group + flip][slot]
                        at = pl.ds(p * sizes.block, sizes.block)
                        right = (high_ref[at, :], low_ref[at, :])
                        tiles[t] = tiles[t] - dot3(halves(unit_data[...]), right, NN)

                tile_out(t).start()

    @pl.loop(0, sizes.tiles)
    def _(t):
        pl.when(active(t))(tile_out(t).wait)


def update(sizes, where, slots, high, low, window, lists):
    tiles = sizes.tiles
    return pl.pallas_call(
        functools.partial(update_kernel, sizes),
        out_shape=jax.ShapeDtypeStruct(window.shape, F32),
        in_specs=[SMEM, SMEM, VMEM, VMEM, ANY] + [VMEM] * len(lists),
        out_specs=ANY,
        input_output_aliases={4: 0},
        scratch_shapes=[
            pltpu.VMEM((tiles, sizes.unit, sizes.width), F32),
            pltpu.VMEM((sizes.unit, sizes.block), F32),
            pltpu.SemaphoreType.DMA((tiles,)),
            pltpu.SemaphoreType.DMA((tiles,)),
        ],
        compiler_params=pltpu.CompilerParams(vmem_limit_bytes=40 * 2**20),
    )(where, slots, high, low, window, *lists)


def swap(value, axis, step):
    size = lax.axis_size(axis)
    return lax.ppermute(value, axis, [(i, i ^ step) for i in range(size)])


def join(index, step, own, other):
    second = (index & step) != 0
    return jnp.where(second, jnp.concatenate([other, own], 0), jnp.concatenate([own, other], 0))


def gather_pivot(sizes, pivot_block):
    r, c = lax.axis_index("row"), lax.axis_index("col")
    share = pivot_block.shape[0] // 2
    value = lax.dynamic_slice_in_dim(pivot_block, r % 2 * share, share, 0)[None]
    step = 1
    while step < sizes.cols:
        value = join(c, step, value, swap(value, "col", step))
        step *= 2
    value = join(r, 1, value[None], swap(value[None], "row", 1))
    return value.transpose(1, 0, 2, 3).reshape(2 * sizes.cols * share, -1)


def gather_column(sizes, panel):
    counts = sizes.sources()
    r, c = lax.axis_index("row"), lax.axis_index("col")
    target = c * sizes.width // sizes.slab
    values = []
    for j in range(max(counts)):
        pairs = []
        for at in range(sizes.cols):
            slab, first = sizes.source(at)
            if j < counts[at]:
                pairs.append(((first + j) * sizes.rows + slab, at * sizes.rows + slab))
        values.append(lax.ppermute(panel, ("col", "row"), pairs))
    start = (c * sizes.width - target * sizes.slab) % sizes.piece
    value = lax.dynamic_slice_in_dim(jnp.concatenate(values, 0), start, sizes.width, 0)
    step = sizes.rows // 2
    while step:
        value = jnp.where(((r ^ target) & step) != 0, swap(value, "row", step), value)
        step //= 2
    return value


def gather_pool(sizes, panel):
    side, core = lax.axis_index("col") % 2, lax.axis_index("row") % 2
    half, quarter = sizes.unit // 2, sizes.unit // 4
    own = lax.dynamic_slice_in_dim(panel, side * half, half, 1)
    from_side = swap(lax.dynamic_slice_in_dim(panel, (1 - side) * half, half, 1), "col", 1)
    both = jnp.stack([own, from_side])
    from_core = swap(lax.dynamic_slice_in_dim(both, (1 - core) * quarter, quarter, 2), "row", 1)
    return from_side, from_core


def per_device(trailing, panel_rows, pivot_block, panel_fill):
    sizes = Sizes(trailing, panel_rows, panel_fill)
    fill = panel_fill.reshape(-1)
    where = jnp.stack([lax.axis_index("col"), lax.axis_index("row")]).astype(jnp.int32)
    units = panel_rows.reshape(sizes.per_piece, sizes.unit, -1)
    most = 8 * sizes.per_piece

    def run(cap, trailing, panel_rows, pivot_block, fill, units):
        from_side, from_core = gather_pool(sizes, units)
        own = pack(sizes, cap, where, fill, units, from_side, from_core)
        pivot = gather_pivot(sizes, pivot_block)
        column = gather_column(sizes, panel_rows)
        arrived = [own] + [swap(own, "col", k) for k in range(2, sizes.cols, 2)]
        pivot, trailing, *arrived = lax.optimization_barrier((pivot, trailing, *arrived))
        w = inverse_factor(pivot)
        own_factor, high, low, slots = apply_factor(sizes, where, fill, w, panel_rows, column)
        lists = []
        for value in arrived:
            other = swap(value, "col", 1)
            lists += [value, swap(value, "row", 1), other, swap(other, "row", 1)]
        return update(sizes, where, slots, high, low, trailing, lists), own_factor

    cap = most * 5 // 12
    operands = (trailing, panel_rows, pivot_block, fill, units)
    return lax.cond(
        fits(sizes, cap, fill)[0] != 0,
        functools.partial(run, cap),
        functools.partial(run, most),
        *operands,
    )


def solution(mesh):
    in_specs = (P("row", "col"), P(("row", "col"), None), P("col", None), P())
    out_specs = (P("row", "col"), P(("row", "col"), None))
    return jax.shard_map(
        per_device, mesh=mesh, in_specs=in_specs, out_specs=out_specs, check_vma=False
    )
```

```python
import functools
import math

import jax
import jax.numpy as jnp
from jax import lax
from jax.experimental import pallas as pl
from jax.experimental.pallas import tpu as pltpu
from jax.sharding import PartitionSpec as P

F32, BF16 = jnp.float32, jnp.bfloat16
VMEM = pl.BlockSpec(memory_space=pltpu.VMEM)
SMEM = pl.BlockSpec(memory_space=pltpu.SMEM)
ANY = pl.BlockSpec(memory_space=pl.ANY)
COARSE_STEPS = 2
FINE_STEPS = 16
RESIDUAL = 5e-4


def halves(value):
    high = value.astype(BF16)
    return high, (value - high.astype(F32)).astype(BF16)


def dot(a, b, dims):
    return lax.dot_general(a, b, (dims, ((), ())), preferred_element_type=F32)


NN, NT, TN = ((1,), (0,)), ((1,), (1,)), ((0,), (0,))


def dot3(a, b, dims):
    (ah, al), (bh, bl) = a, b
    return dot(ah, bh, dims) + (dot(ah, bl, dims) + dot(al, bh, dims))


def inverse_factor_kernel(a_ref, w_ref, s_ref, flag):
    n = a_ref.shape[0]
    rows = lax.broadcasted_iota(jnp.int32, (n, n), 0)
    cols = lax.broadcasted_iota(jnp.int32, (n, n), 1)
    eye = (rows == cols).astype(F32)
    take = jnp.where(rows > cols, 1.0, 0.5 * eye)
    a = a_ref[...]
    diag_row = jnp.sum(a * eye, axis=0, keepdims=True)
    diag_col = jnp.sum(a * eye, axis=1, keepdims=True)
    scale_row, scale_col = lax.rsqrt(diag_row), lax.rsqrt(diag_col)
    scaled = jnp.where(rows == cols, 1.0, a * scale_row * scale_col)
    s_ref[...] = scaled
    scaled_parts = halves(scaled)
    w = eye - take * (scaled - eye)
    for _ in range(COARSE_STEPS):
        wh = w.astype(BF16)
        t = dot(wh, scaled_parts[0], NN).astype(BF16)
        change = take * (dot(t, wh, NT) - eye)
        w = w - dot(change.astype(BF16), wh, NN)
    w_ref[...] = w
    flag[0] = 0

    def fine(state):
        step, _ = state
        w = w_ref[...]
        parts = halves(w)
        t = halves(dot3(parts, halves(s_ref[...]), NN))
        residual = dot3(t, parts, NT) - eye
        w_ref[...] = w - dot((take * residual).astype(BF16), parts[0], NN)
        return step + 1, jnp.sum(residual * residual)

    _, left = lax.while_loop(
        lambda state: jnp.logical_and(state[0] < FINE_STEPS, jnp.logical_not(state[1] < RESIDUAL**2)),
        fine,
        (jnp.int32(0), jnp.float32(1.0)),
    )
    done = left < RESIDUAL**2

    @pl.when(jnp.logical_not(done))
    def _():
        w_ref[...] = eye

        def eliminate(j, carry):
            row = s_ref[pl.ds(j, 1), :]
            pick = lax.broadcasted_iota(jnp.int32, (1, n), 1) == j
            pivot = jnp.sum(jnp.where(pick, row, 0.0), axis=1, keepdims=True)
            column = jnp.sum(jnp.where(pick, s_ref[...], 0.0), axis=1, keepdims=True)
            below = lax.broadcasted_iota(jnp.int32, (n, 1), 0) > j
            ratio = jnp.where(below, column / pivot, 0.0)
            s_ref[...] = s_ref[...] - ratio * row
            w_ref[...] = w_ref[...] - ratio * w_ref[pl.ds(j, 1), :]
            return carry

        lax.fori_loop(0, n, eliminate, 0)
        pivots = jnp.sum(s_ref[...] * eye, axis=1, keepdims=True)
        w_ref[...] = w_ref[...] * lax.rsqrt(pivots)

    w_ref[...] = w_ref[...] * scale_row


def inverse_factor(pivot):
    n = pivot.shape[0]
    return pl.pallas_call(
        inverse_factor_kernel,
        out_shape=jax.ShapeDtypeStruct((n, n), F32),
        in_specs=[VMEM],
        out_specs=VMEM,
        scratch_shapes=[pltpu.VMEM((n, n), F32), pltpu.SMEM((1,), jnp.int32)],
        compiler_params=pltpu.CompilerParams(vmem_limit_bytes=32 * 2**20),
    )(pivot)


class Sizes:
    def __init__(self, trailing, panel_rows, panel_fill):
        self.cols, self.rows = lax.axis_size("col"), lax.axis_size("row")
        self.block = panel_rows.shape[1] // 2
        self.piece = panel_rows.shape[0]
        self.unit = math.gcd(self.piece, self.block)
        self.per_piece = self.piece // self.unit
        self.per_block = self.block // self.unit
        self.slab = self.piece * self.cols
        self.width = trailing.shape[1]
        self.tiles = self.cols * self.per_piece

    def source(self, c):
        slab = c * self.width // self.slab
        return slab, (c * self.width - slab * self.slab) // self.piece

    def sources(self):
        found = []
        for c in range(self.cols):
            slab, first = self.source(c)
            last = ((c + 1) * self.width - 1 - slab * self.slab) // self.piece
            found.append(last - first + 1)
        return found


def unit_flag(sizes, fill_ref, piece_index, unit, panel):
    block = (piece_index * sizes.per_piece + unit) // sizes.per_block
    return fill_ref[block * 2 + panel] != 0


def pool_pieces(sizes, pool_row, pool_col):
    for core in range(2):
        for side in range(2):
            yield core, side, (pool_row * 2 + core) * sizes.cols + pool_col * 2 + side


def fits_kernel(sizes, cap, fill_ref, out_ref):
    most = jnp.int32(0)
    for pool_row in range(sizes.rows // 2):
        for pool_col in range(sizes.cols // 2):
            count = jnp.int32(0)
            for _, _, piece in pool_pieces(sizes, pool_row, pool_col):
                for u in range(sizes.per_piece):
                    for p in range(2):
                        count = count + unit_flag(sizes, fill_ref, piece, u, p).astype(jnp.int32)
            most = jnp.maximum(most, count)
    out_ref[0] = (most <= cap).astype(jnp.int32)


def fits(sizes, cap, fill):
    return pl.pallas_call(
        functools.partial(fits_kernel, sizes, cap),
        out_shape=jax.ShapeDtypeStruct((1,), jnp.int32),
        in_specs=[SMEM],
        out_specs=SMEM,
    )(fill)


def pack_kernel(sizes, cap, where_ref, fill_ref, panel_ref, side_ref, core_ref, out_ref, pool):
    c, r = where_ref[0], where_ref[1]
    side, core = c % 2, r % 2
    half, quarter = sizes.unit // 2, sizes.unit // 4
    own_at = pl.multiple_of(side * half + core * quarter, quarter)
    side_at = pl.multiple_of(core * quarter, quarter)
    for u in range(sizes.per_piece):
        pool[core, side, u] = panel_ref[u, pl.ds(own_at, quarter), :]
        pool[core, 1 - side, u] = side_ref[u, pl.ds(side_at, quarter), :]
        pool[1 - core, side, u] = core_ref[0, u]
        pool[1 - core, 1 - side, u] = core_ref[1, u]
    slot = jnp.int32(0)
    for core_at, side_at, piece in pool_pieces(sizes, r // 2, c // 2):
        for u in range(sizes.per_piece):
            for p in range(2):
                flag = unit_flag(sizes, fill_ref, piece, u, p)

                @pl.when(flag)
                def _(slot=slot, core_at=core_at, side_at=side_at, u=u, p=p):
                    out_ref[jnp.minimum(slot, cap - 1)] = pool[
                        core_at, side_at, u, :, p * sizes.block : (p + 1) * sizes.block
                    ]

                slot = slot + flag.astype(jnp.int32)


def pack(sizes, cap, where, fill, panel, from_side, from_core):
    quarter = sizes.unit // 4
    return pl.pallas_call(
        functools.partial(pack_kernel, sizes, cap),
        out_shape=jax.ShapeDtypeStruct((cap, quarter, sizes.block), F32),
        in_specs=[SMEM, SMEM, VMEM, VMEM, VMEM],
        out_specs=VMEM,
        scratch_shapes=[pltpu.VMEM((2, 2, sizes.per_piece, quarter, 2 * sizes.block), F32)],
        compiler_params=pltpu.CompilerParams(vmem_limit_bytes=16 * 2**20),
    )(where, fill, panel, from_side, from_core)


def apply_factor_kernel(
    sizes, where_ref, fill_ref, w_ref, panel_ref, column_ref, x_ref, high_ref, low_ref, slot_ref, masked, column
):
    c, r = where_ref[0], where_ref[1]

    def mask(source, target, first_unit, count):
        for u in range(count):
            for p in range(2):
                at = (pl.ds(u * sizes.unit, sizes.unit), pl.ds(p * sizes.block, sizes.block))
                flag = fill_ref[(first_unit + u) // sizes.per_block * 2 + p] != 0
                target[at] = jnp.where(flag, source[at], 0.0)

    mask(panel_ref, masked, (r * sizes.cols + c) * sizes.per_piece, sizes.per_piece)
    mask(column_ref, column, c * (sizes.width // sizes.unit), sizes.width // sizes.unit)
    w = halves(w_ref[...])
    x_ref[...] = dot3(halves(masked[...]), w, NT)
    solved = dot3(w, halves(column[...]), NT)
    high_ref[...], low_ref[...] = halves(dot3(w, halves(solved), TN))

    @pl.loop(0, sizes.cols // 2)
    def _(group):
        pool_col = jnp.bitwise_xor(c // 2, group)
        slot = jnp.int32(0)
        for core, side, piece in pool_pieces(sizes, r // 2, pool_col):
            for u in range(sizes.per_piece):
                for p in range(2):
                    flag = unit_flag(sizes, fill_ref, piece, u, p)

                    @pl.when(core == r % 2)
                    def _(slot=slot, flag=flag, side=side, u=u, p=p):
                        at = ((group * 2 + side) * sizes.per_piece + u) * 2 + p
                        slot_ref[at] = jnp.where(flag, slot, -1)

                    slot = slot + flag.astype(jnp.int32)


def apply_factor(sizes, where, fill, w, panel, column):
    n = w.shape[0]
    return pl.pallas_call(
        functools.partial(apply_factor_kernel, sizes),
        out_shape=(
            jax.ShapeDtypeStruct(panel.shape, F32),
            jax.ShapeDtypeStruct((n, sizes.width), BF16),
            jax.ShapeDtypeStruct((n, sizes.width), BF16),
            jax.ShapeDtypeStruct((2 * sizes.tiles,), jnp.int32),
        ),
        in_specs=[SMEM, SMEM, VMEM, VMEM, VMEM],
        out_specs=(VMEM, VMEM, VMEM, SMEM),
        scratch_shapes=[pltpu.VMEM(panel.shape, F32), pltpu.VMEM((sizes.width, n), F32)],
        compiler_params=pltpu.CompilerParams(vmem_limit_bytes=32 * 2**20),
    )(where, fill, w, panel, column)


def update_kernel(sizes, where_ref, slot_ref, high_ref, low_ref, window_ref, *refs):
    groups = sizes.cols // 2
    lists, (out_ref, tiles, unit_data, in_sems, out_sems) = refs[: 4 * groups], refs[4 * groups :]
    c, r = where_ref[0], where_ref[1]
    side, core = c % 2, r % 2
    per_group = 2 * sizes.per_piece
    quarter = sizes.unit // 4

    def rows_of(t):
        group = jnp.bitwise_xor(c // 2, t // per_group)
        return pl.ds(pl.multiple_of((group * per_group + t % per_group) * sizes.unit, sizes.unit), sizes.unit)

    def tile_in(t):
        return pltpu.make_async_copy(window_ref.at[rows_of(t)], tiles.at[t], in_sems.at[t])

    def tile_out(t):
        return pltpu.make_async_copy(tiles.at[t], out_ref.at[rows_of(t)], out_sems.at[t])

    def active(t):
        return jnp.logical_or(slot_ref[2 * t] >= 0, slot_ref[2 * t + 1] >= 0)

    @pl.loop(0, sizes.tiles)
    def _(t):
        pl.when(active(t))(tile_in(t).start)

    for group in range(groups):

        @pl.loop(group * per_group, (group + 1) * per_group)
        def _(t, group=group):
            @pl.when(active(t))
            def _():
                tile_in(t).wait()
                for p in range(2):
                    slot = slot_ref[2 * t + p]

                    @pl.when(slot >= 0)
                    def _(p=p, slot=slot):
                        for flip in range(4):
                            from_side = jnp.bitwise_xor(side, flip // 2)
                            from_core = jnp.bitwise_xor(core, flip % 2)
                            at = pl.multiple_of((from_side * 2 + from_core) * quarter, quarter)
                            unit_data[pl.ds(at, quarter), :] = lists[4 * group + flip][slot]
                        at = pl.ds(p * sizes.block, sizes.block)
                        right = (high_ref[at, :], low_ref[at, :])
                        tiles[t] = tiles[t] - dot3(halves(unit_data[...]), right, NN)

                tile_out(t).start()

    @pl.loop(0, sizes.tiles)
    def _(t):
        pl.when(active(t))(tile_out(t).wait)


def update(sizes, where, slots, high, low, window, lists):
    tiles = sizes.tiles
    return pl.pallas_call(
        functools.partial(update_kernel, sizes),
        out_shape=jax.ShapeDtypeStruct(window.shape, F32),
        in_specs=[SMEM, SMEM, VMEM, VMEM, ANY] + [VMEM] * len(lists),
        out_specs=ANY,
        input_output_aliases={4: 0},
        scratch_shapes=[
            pltpu.VMEM((tiles, sizes.unit, sizes.width), F32),
            pltpu.VMEM((sizes.unit, sizes.block), F32),
            pltpu.SemaphoreType.DMA((tiles,)),
            pltpu.SemaphoreType.DMA((tiles,)),
        ],
        compiler_params=pltpu.CompilerParams(vmem_limit_bytes=40 * 2**20),
    )(where, slots, high, low, window, *lists)


def swap(value, axis, step):
    size = lax.axis_size(axis)
    return lax.ppermute(value, axis, [(i, i ^ step) for i in range(size)])


def join(index, step, own, other):
    second = (index & step) != 0
    return jnp.where(second, jnp.concatenate([other, own], 0), jnp.concatenate([own, other], 0))


def after(value, *earlier):
    return lax.optimization_barrier((value, *earlier))[0]


def gather_column(sizes, panel):
    counts = sizes.sources()
    values = []
    for j in range(max(counts)):
        pairs = []
        for at in range(sizes.cols):
            slab, first = sizes.source(at)
            if j < counts[at]:
                pairs.append(((first + j) * sizes.rows + slab, at * sizes.rows + slab))
        values.append(lax.ppermute(panel, ("col", "row"), pairs))
    return values


def select_column(sizes, values):
    start = lax.axis_index("col") * sizes.width % sizes.slab % sizes.piece
    return lax.dynamic_slice_in_dim(jnp.concatenate(values, 0), start, sizes.width, 0)


def spread_column(sizes, value, step):
    r, c = lax.axis_index("row"), lax.axis_index("col")
    target = c * sizes.width // sizes.slab
    return jnp.where(((r ^ target) & step) != 0, swap(value, "row", step), value)


def copy_kernel(source_ref, target_ref):
    target_ref[...] = source_ref[...]


def copy(window, rows):
    spec = pl.BlockSpec((rows, window.shape[1]), lambda i: (i, 0))
    return pl.pallas_call(
        copy_kernel,
        out_shape=jax.ShapeDtypeStruct(window.shape, F32),
        grid=(window.shape[0] // rows,),
        in_specs=[spec],
        out_specs=spec,
    )(window)


def per_device(trailing, panel_rows, pivot_block, panel_fill):
    sizes = Sizes(trailing, panel_rows, panel_fill)
    fill = panel_fill.reshape(-1)
    where = jnp.stack([lax.axis_index("col"), lax.axis_index("row")]).astype(jnp.int32)
    units = panel_rows.reshape(sizes.per_piece, sizes.unit, -1)
    most = 8 * sizes.per_piece

    def run(cap, trailing, panel_rows, pivot_block, fill, units):
        r, c = lax.axis_index("row"), lax.axis_index("col")
        side, core = c % 2, r % 2
        half, quarter = sizes.unit // 2, sizes.unit // 4
        share = pivot_block.shape[0] // 2

        kept = lax.dynamic_slice_in_dim(units, side * half, half, 1)
        from_side = swap(lax.dynamic_slice_in_dim(units, (1 - side) * half, half, 1), "col", 1)
        pivot = lax.dynamic_slice_in_dim(pivot_block, core * share, share, 0)[None]
        pivot = join(c, 1, pivot, swap(pivot, "col", 1))
        column = gather_column(sizes, panel_rows)
        from_side, pivot, *column = lax.optimization_barrier((from_side, pivot, *column))

        both = jnp.stack([kept, from_side])
        from_core = swap(lax.dynamic_slice_in_dim(both, (1 - core) * quarter, quarter, 2), "row", 1)
        pivot = join(c, 2, pivot, swap(pivot, "col", 2))
        from_core, pivot = lax.optimization_barrier((from_core, pivot))
        own = pack(sizes, cap, where, fill, units, from_side, from_core)

        far = list(range(2, sizes.cols, 2))
        first, later = [far[-1]] + far[:-2], far[-2:-1]
        lists = {k: swap(own, "col", k) for k in first}
        sides = {0: swap(own, "col", 1)}
        step = 4
        while step < sizes.cols:
            pivot = join(c, step, pivot, swap(pivot, "col", step))
            step *= 2
        column = lax.optimization_barrier((own, *column))[1:]
        column = select_column(sizes, column)
        step = sizes.rows // 2
        while step > 1:
            column = spread_column(sizes, column, step)
            step //= 2
        held = lax.optimization_barrier((own, pivot, column, sides[0], *lists.values()))
        own, pivot, column, sides[0] = held[:4]
        lists = dict(zip(first, held[4:]))

        lists |= {k: swap(own, "col", k) for k in later}
        sides |= {k: swap(lists[k], "col", 1) for k in first}
        pivot = join(r, 1, pivot[None], swap(pivot[None], "row", 1))
        pivot = pivot.transpose(1, 0, 2, 3).reshape(2 * sizes.cols * share, -1)
        window = copy(after(trailing, own), sizes.block)
        w = inverse_factor(after(pivot, window))
        column = spread_column(sizes, column, 1)
        own_factor, high, low, slots = apply_factor(sizes, where, fill, w, panel_rows, column)
        for k in later:
            lists[k] = after(lists[k], high, *(sides[j] for j in first))
            sides[k] = swap(lists[k], "col", 1)
        lists[0] = own
        ordered = []
        for k in range(0, sizes.cols, 2):
            value, other = lists[k], sides[k]
            ordered += [value, swap(value, "row", 1), other, swap(other, "row", 1)]
        return update(sizes, where, slots, high, low, window, ordered), own_factor

    cap = most * 5 // 12
    operands = (trailing, panel_rows, pivot_block, fill, units)
    return lax.cond(
        fits(sizes, cap, fill)[0] != 0,
        functools.partial(run, cap),
        functools.partial(run, most),
        *operands,
    )


def solution(mesh):
    in_specs = (P("row", "col"), P(("row", "col"), None), P("col", None), P())
    out_specs = (P("row", "col"), P(("row", "col"), None))
    return jax.shard_map(
        per_device, mesh=mesh, in_specs=in_specs, out_specs=out_specs, check_vma=False
    )
```

```python
import functools
import math

import jax
import jax.numpy as jnp
from jax import lax
from jax.experimental import pallas as pl
from jax.experimental.pallas import tpu as pltpu
from jax.sharding import PartitionSpec as P

F32, BF16 = jnp.float32, jnp.bfloat16
VMEM = pl.BlockSpec(memory_space=pltpu.VMEM)
SMEM = pl.BlockSpec(memory_space=pltpu.SMEM)
HBM = pl.BlockSpec(memory_space=pltpu.HBM)
COARSE_STEPS = 2
FINE_STEPS = 16
RESIDUAL = 5e-4


def halves(value):
    high = value.astype(BF16)
    return high, (value - high.astype(F32)).astype(BF16)


def dot(a, b, dims):
    return lax.dot_general(a, b, (dims, ((), ())), preferred_element_type=F32)


NN, NT, TN = ((1,), (0,)), ((1,), (1,)), ((0,), (0,))


def dot3(a, b, dims):
    (ah, al), (bh, bl) = a, b
    return dot(ah, bh, dims) + (dot(ah, bl, dims) + dot(al, bh, dims))


def inverse_factor_kernel(where_ref, own_ref, other_ref, w_ref, s_ref):
    n = w_ref.shape[0]
    pieces, share = own_ref.shape[0], own_ref.shape[1]
    core = where_ref[1] % 2
    for i in range(pieces):
        for ref, half in ((own_ref, core), (other_ref, 1 - core)):
            s_ref[pl.ds(pl.multiple_of((2 * i + half) * share, share), share), :] = ref[i]
    rows = lax.broadcasted_iota(jnp.int32, (n, n), 0)
    cols = lax.broadcasted_iota(jnp.int32, (n, n), 1)
    eye = (rows == cols).astype(F32)
    take = jnp.where(rows > cols, 1.0, 0.5 * eye)
    a = s_ref[...]
    diag_row = jnp.sum(a * eye, axis=0, keepdims=True)
    diag_col = jnp.sum(a * eye, axis=1, keepdims=True)
    scale_row, scale_col = lax.rsqrt(diag_row), lax.rsqrt(diag_col)
    scaled = jnp.where(rows == cols, 1.0, a * scale_row * scale_col)
    s_ref[...] = scaled
    scaled_parts = halves(scaled)
    w = eye - take * (scaled - eye)
    for _ in range(COARSE_STEPS):
        wh = w.astype(BF16)
        t = dot(wh, scaled_parts[0], NN).astype(BF16)
        change = take * (dot(t, wh, NT) - eye)
        w = w - dot(change.astype(BF16), wh, NN)
    w_ref[...] = w

    def fine(state):
        step, _ = state
        w = w_ref[...]
        parts = halves(w)
        t = halves(dot3(parts, halves(s_ref[...]), NN))
        residual = dot3(t, parts, NT) - eye
        w_ref[...] = w - dot((take * residual).astype(BF16), parts[0], NN)
        return step + 1, jnp.sum(residual * residual)

    _, left = lax.while_loop(
        lambda state: jnp.logical_and(state[0] < FINE_STEPS, jnp.logical_not(state[1] < RESIDUAL**2)),
        fine,
        (jnp.int32(0), jnp.float32(1.0)),
    )
    done = left < RESIDUAL**2

    @pl.when(jnp.logical_not(done))
    def _():
        w_ref[...] = eye

        def eliminate(j, carry):
            row = s_ref[pl.ds(j, 1), :]
            pick = lax.broadcasted_iota(jnp.int32, (1, n), 1) == j
            pivot = jnp.sum(jnp.where(pick, row, 0.0), axis=1, keepdims=True)
            column = jnp.sum(jnp.where(pick, s_ref[...], 0.0), axis=1, keepdims=True)
            below = lax.broadcasted_iota(jnp.int32, (n, 1), 0) > j
            ratio = jnp.where(below, column / pivot, 0.0)
            s_ref[...] = s_ref[...] - ratio * row
            w_ref[...] = w_ref[...] - ratio * w_ref[pl.ds(j, 1), :]
            return carry

        lax.fori_loop(0, n, eliminate, 0)
        pivots = jnp.sum(s_ref[...] * eye, axis=1, keepdims=True)
        w_ref[...] = w_ref[...] * lax.rsqrt(pivots)

    w_ref[...] = w_ref[...] * scale_row


def inverse_factor(where, own, other):
    n = own.shape[-1]
    return pl.pallas_call(
        inverse_factor_kernel,
        out_shape=jax.ShapeDtypeStruct((n, n), F32),
        in_specs=[SMEM, VMEM, VMEM],
        out_specs=VMEM,
        scratch_shapes=[pltpu.VMEM((n, n), F32)],
        compiler_params=pltpu.CompilerParams(vmem_limit_bytes=32 * 2**20),
    )(where, own, other)


class Sizes:
    def __init__(self, trailing, panel_rows, panel_fill):
        self.cols, self.rows = lax.axis_size("col"), lax.axis_size("row")
        self.block = panel_rows.shape[1] // 2
        self.piece = panel_rows.shape[0]
        self.unit = math.gcd(self.piece, self.block)
        self.per_piece = self.piece // self.unit
        self.per_block = self.block // self.unit
        self.slab = self.piece * self.cols
        self.width = trailing.shape[1]
        self.tiles = self.cols * self.per_piece

    def source(self, c):
        slab = c * self.width // self.slab
        return slab, (c * self.width - slab * self.slab) // self.piece

    def sources(self):
        found = []
        for c in range(self.cols):
            slab, first = self.source(c)
            last = ((c + 1) * self.width - 1 - slab * self.slab) // self.piece
            found.append(last - first + 1)
        return found


def unit_flag(sizes, fill_ref, piece_index, unit, panel):
    block = (piece_index * sizes.per_piece + unit) // sizes.per_block
    return fill_ref[block * 2 + panel] != 0


def pool_pieces(sizes, pool_row, pool_col):
    for core in range(2):
        for side in range(2):
            yield core, side, (pool_row * 2 + core) * sizes.cols + pool_col * 2 + side


def fits_kernel(sizes, cap, fill_ref, out_ref):
    most = jnp.int32(0)
    for pool_row in range(sizes.rows // 2):
        for pool_col in range(sizes.cols // 2):
            count = jnp.int32(0)
            for _, _, piece in pool_pieces(sizes, pool_row, pool_col):
                for u in range(sizes.per_piece):
                    for p in range(2):
                        count = count + unit_flag(sizes, fill_ref, piece, u, p).astype(jnp.int32)
            most = jnp.maximum(most, count)
    out_ref[0] = (most <= cap).astype(jnp.int32)


def fits(sizes, cap, fill):
    return pl.pallas_call(
        functools.partial(fits_kernel, sizes, cap),
        out_shape=jax.ShapeDtypeStruct((1,), jnp.int32),
        in_specs=[SMEM],
        out_specs=SMEM,
    )(fill)


def pack_kernel(sizes, cap, where_ref, fill_ref, panel_ref, core_ref, side_ref, out_ref, pool):
    c, r = where_ref[0], where_ref[1]
    side, core = c % 2, r % 2
    quarter = sizes.unit // 4
    own_at = pl.multiple_of((side * 2 + core) * quarter, quarter)
    for u in range(sizes.per_piece):
        pool[core, side, u] = panel_ref[u, pl.ds(own_at, quarter), :]
        pool[1 - core, side, u] = core_ref[u, side]
        pool[core, 1 - side, u] = side_ref[0, u]
        pool[1 - core, 1 - side, u] = side_ref[1, u]
    slot = jnp.int32(0)
    for core_at, side_at, piece in pool_pieces(sizes, r // 2, c // 2):
        for u in range(sizes.per_piece):
            for p in range(2):
                flag = unit_flag(sizes, fill_ref, piece, u, p)

                @pl.when(flag)
                def _(slot=slot, core_at=core_at, side_at=side_at, u=u, p=p):
                    out_ref[jnp.minimum(slot, cap - 1)] = pool[
                        core_at, side_at, u, :, p * sizes.block : (p + 1) * sizes.block
                    ]

                slot = slot + flag.astype(jnp.int32)


def pack(sizes, cap, where, fill, panel, from_core, from_side):
    quarter = sizes.unit // 4
    return pl.pallas_call(
        functools.partial(pack_kernel, sizes, cap),
        out_shape=jax.ShapeDtypeStruct((cap, quarter, sizes.block), F32),
        in_specs=[SMEM, SMEM, VMEM, VMEM, VMEM],
        out_specs=VMEM,
        scratch_shapes=[pltpu.VMEM((2, 2, sizes.per_piece, quarter, 2 * sizes.block), F32)],
        compiler_params=pltpu.CompilerParams(vmem_limit_bytes=16 * 2**20),
    )(where, fill, panel, from_core, from_side)


def apply_factor_kernel(
    sizes, where_ref, fill_ref, w_ref, panel_ref, column_ref, x_ref, high_ref, low_ref, slot_ref, masked, column, sem
):
    c, r = where_ref[0], where_ref[1]

    def mask(source, target, first_unit, count):
        for u in range(count):
            for p in range(2):
                at = (pl.ds(u * sizes.unit, sizes.unit), pl.ds(p * sizes.block, sizes.block))
                flag = fill_ref[(first_unit + u) // sizes.per_block * 2 + p] != 0
                target[at] = jnp.where(flag, source[at], 0.0)

    mask(panel_ref, masked, (r * sizes.cols + c) * sizes.per_piece, sizes.per_piece)
    mask(column_ref, column, c * (sizes.width // sizes.unit), sizes.width // sizes.unit)
    w = halves(w_ref[...])
    masked[...] = dot3(halves(masked[...]), w, NT)
    copy_out = pltpu.make_async_copy(masked, x_ref, sem)
    copy_out.start()
    solved = dot3(w, halves(column[...]), NT)
    high_ref[...], low_ref[...] = halves(dot3(w, halves(solved), TN))

    @pl.loop(0, sizes.cols // 2)
    def _(group):
        pool_col = jnp.bitwise_xor(c // 2, group)
        slot = jnp.int32(0)
        for core, side, piece in pool_pieces(sizes, r // 2, pool_col):
            for u in range(sizes.per_piece):
                for p in range(2):
                    flag = unit_flag(sizes, fill_ref, piece, u, p)

                    @pl.when(core == r % 2)
                    def _(slot=slot, flag=flag, side=side, u=u, p=p):
                        at = ((group * 2 + side) * sizes.per_piece + u) * 2 + p
                        slot_ref[at] = jnp.where(flag, slot, -1)

                    slot = slot + flag.astype(jnp.int32)

    copy_out.wait()


def apply_factor(sizes, where, fill, w, panel, column):
    n = w.shape[0]
    return pl.pallas_call(
        functools.partial(apply_factor_kernel, sizes),
        out_shape=(
            jax.ShapeDtypeStruct(panel.shape, F32),
            jax.ShapeDtypeStruct((n, sizes.width), BF16),
            jax.ShapeDtypeStruct((n, sizes.width), BF16),
            jax.ShapeDtypeStruct((2 * sizes.tiles,), jnp.int32),
        ),
        in_specs=[SMEM, SMEM, VMEM, VMEM, VMEM],
        out_specs=(HBM, VMEM, VMEM, SMEM),
        scratch_shapes=[
            pltpu.VMEM(panel.shape, F32),
            pltpu.VMEM((sizes.width, n), F32),
            pltpu.SemaphoreType.DMA,
        ],
        compiler_params=pltpu.CompilerParams(vmem_limit_bytes=32 * 2**20),
    )(where, fill, w, panel, column)


def update_kernel(sizes, where_ref, slot_ref, high_ref, low_ref, window_ref, *refs):
    groups = sizes.cols // 2
    lists, (out_ref, tiles, unit_data, out_sems) = refs[: 4 * groups], refs[4 * groups :]
    c, r = where_ref[0], where_ref[1]
    side, core = c % 2, r % 2
    per_group = 2 * sizes.per_piece
    quarter = sizes.unit // 4

    def rows_of(t):
        group = jnp.bitwise_xor(c // 2, t // per_group)
        return pl.ds(pl.multiple_of((group * per_group + t % per_group) * sizes.unit, sizes.unit), sizes.unit)

    def tile_out(t, source):
        return pltpu.make_async_copy(source, out_ref.at[rows_of(t)], out_sems.at[t])

    def active(t):
        return jnp.logical_or(slot_ref[2 * t] >= 0, slot_ref[2 * t + 1] >= 0)

    @pl.loop(0, sizes.tiles)
    def _(t):
        pl.when(jnp.logical_not(active(t)))(tile_out(t, window_ref.at[rows_of(t)]).start)

    for group in range(groups):

        @pl.loop(group * per_group, (group + 1) * per_group)
        def _(t, group=group):
            @pl.when(active(t))
            def _():
                tiles[t] = window_ref[rows_of(t), :]
                for p in range(2):
                    slot = slot_ref[2 * t + p]

                    @pl.when(slot >= 0)
                    def _(p=p, slot=slot):
                        for flip in range(4):
                            from_side = jnp.bitwise_xor(side, flip // 2)
                            from_core = jnp.bitwise_xor(core, flip % 2)
                            at = pl.multiple_of((from_side * 2 + from_core) * quarter, quarter)
                            unit_data[pl.ds(at, quarter), :] = lists[4 * group + flip][slot]
                        at = pl.ds(p * sizes.block, sizes.block)
                        right = (high_ref[at, :], low_ref[at, :])
                        tiles[t] = tiles[t] - dot3(halves(unit_data[...]), right, NN)

                tile_out(t, tiles.at[t]).start()

    @pl.loop(0, sizes.tiles)
    def _(t):
        tile_out(t, tiles.at[t]).wait()


def update(sizes, where, slots, high, low, window, lists):
    tiles = sizes.tiles
    return pl.pallas_call(
        functools.partial(update_kernel, sizes),
        out_shape=jax.ShapeDtypeStruct(window.shape, F32),
        in_specs=[SMEM, SMEM, VMEM, VMEM, VMEM] + [VMEM] * len(lists),
        out_specs=HBM,
        scratch_shapes=[
            pltpu.VMEM((tiles, sizes.unit, sizes.width), F32),
            pltpu.VMEM((sizes.unit, sizes.block), F32),
            pltpu.SemaphoreType.DMA((tiles,)),
        ],
        compiler_params=pltpu.CompilerParams(vmem_limit_bytes=48 * 2**20),
    )(where, slots, high, low, window, *lists)


def swap(value, axis, step):
    size = lax.axis_size(axis)
    return lax.ppermute(value, axis, [(i, i ^ step) for i in range(size)])


def join(index, step, own, other):
    second = (index & step) != 0
    return jnp.where(second, jnp.concatenate([other, own], 0), jnp.concatenate([own, other], 0))


def after(value, *earlier):
    return lax.optimization_barrier((value, *earlier))[0]


def gather_column(sizes, panel):
    counts = sizes.sources()
    values = []
    for j in range(max(counts)):
        pairs = []
        for at in range(sizes.cols):
            slab, first = sizes.source(at)
            if j < counts[at]:
                pairs.append(((first + j) * sizes.rows + slab, at * sizes.rows + slab))
        values.append(lax.ppermute(panel, ("col", "row"), pairs))
    return values


def select_column(sizes, values):
    start = lax.axis_index("col") * sizes.width % sizes.slab % sizes.piece
    return lax.dynamic_slice_in_dim(jnp.concatenate(values, 0), start, sizes.width, 0)


def spread_column(sizes, value, step):
    r, c = lax.axis_index("row"), lax.axis_index("col")
    pairs = []
    for at in range(sizes.cols):
        slab, _ = sizes.source(at)
        for row in range(sizes.rows):
            if (row ^ slab) % (2 * step) == 0:
                pairs.append((at * sizes.rows + row, at * sizes.rows + (row ^ step)))
    other = lax.ppermute(value, ("col", "row"), pairs)
    return jnp.where(((r ^ (c * sizes.width // sizes.slab)) & step) != 0, other, value)


def per_device(trailing, panel_rows, pivot_block, panel_fill):
    sizes = Sizes(trailing, panel_rows, panel_fill)
    fill = panel_fill.reshape(-1)
    r, c = lax.axis_index("row"), lax.axis_index("col")
    where = jnp.stack([c, r]).astype(jnp.int32)
    side, core = c % 2, r % 2
    quarter = sizes.unit // 4
    share = pivot_block.shape[0] // 2
    most = 8 * sizes.per_piece
    cap = most * 5 // 12

    units = panel_rows.reshape(sizes.per_piece, sizes.unit, -1)
    quarters = panel_rows.reshape(sizes.per_piece, 2, 2, quarter, -1)

    def at_core(which):
        return lax.dynamic_index_in_dim(quarters, which, 2, keepdims=False)

    from_core = swap(at_core(1 - core), "row", 1)
    both = jnp.stack([at_core(core), from_core])
    from_side = swap(lax.dynamic_index_in_dim(both, 1 - side, 2, keepdims=False), "col", 1)
    pivot = lax.dynamic_slice_in_dim(pivot_block, core * share, share, 0)[None]
    pivot = join(c, 1, pivot, swap(pivot, "col", 1))
    pivot = join(c, 2, pivot, swap(pivot, "col", 2))
    column = gather_column(sizes, panel_rows)

    def run(cap, trailing, panel_rows, fill, units, from_core, from_side, pivot, *column):
        own = pack(sizes, cap, where, fill, units, from_core, from_side)

        far = list(range(2, sizes.cols, 2))
        first, later = [far[-1]] + far[:-2], far[-2:-1]
        lists = {k: swap(own, "col", k) for k in first}
        sides = {0: swap(own, "col", 1)}
        step = 4
        while step < sizes.cols:
            pivot = join(c, step, pivot, swap(pivot, "col", step))
            step *= 2
        column = lax.optimization_barrier((own, *column))[1:]
        column = select_column(sizes, column)
        step = sizes.rows // 2
        while step > 1:
            column = spread_column(sizes, column, step)
            step //= 2
        held = lax.optimization_barrier((own, pivot, column, sides[0], *lists.values()))
        own, pivot, column, sides[0] = held[:4]
        lists = dict(zip(first, held[4:]))

        lists |= {k: swap(own, "col", k) for k in later}
        sides |= {k: swap(lists[k], "col", 1) for k in first}
        w = inverse_factor(where, pivot, swap(pivot, "row", 1))
        column = spread_column(sizes, column, 1)
        own_factor, high, low, slots = apply_factor(sizes, where, fill, w, panel_rows, column)
        for k in later:
            lists[k] = lax.optimization_barrier((lists[k], high, *(sides[j] for j in first)))[0]
            sides[k] = swap(lists[k], "col", 1)
        lists[0] = own
        ordered = []
        for k in range(0, sizes.cols, 2):
            value, other = lists[k], sides[k]
            ordered += [value, swap(value, "row", 1), other, swap(other, "row", 1)]
        return update(sizes, where, slots, high, low, trailing, ordered), own_factor

    operands = (trailing, panel_rows, fill, units, from_core, from_side, pivot, *column)
    return lax.cond(
        fits(sizes, cap, fill)[0] != 0,
        functools.partial(run, cap),
        functools.partial(run, most),
        *operands,
    )


def solution(mesh):
    in_specs = (P("row", "col"), P(("row", "col"), None), P("col", None), P())
    out_specs = (P("row", "col"), P(("row", "col"), None))
    return jax.shard_map(
        per_device, mesh=mesh, in_specs=in_specs, out_specs=out_specs, check_vma=False
    )
```

```python
import functools
import math

import jax
import jax.numpy as jnp
from jax import lax
from jax.experimental import pallas as pl
from jax.experimental.pallas import tpu as pltpu
from jax.sharding import PartitionSpec as P

F32, BF16 = jnp.float32, jnp.bfloat16
VMEM = pl.BlockSpec(memory_space=pltpu.VMEM)
SMEM = pl.BlockSpec(memory_space=pltpu.SMEM)
HBM = pl.BlockSpec(memory_space=pltpu.HBM)
COARSE_STEPS = 2
FINE_STEPS = 16
RESIDUAL = 5e-4


def halves(value):
    high = value.astype(BF16)
    return high, (value - high.astype(F32)).astype(BF16)


def dot(a, b, dims):
    return lax.dot_general(a, b, (dims, ((), ())), preferred_element_type=F32)


NN, NT, TN = ((1,), (0,)), ((1,), (1,)), ((0,), (0,))


def dot3(a, b, dims):
    (ah, al), (bh, bl) = a, b
    return dot(ah, bh, dims) + (dot(ah, bl, dims) + dot(al, bh, dims))


def inverse_factor_kernel(where_ref, *refs):
    parts, (w_ref, s_ref) = refs[:-2], refs[-2:]
    n = w_ref.shape[0]
    pieces, share = parts[0].shape[0], parts[0].shape[1]
    own = where_ref[1] % len(parts)
    for flip, ref in enumerate(parts):
        at = jnp.bitwise_xor(own, flip) * share
        for i in range(pieces):
            s_ref[pl.ds(pl.multiple_of(i * len(parts) * share + at, share), share), :] = ref[i]
    rows = lax.broadcasted_iota(jnp.int32, (n, n), 0)
    cols = lax.broadcasted_iota(jnp.int32, (n, n), 1)
    eye = (rows == cols).astype(F32)
    take = jnp.where(rows > cols, 1.0, 0.5 * eye)
    a = s_ref[...]
    diag_row = jnp.sum(a * eye, axis=0, keepdims=True)
    diag_col = jnp.sum(a * eye, axis=1, keepdims=True)
    scale_row, scale_col = lax.rsqrt(diag_row), lax.rsqrt(diag_col)
    scaled = jnp.where(rows == cols, 1.0, a * scale_row * scale_col)
    s_ref[...] = scaled
    scaled_parts = halves(scaled)
    w = eye - take * (scaled - eye)
    for _ in range(COARSE_STEPS):
        wh = w.astype(BF16)
        t = dot(wh, scaled_parts[0], NN).astype(BF16)
        change = take * (dot(t, wh, NT) - eye)
        w = w - dot(change.astype(BF16), wh, NN)
    w_ref[...] = w

    def fine(state):
        step, _ = state
        w = w_ref[...]
        parts = halves(w)
        t = halves(dot3(parts, halves(s_ref[...]), NN))
        residual = dot3(t, parts, NT) - eye
        w_ref[...] = w - dot((take * residual).astype(BF16), parts[0], NN)
        return step + 1, jnp.sum(residual * residual)

    _, left = lax.while_loop(
        lambda state: jnp.logical_and(state[0] < FINE_STEPS, jnp.logical_not(state[1] < RESIDUAL**2)),
        fine,
        (jnp.int32(0), jnp.float32(1.0)),
    )
    done = left < RESIDUAL**2

    @pl.when(jnp.logical_not(done))
    def _():
        w_ref[...] = eye

        def eliminate(j, carry):
            row = s_ref[pl.ds(j, 1), :]
            pick = lax.broadcasted_iota(jnp.int32, (1, n), 1) == j
            pivot = jnp.sum(jnp.where(pick, row, 0.0), axis=1, keepdims=True)
            column = jnp.sum(jnp.where(pick, s_ref[...], 0.0), axis=1, keepdims=True)
            below = lax.broadcasted_iota(jnp.int32, (n, 1), 0) > j
            ratio = jnp.where(below, column / pivot, 0.0)
            s_ref[...] = s_ref[...] - ratio * row
            w_ref[...] = w_ref[...] - ratio * w_ref[pl.ds(j, 1), :]
            return carry

        lax.fori_loop(0, n, eliminate, 0)
        pivots = jnp.sum(s_ref[...] * eye, axis=1, keepdims=True)
        w_ref[...] = w_ref[...] * lax.rsqrt(pivots)

    w_ref[...] = w_ref[...] * scale_row


def inverse_factor(where, parts):
    n = parts[0].shape[-1]
    return pl.pallas_call(
        inverse_factor_kernel,
        out_shape=jax.ShapeDtypeStruct((n, n), F32),
        in_specs=[SMEM] + [VMEM] * len(parts),
        out_specs=VMEM,
        scratch_shapes=[pltpu.VMEM((n, n), F32)],
        compiler_params=pltpu.CompilerParams(vmem_limit_bytes=32 * 2**20),
    )(where, *parts)


class Sizes:
    def __init__(self, trailing, panel_rows, panel_fill):
        self.cols, self.rows = lax.axis_size("col"), lax.axis_size("row")
        self.block = panel_rows.shape[1] // 2
        self.piece = panel_rows.shape[0]
        self.unit = math.gcd(self.piece, self.block)
        self.per_piece = self.piece // self.unit
        self.per_block = self.block // self.unit
        self.slab = self.piece * self.cols
        self.width = trailing.shape[1]
        self.tiles = self.cols * self.per_piece

        self.groups = self.cols // 2
        self.pair_units = 4 * self.width // self.unit
        self.needed = sorted({s for g in range(self.groups) for s in self.shifts(g)})

    def pair_slab(self, group):
        return 2 * group * self.width // self.slab

    def pair_start(self, group):
        return (2 * group * self.width - self.pair_slab(group) * self.slab) // self.unit

    def shifts(self, group):
        start = self.pair_start(group) * self.unit
        first, last = start // (2 * self.piece), (start + 2 * self.width - 1) // (2 * self.piece)
        return [(g - group) % self.groups for g in range(first, last + 1)]


def unit_flag(sizes, fill_ref, piece_index, unit, panel):
    block = (piece_index * sizes.per_piece + unit) // sizes.per_block
    return fill_ref[block * 2 + panel] != 0


def pool_pieces(sizes, pool_row, pool_col):
    for core in range(2):
        for side in range(2):
            yield core, side, (pool_row * 2 + core) * sizes.cols + pool_col * 2 + side


def pair_flag(sizes, fill_ref, group, index):
    unit = sizes.pair_slab(group) * sizes.tiles + sizes.pair_start(group) + index // 2
    return fill_ref[unit // sizes.per_block * 2 + index % 2] != 0


def fits_kernel(sizes, cap, pair_cap, fill_ref, out_ref):
    over = jnp.int32(0)
    for pool_row in range(sizes.rows // 2):
        for pool_col in range(sizes.groups):
            count = jnp.int32(0)
            for _, _, piece in pool_pieces(sizes, pool_row, pool_col):
                for u in range(sizes.per_piece):
                    for p in range(2):
                        count = count + unit_flag(sizes, fill_ref, piece, u, p).astype(jnp.int32)
            over = jnp.maximum(over, count - cap)
    for group in range(sizes.groups):
        count = jnp.int32(0)
        for i in range(sizes.pair_units):
            count = count + pair_flag(sizes, fill_ref, group, i).astype(jnp.int32)
        over = jnp.maximum(over, count - pair_cap)
    out_ref[0] = (over <= 0).astype(jnp.int32)


def fits(sizes, cap, pair_cap, fill):
    return pl.pallas_call(
        functools.partial(fits_kernel, sizes, cap, pair_cap),
        out_shape=jax.ShapeDtypeStruct((1,), jnp.int32),
        in_specs=[SMEM],
        out_specs=SMEM,
    )(fill)


def pack_kernel(sizes, cap, where_ref, fill_ref, panel_ref, core_ref, side_ref, out_ref, pool):
    c, r = where_ref[0], where_ref[1]
    side, core = c % 2, r % 2
    quarter = sizes.unit // 4
    own_at = pl.multiple_of((side * 2 + core) * quarter, quarter)
    for u in range(sizes.per_piece):
        pool[core, side, u] = panel_ref[u, pl.ds(own_at, quarter), :]
        pool[1 - core, side, u] = core_ref[u, side]
        pool[core, 1 - side, u] = side_ref[0, u]
        pool[1 - core, 1 - side, u] = side_ref[1, u]
    slot = jnp.int32(0)
    for core_at, side_at, piece in pool_pieces(sizes, r // 2, c // 2):
        for u in range(sizes.per_piece):
            for p in range(2):
                flag = unit_flag(sizes, fill_ref, piece, u, p)

                @pl.when(flag)
                def _(slot=slot, core_at=core_at, side_at=side_at, u=u, p=p):
                    out_ref[jnp.minimum(slot, cap - 1)] = pool[
                        core_at, side_at, u, :, p * sizes.block : (p + 1) * sizes.block
                    ]

                slot = slot + flag.astype(jnp.int32)


def pack(sizes, cap, where, fill, panel, from_core, from_side):
    quarter = sizes.unit // 4
    return pl.pallas_call(
        functools.partial(pack_kernel, sizes, cap),
        out_shape=jax.ShapeDtypeStruct((cap, quarter, sizes.block), F32),
        in_specs=[SMEM, SMEM, VMEM, VMEM, VMEM],
        out_specs=VMEM,
        scratch_shapes=[pltpu.VMEM((2, 2, sizes.per_piece, quarter, 2 * sizes.block), F32)],
        compiler_params=pltpu.CompilerParams(vmem_limit_bytes=16 * 2**20),
    )(where, fill, panel, from_core, from_side)


def pair_slots(sizes, fill_ref, group, slots):
    def step(i, slot):
        flag = pair_flag(sizes, fill_ref, group, i)
        slots[i] = jnp.where(flag, slot, -1)
        return slot + flag.astype(jnp.int32)

    lax.fori_loop(0, sizes.pair_units, step, jnp.int32(0))


def pack_column_kernel(sizes, cap, pair_cap, where_ref, fill_ref, *refs):
    lists, (out_ref, slots) = refs[:-2], refs[-2:]
    own = where_ref[0] // 2
    slab, start = sizes.pair_slab(own), sizes.pair_start(own)
    pair_slots(sizes, fill_ref, own, slots)
    for shift, list_ref in zip(sizes.needed, lists):
        group = lax.rem(own + shift, sizes.groups)
        slot = jnp.int32(0)
        for core, side, piece in pool_pieces(sizes, slab // 2, group):
            for u in range(sizes.per_piece):
                for p in range(2):
                    flag = unit_flag(sizes, fill_ref, piece, u, p)
                    index = (((group * 2 + side) * sizes.per_piece + u) - start) * 2 + p
                    inside = jnp.logical_and(index >= 0, index < sizes.pair_units)
                    wanted = jnp.logical_and(jnp.logical_and(flag, inside), slab % 2 == core)

                    @pl.when(wanted)
                    def _(slot=slot, index=index, list_ref=list_ref):
                        target = slots[jnp.clip(index, 0, sizes.pair_units - 1)]
                        out_ref[jnp.clip(target, 0, pair_cap - 1)] = list_ref[jnp.minimum(slot, cap - 1)]

                    slot = slot + flag.astype(jnp.int32)


def pack_column(sizes, cap, pair_cap, where, fill, lists):
    return pl.pallas_call(
        functools.partial(pack_column_kernel, sizes, cap, pair_cap),
        out_shape=jax.ShapeDtypeStruct((pair_cap, sizes.unit // 4, sizes.block), F32),
        in_specs=[SMEM, SMEM] + [VMEM] * len(lists),
        out_specs=VMEM,
        scratch_shapes=[pltpu.SMEM((sizes.pair_units,), jnp.int32)],
        compiler_params=pltpu.CompilerParams(vmem_limit_bytes=32 * 2**20),
    )(where, fill, *lists)


def own_factor_kernel(sizes, where_ref, fill_ref, w_ref, panel_ref, x_ref, slot_ref, masked, sem):
    c, r = where_ref[0], where_ref[1]
    own = r * sizes.cols + c
    for u in range(sizes.per_piece):
        for p in range(2):
            at = (pl.ds(u * sizes.unit, sizes.unit), pl.ds(p * sizes.block, sizes.block))
            masked[at] = jnp.where(unit_flag(sizes, fill_ref, own, u, p), panel_ref[at], 0.0)
    masked[...] = dot3(halves(masked[...]), halves(w_ref[...]), NT)
    copy_out = pltpu.make_async_copy(masked, x_ref, sem)
    copy_out.start()

    @pl.loop(0, sizes.groups)
    def _(shift):
        group = lax.rem(c // 2 + shift, sizes.groups)
        slot = jnp.int32(0)
        for core, side, piece in pool_pieces(sizes, r // 2, group):
            for u in range(sizes.per_piece):
                for p in range(2):
                    flag = unit_flag(sizes, fill_ref, piece, u, p)

                    @pl.when(core == r % 2)
                    def _(slot=slot, flag=flag, side=side, u=u, p=p):
                        at = ((shift * 2 + side) * sizes.per_piece + u) * 2 + p
                        slot_ref[at] = jnp.where(flag, slot, -1)

                    slot = slot + flag.astype(jnp.int32)

    copy_out.wait()


def own_factor(sizes, where, fill, w, panel):
    return pl.pallas_call(
        functools.partial(own_factor_kernel, sizes),
        out_shape=(
            jax.ShapeDtypeStruct(panel.shape, F32),
            jax.ShapeDtypeStruct((2 * sizes.tiles,), jnp.int32),
        ),
        in_specs=[SMEM, SMEM, VMEM, VMEM],
        out_specs=(HBM, SMEM),
        scratch_shapes=[pltpu.VMEM(panel.shape, F32), pltpu.SemaphoreType.DMA],
        compiler_params=pltpu.CompilerParams(vmem_limit_bytes=32 * 2**20),
    )(where, fill, w, panel)


def column_factor_kernel(sizes, where_ref, fill_ref, w_ref, *refs):
    lists, (out_ref, column, slots) = refs[:4], refs[4:]
    c, r = where_ref[0], where_ref[1]
    side, core = c % 2, r % 2
    quarter = sizes.unit // 4
    pair_slots(sizes, fill_ref, c // 2, slots)
    column[...] = jnp.zeros_like(column)

    @pl.loop(0, sizes.pair_units // 4)
    def _(unit):
        for p in range(2):
            slot = slots[(side * (sizes.pair_units // 4) + unit) * 2 + p]

            @pl.when(slot >= 0)
            def _(slot=slot, p=p):
                for flip in range(4):
                    from_side = jnp.bitwise_xor(side, flip // 2)
                    from_core = jnp.bitwise_xor(core, flip % 2)
                    at = pl.multiple_of(unit * sizes.unit + (from_side * 2 + from_core) * quarter, quarter)
                    column[pl.ds(at, quarter), pl.ds(p * sizes.block, sizes.block)] = lists[flip][slot]

    w = halves(w_ref[...])
    solved = dot3(w, halves(column[...]), NT)
    out_ref[0], out_ref[1] = halves(dot3(w, halves(solved), TN))


def column_factor(sizes, where, fill, w, lists):
    n = w.shape[0]
    return pl.pallas_call(
        functools.partial(column_factor_kernel, sizes),
        out_shape=jax.ShapeDtypeStruct((2, n, sizes.width), BF16),
        in_specs=[SMEM, SMEM, VMEM] + [VMEM] * 4,
        out_specs=VMEM,
        scratch_shapes=[pltpu.VMEM((sizes.width, n), F32), pltpu.SMEM((sizes.pair_units,), jnp.int32)],
        compiler_params=pltpu.CompilerParams(vmem_limit_bytes=32 * 2**20),
    )(where, fill, w, *lists)


def update_kernel(sizes, where_ref, slot_ref, column_ref, window_ref, *refs):
    groups = sizes.cols // 2
    lists, (out_ref, tiles, unit_data, out_sems) = refs[: 4 * groups], refs[4 * groups :]
    c, r = where_ref[0], where_ref[1]
    side, core = c % 2, r % 2
    per_group = 2 * sizes.per_piece
    quarter = sizes.unit // 4

    def rows_of(t):
        group = lax.rem(c // 2 + t // per_group, groups)
        return pl.ds(pl.multiple_of((group * per_group + t % per_group) * sizes.unit, sizes.unit), sizes.unit)

    def tile_out(t, source):
        return pltpu.make_async_copy(source, out_ref.at[rows_of(t)], out_sems.at[t])

    def active(t):
        return jnp.logical_or(slot_ref[2 * t] >= 0, slot_ref[2 * t + 1] >= 0)

    @pl.loop(0, sizes.tiles)
    def _(t):
        pl.when(jnp.logical_not(active(t)))(tile_out(t, window_ref.at[rows_of(t)]).start)

    for group in range(groups):

        @pl.loop(group * per_group, (group + 1) * per_group)
        def _(t, group=group):
            @pl.when(active(t))
            def _():
                tiles[t] = window_ref[rows_of(t), :]
                for p in range(2):
                    slot = slot_ref[2 * t + p]

                    @pl.when(slot >= 0)
                    def _(p=p, slot=slot):
                        for flip in range(4):
                            from_side = jnp.bitwise_xor(side, flip // 2)
                            from_core = jnp.bitwise_xor(core, flip % 2)
                            at = pl.multiple_of((from_side * 2 + from_core) * quarter, quarter)
                            unit_data[pl.ds(at, quarter), :] = lists[4 * group + flip][slot]
                        at = pl.ds(p * sizes.block, sizes.block)
                        right = (column_ref[0, at, :], column_ref[1, at, :])
                        tiles[t] = tiles[t] - dot3(halves(unit_data[...]), right, NN)

                tile_out(t, tiles.at[t]).start()

    @pl.loop(0, sizes.tiles)
    def _(t):
        tile_out(t, tiles.at[t]).wait()


def update(sizes, where, slots, column, window, lists):
    tiles = sizes.tiles
    return pl.pallas_call(
        functools.partial(update_kernel, sizes),
        out_shape=jax.ShapeDtypeStruct(window.shape, F32),
        in_specs=[SMEM, SMEM, VMEM, VMEM] + [VMEM] * len(lists),
        out_specs=HBM,
        scratch_shapes=[
            pltpu.VMEM((tiles, sizes.unit, sizes.width), F32),
            pltpu.VMEM((sizes.unit, sizes.block), F32),
            pltpu.SemaphoreType.DMA((tiles,)),
        ],
        compiler_params=pltpu.CompilerParams(vmem_limit_bytes=48 * 2**20),
    )(where, slots, column, window, *lists)


def swap(value, axis, step):
    size = lax.axis_size(axis)
    return lax.ppermute(value, axis, [(i, i ^ step) for i in range(size)])


def join(index, step, own, other):
    second = (index & step) != 0
    return jnp.where(second, jnp.concatenate([other, own], 0), jnp.concatenate([own, other], 0))


def after(value, *earlier):
    return lax.optimization_barrier((value, *earlier))[0]


def bring(sizes, value, shift):
    pairs = [(i, (i - 2 * shift) % sizes.cols) for i in range(sizes.cols)]
    return lax.ppermute(value, "col", pairs)


def spread_column(sizes, value, step):
    r, c = lax.axis_index("row"), lax.axis_index("col")
    pairs = []
    for at in range(sizes.cols):
        slab = sizes.pair_slab(at // 2)
        for row in range(sizes.rows):
            if (row // 2 ^ slab // 2) % step == 0:
                pairs.append((at * sizes.rows + row, at * sizes.rows + (row ^ step)))
    other = lax.ppermute(value, ("col", "row"), pairs)
    return jnp.where(((r ^ sizes.pair_slab(c // 2)) & step) != 0, other, value)


def per_device(trailing, panel_rows, pivot_block, panel_fill):
    sizes = Sizes(trailing, panel_rows, panel_fill)
    fill = panel_fill.reshape(-1)
    r, c = lax.axis_index("row"), lax.axis_index("col")
    where = jnp.stack([c, r]).astype(jnp.int32)
    side, core = c % 2, r % 2
    quarter = sizes.unit // 4
    split = min(4, pivot_block.shape[0] // 8)
    share = pivot_block.shape[0] // split
    most, pair_most = 8 * sizes.per_piece, sizes.pair_units
    cap, pair_cap = most * 5 // 12, pair_most * 5 // 8

    units = panel_rows.reshape(sizes.per_piece, sizes.unit, -1)
    quarters = panel_rows.reshape(sizes.per_piece, 2, 2, quarter, -1)

    def at_core(which):
        return lax.dynamic_index_in_dim(quarters, which, 2, keepdims=False)

    from_core = swap(at_core(1 - core), "row", 1)
    both = jnp.stack([at_core(core), from_core])
    from_side = swap(lax.dynamic_index_in_dim(both, 1 - side, 2, keepdims=False), "col", 1)
    pivot = lax.dynamic_slice_in_dim(pivot_block, r % split * share, share, 0)[None]
    pivot = join(c, 1, pivot, swap(pivot, "col", 1))
    pivot = join(c, 2, pivot, swap(pivot, "col", 2))

    def run(cap, pair_cap, trailing, panel_rows, fill, units, from_core, from_side, pivot):
        own = pack(sizes, cap, where, fill, units, from_core, from_side)
        lists = {0: own}
        first = [s for s in range(1, sizes.groups) if s in sizes.needed]
        later = [s for s in range(1, sizes.groups) if s not in sizes.needed]
        lists |= {s: bring(sizes, own, s) for s in first}
        sides = {0: swap(own, "col", 1)}
        step = 4
        while step < sizes.cols:
            pivot = join(c, step, pivot, swap(pivot, "col", step))
            step *= 2
        near = first[0]
        pivot, sides[0], lists[near] = lax.optimization_barrier((pivot, sides[0], lists[near]))
        parts = [pivot] + ([swap(pivot, "row", 2)] if split == 4 else [])
        parts = [part for value in parts for part in (value, swap(value, "row", 1))]
        w = inverse_factor(where, parts)
        held = lax.optimization_barrier((w, sides[0], *lists.values()))
        w, sides[0] = held[:2]
        lists = dict(zip(lists, held[2:]))

        column = pack_column(sizes, cap, pair_cap, where, fill, [lists[s] for s in sizes.needed])
        lists |= {s: bring(sizes, lists[0], s) for s in later}
        sides |= {s: swap(lists[s], "col", 1) for s in first}
        step = sizes.rows // 2
        while step > 1:
            column = spread_column(sizes, column, step)
            step //= 2
        across = swap(column, "col", 1)
        columns = [column, swap(column, "row", 1), across, swap(across, "row", 1)]
        panel_factor, slots = own_factor(sizes, where, fill, w, panel_rows)
        for s in later:
            lists[s] = lax.optimization_barrier((lists[s], slots, *(sides[j] for j in first)))[0]
            sides[s] = swap(lists[s], "col", 1)
        column = column_factor(sizes, where, fill, w, columns)
        ordered = []
        for s in range(sizes.groups):
            value, other = lists[s], sides[s]
            ordered += [value, swap(value, "row", 1), other, swap(other, "row", 1)]
        return update(sizes, where, slots, column, trailing, ordered), panel_factor

    operands = (trailing, panel_rows, fill, units, from_core, from_side, pivot)
    return lax.cond(
        fits(sizes, cap, pair_cap, fill)[0] != 0,
        functools.partial(run, cap, pair_cap),
        functools.partial(run, most, pair_most),
        *operands,
    )


def solution(mesh):
    in_specs = (P("row", "col"), P(("row", "col"), None), P("col", None), P())
    out_specs = (P("row", "col"), P(("row", "col"), None))
    return jax.shard_map(
        per_device, mesh=mesh, in_specs=in_specs, out_specs=out_specs, check_vma=False
    )
```

```python
import functools
import math

import jax
import jax.numpy as jnp
from jax import lax
from jax.experimental import pallas as pl
from jax.experimental.pallas import tpu as pltpu
from jax.sharding import PartitionSpec as P

F32, BF16 = jnp.float32, jnp.bfloat16
VMEM = pl.BlockSpec(memory_space=pltpu.VMEM)
SMEM = pl.BlockSpec(memory_space=pltpu.SMEM)
HBM = pl.BlockSpec(memory_space=pltpu.HBM)
COARSE_STEPS = 2
FINE_STEPS = 16
RESIDUAL = 5e-4


def halves(value):
    high = value.astype(BF16)
    return high, (value - high.astype(F32)).astype(BF16)


def dot(a, b, dims):
    return lax.dot_general(a, b, (dims, ((), ())), preferred_element_type=F32)


NN, NT, TN = ((1,), (0,)), ((1,), (1,)), ((0,), (0,))


def dot3(a, b, dims):
    (ah, al), (bh, bl) = a, b
    return dot(ah, bh, dims) + (dot(ah, bl, dims) + dot(al, bh, dims))


def inverse_factor_kernel(where_ref, *refs):
    parts, (w_ref, s_ref) = refs[:-2], refs[-2:]
    n = w_ref.shape[0]
    pieces, share = parts[0].shape[0], parts[0].shape[1]
    own = where_ref[1] % len(parts)
    for flip, ref in enumerate(parts):
        at = jnp.bitwise_xor(own, flip) * share
        for i in range(pieces):
            s_ref[pl.ds(pl.multiple_of(i * len(parts) * share + at, share), share), :] = ref[i]
    rows = lax.broadcasted_iota(jnp.int32, (n, n), 0)
    cols = lax.broadcasted_iota(jnp.int32, (n, n), 1)
    eye = (rows == cols).astype(F32)
    take = jnp.where(rows > cols, 1.0, 0.5 * eye)
    a = s_ref[...]
    diag_row = jnp.sum(a * eye, axis=0, keepdims=True)
    diag_col = jnp.sum(a * eye, axis=1, keepdims=True)
    scale_row, scale_col = lax.rsqrt(diag_row), lax.rsqrt(diag_col)
    scaled = jnp.where(rows == cols, 1.0, a * scale_row * scale_col)
    s_ref[...] = scaled
    scaled_parts = halves(scaled)
    w = eye - take * (scaled - eye)
    for _ in range(COARSE_STEPS):
        wh = w.astype(BF16)
        t = dot(wh, scaled_parts[0], NN).astype(BF16)
        change = take * (dot(t, wh, NT) - eye)
        w = w - dot(change.astype(BF16), wh, NN)
    w_ref[...] = w

    def fine(state):
        step, _ = state
        w = w_ref[...]
        parts = halves(w)
        t = halves(dot3(parts, halves(s_ref[...]), NN))
        residual = dot3(t, parts, NT) - eye
        w_ref[...] = w - dot((take * residual).astype(BF16), parts[0], NN)
        return step + 1, jnp.sum(residual * residual)

    _, left = lax.while_loop(
        lambda state: jnp.logical_and(state[0] < FINE_STEPS, jnp.logical_not(state[1] < RESIDUAL**2)),
        fine,
        (jnp.int32(0), jnp.float32(1.0)),
    )
    done = left < RESIDUAL**2

    @pl.when(jnp.logical_not(done))
    def _():
        w_ref[...] = eye

        def eliminate(j, carry):
            row = s_ref[pl.ds(j, 1), :]
            pick = lax.broadcasted_iota(jnp.int32, (1, n), 1) == j
            pivot = jnp.sum(jnp.where(pick, row, 0.0), axis=1, keepdims=True)
            column = jnp.sum(jnp.where(pick, s_ref[...], 0.0), axis=1, keepdims=True)
            below = lax.broadcasted_iota(jnp.int32, (n, 1), 0) > j
            ratio = jnp.where(below, column / pivot, 0.0)
            s_ref[...] = s_ref[...] - ratio * row
            w_ref[...] = w_ref[...] - ratio * w_ref[pl.ds(j, 1), :]
            return carry

        lax.fori_loop(0, n, eliminate, 0)
        pivots = jnp.sum(s_ref[...] * eye, axis=1, keepdims=True)
        w_ref[...] = w_ref[...] * lax.rsqrt(pivots)

    w_ref[...] = w_ref[...] * scale_row


def inverse_factor(where, parts):
    n = parts[0].shape[-1]
    return pl.pallas_call(
        inverse_factor_kernel,
        out_shape=jax.ShapeDtypeStruct((n, n), F32),
        in_specs=[SMEM] + [VMEM] * len(parts),
        out_specs=VMEM,
        scratch_shapes=[pltpu.VMEM((n, n), F32)],
        compiler_params=pltpu.CompilerParams(vmem_limit_bytes=20 * 2**20),
    )(where, *parts)


class Sizes:
    def __init__(self, trailing, panel_rows, panel_fill):
        self.cols, self.rows = lax.axis_size("col"), lax.axis_size("row")
        self.block = panel_rows.shape[1] // 2
        self.piece = panel_rows.shape[0]
        self.unit = math.gcd(self.piece, self.block)
        self.per_piece = self.piece // self.unit
        self.per_block = self.block // self.unit
        self.slab = self.piece * self.cols
        self.merge = self.per_block if 2 * self.piece % self.block == 0 else 1
        self.width = trailing.shape[1]
        self.tiles = self.cols * self.per_piece

        self.groups = self.cols // 2
        self.column_units = 2 * self.width // self.unit
        self.needed = sorted({s for g in range(self.groups) for s in self.shifts(g)})

    def pair_slab(self, group):
        return 2 * group * self.width // self.slab

    def pair_start(self, group):
        return (2 * group * self.width - self.pair_slab(group) * self.slab) // self.unit

    def shifts(self, group):
        start = self.pair_start(group) * self.unit
        first, last = start // (2 * self.piece), (start + 2 * self.width - 1) // (2 * self.piece)
        return [(g - group) % self.groups for g in range(first, last + 1)]


def unit_flag(sizes, fill_ref, piece_index, unit, panel):
    block = (piece_index * sizes.per_piece + unit) // sizes.per_block
    return fill_ref[block * 2 + panel] != 0


def pool_pieces(sizes, pool_row, pool_col):
    for core in range(2):
        for side in range(2):
            yield core, side, (pool_row * 2 + core) * sizes.cols + pool_col * 2 + side


def pair_flag(sizes, fill_ref, group, index):
    unit = sizes.pair_slab(group) * sizes.tiles + sizes.pair_start(group) + index // 2
    return fill_ref[unit // sizes.per_block * 2 + index % 2] != 0


def fits_kernel(sizes, cap, column_cap, fill_ref, out_ref):
    over = jnp.int32(0)
    for pool_row in range(sizes.rows // 2):
        for pool_col in range(sizes.groups):
            count = jnp.int32(0)
            for _, _, piece in pool_pieces(sizes, pool_row, pool_col):
                for u in range(sizes.per_piece):
                    for p in range(2):
                        count = count + unit_flag(sizes, fill_ref, piece, u, p).astype(jnp.int32)
            over = jnp.maximum(over, count - cap)
    for group in range(sizes.groups):
        for side in range(2):
            count = jnp.int32(0)
            for i in range(sizes.column_units):
                flag = pair_flag(sizes, fill_ref, group, side * sizes.column_units + i)
                count = count + flag.astype(jnp.int32)
            over = jnp.maximum(over, count - column_cap)
    out_ref[0] = (over <= 0).astype(jnp.int32)


def fits(sizes, cap, column_cap, fill):
    return pl.pallas_call(
        functools.partial(fits_kernel, sizes, cap, column_cap),
        out_shape=jax.ShapeDtypeStruct((1,), jnp.int32),
        in_specs=[SMEM],
        out_specs=SMEM,
    )(fill)


def pack_kernel(sizes, cap, where_ref, fill_ref, panel_ref, core_ref, side_ref, out_ref, pool):
    c, r = where_ref[0], where_ref[1]
    side, core = c % 2, r % 2
    quarter = sizes.unit // 4
    own_at = pl.multiple_of((side * 2 + core) * quarter, quarter)
    for u in range(sizes.per_piece):
        pool[core, side, u] = panel_ref[u, pl.ds(own_at, quarter), :]
        pool[1 - core, side, u] = core_ref[u, side]
        pool[core, 1 - side, u] = side_ref[0, u]
        pool[1 - core, 1 - side, u] = side_ref[1, u]
    slot = jnp.int32(0)
    for core_at, side_at, piece in pool_pieces(sizes, r // 2, c // 2):
        for u in range(sizes.per_piece):
            for p in range(2):
                flag = unit_flag(sizes, fill_ref, piece, u, p)

                @pl.when(flag)
                def _(slot=slot, core_at=core_at, side_at=side_at, u=u, p=p):
                    out_ref[jnp.minimum(slot, cap - 1)] = pool[
                        core_at, side_at, u, :, p * sizes.block : (p + 1) * sizes.block
                    ]

                slot = slot + flag.astype(jnp.int32)


def pack(sizes, cap, where, fill, panel, from_core, from_side):
    quarter = sizes.unit // 4
    return pl.pallas_call(
        functools.partial(pack_kernel, sizes, cap),
        out_shape=jax.ShapeDtypeStruct((cap, quarter, sizes.block), F32),
        in_specs=[SMEM, SMEM, VMEM, VMEM, VMEM],
        out_specs=VMEM,
        scratch_shapes=[pltpu.VMEM((2, 2, sizes.per_piece, quarter, 2 * sizes.block), F32)],
        compiler_params=pltpu.CompilerParams(vmem_limit_bytes=16 * 2**20),
    )(where, fill, panel, from_core, from_side)


def pair_slots(sizes, fill_ref, group, slots):
    def step(i, slot):
        flag = pair_flag(sizes, fill_ref, group, i)
        slot = jnp.where(i == sizes.column_units, 0, slot)
        slots[i] = jnp.where(flag, slot, -1)
        return slot + flag.astype(jnp.int32)

    lax.fori_loop(0, 2 * sizes.column_units, step, jnp.int32(0))


def pack_column_kernel(sizes, cap, column_cap, where_ref, fill_ref, *refs):
    lists, (out_ref, slots) = refs[:-2], refs[-2:]
    own = where_ref[0] // 2
    slab, start = sizes.pair_slab(own), sizes.pair_start(own)
    pair_slots(sizes, fill_ref, own, slots)
    for shift, list_ref in zip(sizes.needed, lists):
        group = lax.rem(own + shift, sizes.groups)
        slot = jnp.int32(0)
        for core, side, piece in pool_pieces(sizes, slab // 2, group):
            for u in range(sizes.per_piece):
                for p in range(2):
                    flag = unit_flag(sizes, fill_ref, piece, u, p)
                    index = (((group * 2 + side) * sizes.per_piece + u) - start) * 2 + p
                    inside = jnp.logical_and(index >= 0, index < 2 * sizes.column_units)
                    wanted = jnp.logical_and(jnp.logical_and(flag, inside), slab % 2 == core)

                    @pl.when(wanted)
                    def _(slot=slot, index=index, list_ref=list_ref):
                        index = jnp.clip(index, 0, 2 * sizes.column_units - 1)
                        target = jnp.clip(slots[index], 0, column_cap - 1)
                        out_ref[index // sizes.column_units, target] = list_ref[jnp.minimum(slot, cap - 1)]

                    slot = slot + flag.astype(jnp.int32)


def pack_column(sizes, cap, column_cap, where, fill, lists):
    return pl.pallas_call(
        functools.partial(pack_column_kernel, sizes, cap, column_cap),
        out_shape=jax.ShapeDtypeStruct((2, column_cap, sizes.unit // 4, sizes.block), F32),
        in_specs=[SMEM, SMEM] + [VMEM] * len(lists),
        out_specs=VMEM,
        scratch_shapes=[pltpu.SMEM((2 * sizes.column_units,), jnp.int32)],
        compiler_params=pltpu.CompilerParams(vmem_limit_bytes=20 * 2**20),
    )(where, fill, *lists)


def own_factor_kernel(sizes, where_ref, fill_ref, w_ref, panel_ref, x_ref, slot_ref, masked, sem):
    c, r = where_ref[0], where_ref[1]
    own = r * sizes.cols + c
    for u in range(sizes.per_piece):
        for p in range(2):
            at = (pl.ds(u * sizes.unit, sizes.unit), pl.ds(p * sizes.block, sizes.block))
            masked[at] = jnp.where(unit_flag(sizes, fill_ref, own, u, p), panel_ref[at], 0.0)
    masked[...] = dot3(halves(masked[...]), halves(w_ref[...]), NT)
    copy_out = pltpu.make_async_copy(masked, x_ref, sem)
    copy_out.start()

    @pl.loop(0, sizes.groups)
    def _(shift):
        group = lax.rem(c // 2 + shift, sizes.groups)
        slot = jnp.int32(0)
        for core, side, piece in pool_pieces(sizes, r // 2, group):
            for u in range(sizes.per_piece):
                for p in range(2):
                    flag = unit_flag(sizes, fill_ref, piece, u, p)

                    @pl.when(core == r % 2)
                    def _(slot=slot, flag=flag, side=side, u=u, p=p):
                        at = ((shift * 2 + side) * sizes.per_piece + u) * 2 + p
                        slot_ref[at] = jnp.where(flag, slot, -1)

                    slot = slot + flag.astype(jnp.int32)

    copy_out.wait()


def own_factor(sizes, where, fill, w, panel):
    return pl.pallas_call(
        functools.partial(own_factor_kernel, sizes),
        out_shape=(
            pltpu.HBM(panel.shape, F32),
            jax.ShapeDtypeStruct((2 * sizes.tiles,), jnp.int32),
        ),
        in_specs=[SMEM, SMEM, VMEM, VMEM],
        out_specs=(HBM, SMEM),
        scratch_shapes=[pltpu.VMEM(panel.shape, F32), pltpu.SemaphoreType.DMA],
        compiler_params=pltpu.CompilerParams(vmem_limit_bytes=20 * 2**20),
    )(where, fill, w, panel)


def column_factor_kernel(sizes, where_ref, fill_ref, w_ref, *refs):
    lists, (out_ref, column, slots) = refs[:4], refs[4:]
    c, r = where_ref[0], where_ref[1]
    side, core = c % 2, r % 2
    quarter = sizes.unit // 4
    pair_slots(sizes, fill_ref, c // 2, slots)
    column[...] = jnp.zeros_like(column)

    @pl.loop(0, sizes.column_units // 2)
    def _(unit):
        for p in range(2):
            slot = slots[side * sizes.column_units + unit * 2 + p]

            @pl.when(slot >= 0)
            def _(slot=slot, p=p):
                for flip in range(4):
                    from_side = jnp.bitwise_xor(side, flip // 2)
                    from_core = jnp.bitwise_xor(core, flip % 2)
                    at = pl.multiple_of(unit * sizes.unit + (from_side * 2 + from_core) * quarter, quarter)
                    column[pl.ds(at, quarter), pl.ds(p * sizes.block, sizes.block)] = lists[flip][slot]

    w = halves(w_ref[...])
    solved = dot3(w, halves(column[...]), NT)
    out_ref[...] = dot3(w, halves(solved), TN)


def column_factor(sizes, where, fill, w, lists):
    n = w.shape[0]
    return pl.pallas_call(
        functools.partial(column_factor_kernel, sizes),
        out_shape=jax.ShapeDtypeStruct((n, sizes.width), F32),
        in_specs=[SMEM, SMEM, VMEM] + [VMEM] * 4,
        out_specs=VMEM,
        scratch_shapes=[pltpu.VMEM((sizes.width, n), F32), pltpu.SMEM((2 * sizes.column_units,), jnp.int32)],
        compiler_params=pltpu.CompilerParams(vmem_limit_bytes=20 * 2**20),
    )(where, fill, w, *lists)


def update_kernel(sizes, where_ref, slot_ref, column_ref, window_ref, *refs):
    groups, merge = sizes.groups, sizes.merge
    lists, (out_ref, tiles, data, right, out_sems) = refs[: 4 * groups], refs[4 * groups :]
    c, r = where_ref[0], where_ref[1]
    side, core = c % 2, r % 2
    per_group = 2 * sizes.per_piece // merge
    rows = merge * sizes.unit
    quarter = sizes.unit // 4

    def rows_of(t):
        group = lax.rem(c // 2 + t // per_group, groups)
        return pl.ds(pl.multiple_of((group * per_group + t % per_group) * rows, rows), rows)

    def tile_out(t, source):
        return pltpu.make_async_copy(source, out_ref.at[rows_of(t)], out_sems.at[t])

    def slot_of(t, p, part):
        return slot_ref[(t * merge + part) * 2 + p]

    def active(t):
        return jnp.logical_or(slot_of(t, 0, 0) >= 0, slot_of(t, 1, 0) >= 0)

    @pl.loop(0, per_group * groups)
    def _(t):
        pl.when(jnp.logical_not(active(t)))(tile_out(t, window_ref.at[rows_of(t)]).start)

    for p in range(2):
        high, low = halves(column_ref[p * sizes.block : (p + 1) * sizes.block, :])
        for i, part in enumerate((high, low, high)):
            right[p, i * sizes.block : (i + 1) * sizes.block, :] = part

    for group in range(groups):

        @pl.loop(group * per_group, (group + 1) * per_group)
        def _(t, group=group):
            @pl.when(active(t))
            def _():
                tiles[t] = window_ref[rows_of(t), :]
                for p in range(2):

                    @pl.when(slot_of(t, p, 0) >= 0)
                    def _(p=p):
                        for part in range(merge):
                            slot = slot_of(t, p, part)
                            for flip in range(4):
                                from_side = jnp.bitwise_xor(side, flip // 2)
                                from_core = jnp.bitwise_xor(core, flip % 2)
                                at = pl.multiple_of((part * 4 + from_side * 2 + from_core) * quarter, quarter)
                                data[pl.ds(at, quarter), :] = lists[4 * group + flip][slot]
                        high, low = halves(data[...])
                        left = jnp.concatenate([high, high, low], axis=1)
                        tiles[t] = tiles[t] - dot(left, right[p], NN)

                tile_out(t, tiles.at[t]).start()

    @pl.loop(0, per_group * groups)
    def _(t):
        tile_out(t, tiles.at[t]).wait()


def update(sizes, where, slots, column, window, lists):
    rows = sizes.merge * sizes.unit
    tiles = sizes.slab // rows
    return pl.pallas_call(
        functools.partial(update_kernel, sizes),
        out_shape=pltpu.HBM(window.shape, F32),
        in_specs=[SMEM, SMEM, VMEM, VMEM] + [VMEM] * len(lists),
        out_specs=HBM,
        scratch_shapes=[
            pltpu.VMEM((tiles, rows, sizes.width), F32),
            pltpu.VMEM((rows, sizes.block), F32),
            pltpu.VMEM((2, 3 * sizes.block, sizes.width), BF16),
            pltpu.SemaphoreType.DMA((tiles,)),
        ],
        compiler_params=pltpu.CompilerParams(vmem_limit_bytes=36 * 2**20),
    )(where, slots, column, window, *lists)


def swap(value, axis, step):
    size = lax.axis_size(axis)
    return lax.ppermute(value, axis, [(i, i ^ step) for i in range(size)])


def join(index, step, own, other):
    second = (index & step) != 0
    return jnp.where(second, jnp.concatenate([other, own], 0), jnp.concatenate([own, other], 0))


def after(value, *earlier):
    return lax.optimization_barrier((value, *earlier))[0]


def bring(sizes, value, shift):
    pairs = [(i, (i - 2 * shift) % sizes.cols) for i in range(sizes.cols)]
    return lax.ppermute(value, "col", pairs)


def spread_column(sizes, value, step):
    r, c = lax.axis_index("row"), lax.axis_index("col")
    pairs = []
    for at in range(sizes.cols):
        slab = sizes.pair_slab(at // 2)
        for row in range(sizes.rows):
            if (row // 2 ^ slab // 2) % step == 0:
                pairs.append((at * sizes.rows + row, at * sizes.rows + (row ^ step)))
    other = lax.ppermute(value, ("col", "row"), pairs)
    return jnp.where(((r ^ sizes.pair_slab(c // 2)) & step) != 0, other, value)


def per_device(trailing, panel_rows, pivot_block, panel_fill):
    sizes = Sizes(trailing, panel_rows, panel_fill)
    fill = panel_fill.reshape(-1)
    r, c = lax.axis_index("row"), lax.axis_index("col")
    where = jnp.stack([c, r]).astype(jnp.int32)
    side, core = c % 2, r % 2
    quarter = sizes.unit // 4
    split = min(4, pivot_block.shape[0] // 8)
    share = pivot_block.shape[0] // split
    most, column_most = 8 * sizes.per_piece, sizes.column_units
    cap, column_cap = most * 5 // 12, column_most * 3 // 4

    units = panel_rows.reshape(sizes.per_piece, sizes.unit, -1)
    quarters = panel_rows.reshape(sizes.per_piece, 2, 2, quarter, -1)

    def at_core(which):
        return lax.dynamic_index_in_dim(quarters, which, 2, keepdims=False)

    pivot = lax.dynamic_slice_in_dim(pivot_block, r % split * share, share, 0)[None]
    pivot = join(c, 1, pivot, swap(pivot, "col", 1))
    from_core = swap(at_core(1 - core), "row", 1)
    from_core, pivot = lax.optimization_barrier((from_core, pivot))
    both = jnp.stack([at_core(core), from_core])
    from_side = swap(lax.dynamic_index_in_dim(both, 1 - side, 2, keepdims=False), "col", 1)
    step = 2
    while step < sizes.cols:
        pivot = join(c, step, pivot, swap(pivot, "col", step))
        step *= 2

    def run(cap, column_cap, trailing, panel_rows, fill, units, from_core, from_side, pivot):
        own = pack(sizes, cap, where, fill, units, from_core, from_side)
        lists = {0: own}
        first = [s for s in range(1, sizes.groups) if s in sizes.needed]
        later = [s for s in range(1, sizes.groups) if s not in sizes.needed]
        lists |= {s: bring(sizes, own, s) for s in first}
        sides = {0: swap(own, "col", 1)}
        parts = [pivot] + ([swap(pivot, "row", 2)] if split == 4 else [])
        parts = [part for value in parts for part in (value, swap(value, "row", 1))]
        near = first[0]
        lists[near], sides[0], *parts = lax.optimization_barrier((lists[near], sides[0], *parts))
        sides[near] = swap(lists[near], "col", 1)
        w = inverse_factor(where, parts)
        held = lax.optimization_barrier((w, sides[0], sides[near], *lists.values()))
        w, sides[0], sides[near] = held[:3]
        lists = dict(zip(lists, held[3:]))

        column = pack_column(sizes, cap, column_cap, where, fill, [lists[s] for s in sizes.needed])
        lists |= {s: bring(sizes, lists[0], s) for s in later}
        sides |= {s: swap(lists[s], "col", 1) for s in first[1:]}
        step = sizes.rows // 2
        while step > 1:
            column = spread_column(sizes, column, step)
            step //= 2
        across = swap(lax.dynamic_index_in_dim(column, 1 - side, 0, keepdims=False), "col", 1)
        column = lax.dynamic_index_in_dim(column, side, 0, keepdims=False)
        columns = [column, swap(column, "row", 1), across, swap(across, "row", 1)]
        panel_factor, slots = own_factor(sizes, where, fill, w, panel_rows)
        for s in later:
            lists[s] = lax.optimization_barrier((lists[s], slots, *(sides[j] for j in first)))[0]
            sides[s] = swap(lists[s], "col", 1)
        column = column_factor(sizes, where, fill, w, columns)
        ordered = []
        for s in range(sizes.groups):
            value, other = lists[s], sides[s]
            ordered += [value, swap(value, "row", 1), other, swap(other, "row", 1)]
        return update(sizes, where, slots, column, trailing, ordered), panel_factor

    operands = (trailing, panel_rows, fill, units, from_core, from_side, pivot)
    return lax.cond(
        fits(sizes, cap, column_cap, fill)[0] != 0,
        functools.partial(run, cap, column_cap),
        functools.partial(run, most, column_most),
        *operands,
    )


def solution(mesh):
    in_specs = (P("row", "col"), P(("row", "col"), None), P("col", None), P())
    out_specs = (P("row", "col"), P(("row", "col"), None))
    return jax.shard_map(
        per_device, mesh=mesh, in_specs=in_specs, out_specs=out_specs, check_vma=False
    )
```

```python
import functools
import math

import jax
import jax.numpy as jnp
from jax import lax
from jax.experimental import pallas as pl
from jax.experimental.pallas import tpu as pltpu
from jax.sharding import PartitionSpec as P

F32, BF16 = jnp.float32, jnp.bfloat16
VMEM = pl.BlockSpec(memory_space=pltpu.VMEM)
SMEM = pl.BlockSpec(memory_space=pltpu.SMEM)
HBM = pl.BlockSpec(memory_space=pltpu.HBM)
COARSE_STEPS = 2
FINE_STEPS = 16
RESIDUAL = 5e-4


def halves(value):
    high = value.astype(BF16)
    return high, (value - high.astype(F32)).astype(BF16)


def dot(a, b, dims):
    return lax.dot_general(a, b, (dims, ((), ())), preferred_element_type=F32)


NN, NT, TN = ((1,), (0,)), ((1,), (1,)), ((0,), (0,))


def dot3(a, b, dims):
    (ah, al), (bh, bl) = a, b
    return dot(ah, bh, dims) + (dot(ah, bl, dims) + dot(al, bh, dims))


def inverse_factor_kernel(where_ref, *refs):
    parts, (w_ref, s_ref) = refs[:-2], refs[-2:]
    n = w_ref.shape[0]
    pieces, share = parts[0].shape[0], parts[0].shape[1]
    own = where_ref[1] % len(parts)
    for flip, ref in enumerate(parts):
        at = jnp.bitwise_xor(own, flip) * share
        for i in range(pieces):
            s_ref[pl.ds(pl.multiple_of(i * len(parts) * share + at, share), share), :] = ref[i]
    rows = lax.broadcasted_iota(jnp.int32, (n, n), 0)
    cols = lax.broadcasted_iota(jnp.int32, (n, n), 1)
    eye = (rows == cols).astype(F32)
    take = jnp.where(rows > cols, 1.0, 0.5 * eye)
    a = s_ref[...]
    diag_row = jnp.sum(a * eye, axis=0, keepdims=True)
    diag_col = jnp.sum(a * eye, axis=1, keepdims=True)
    scale_row, scale_col = lax.rsqrt(diag_row), lax.rsqrt(diag_col)
    scaled = jnp.where(rows == cols, 1.0, a * scale_row * scale_col)
    s_ref[...] = scaled
    scaled_parts = halves(scaled)
    w = eye - take * (scaled - eye)
    for _ in range(COARSE_STEPS):
        wh = w.astype(BF16)
        t = dot(wh, scaled_parts[0], NN).astype(BF16)
        change = take * (dot(t, wh, NT) - eye)
        w = w - dot(change.astype(BF16), wh, NN)
    w_ref[...] = w

    def fine(state):
        step, _ = state
        w = w_ref[...]
        parts = halves(w)
        t = halves(dot3(parts, halves(s_ref[...]), NN))
        residual = dot3(t, parts, NT) - eye
        w_ref[...] = w - dot((take * residual).astype(BF16), parts[0], NN)
        return step + 1, jnp.sum(residual * residual)

    _, left = lax.while_loop(
        lambda state: jnp.logical_and(state[0] < FINE_STEPS, jnp.logical_not(state[1] < RESIDUAL**2)),
        fine,
        (jnp.int32(0), jnp.float32(1.0)),
    )
    done = left < RESIDUAL**2

    @pl.when(jnp.logical_not(done))
    def _():
        w_ref[...] = eye

        def eliminate(j, carry):
            row = s_ref[pl.ds(j, 1), :]
            pick = lax.broadcasted_iota(jnp.int32, (1, n), 1) == j
            pivot = jnp.sum(jnp.where(pick, row, 0.0), axis=1, keepdims=True)
            column = jnp.sum(jnp.where(pick, s_ref[...], 0.0), axis=1, keepdims=True)
            below = lax.broadcasted_iota(jnp.int32, (n, 1), 0) > j
            ratio = jnp.where(below, column / pivot, 0.0)
            s_ref[...] = s_ref[...] - ratio * row
            w_ref[...] = w_ref[...] - ratio * w_ref[pl.ds(j, 1), :]
            return carry

        lax.fori_loop(0, n, eliminate, 0)
        pivots = jnp.sum(s_ref[...] * eye, axis=1, keepdims=True)
        w_ref[...] = w_ref[...] * lax.rsqrt(pivots)

    w_ref[...] = w_ref[...] * scale_row


def inverse_factor(where, parts):
    n = parts[0].shape[-1]
    return pl.pallas_call(
        inverse_factor_kernel,
        out_shape=jax.ShapeDtypeStruct((n, n), F32),
        in_specs=[SMEM] + [VMEM] * len(parts),
        out_specs=VMEM,
        scratch_shapes=[pltpu.VMEM((n, n), F32)],
        compiler_params=pltpu.CompilerParams(vmem_limit_bytes=20 * 2**20),
    )(where, *parts)


class Sizes:
    def __init__(self, trailing, panel_rows, panel_fill):
        self.cols, self.rows = lax.axis_size("col"), lax.axis_size("row")
        self.block = panel_rows.shape[1] // 2
        self.piece = panel_rows.shape[0]
        self.unit = math.gcd(self.piece, self.block)
        self.per_piece = self.piece // self.unit
        self.per_block = self.block // self.unit
        self.slab = self.piece * self.cols
        self.merge = self.per_block if 2 * self.piece % self.block == 0 else 1
        self.width = trailing.shape[1]
        self.tiles = self.cols * self.per_piece

        self.groups = self.cols // 2
        self.column_units = 2 * self.width // self.unit
        self.needed = sorted({s for g in range(self.groups) for s in self.shifts(g)})

    def pair_slab(self, group):
        return 2 * group * self.width // self.slab

    def pair_start(self, group):
        return (2 * group * self.width - self.pair_slab(group) * self.slab) // self.unit

    def shifts(self, group):
        start = self.pair_start(group) * self.unit
        first, last = start // (2 * self.piece), (start + 2 * self.width - 1) // (2 * self.piece)
        return [(g - group) % self.groups for g in range(first, last + 1)]


def unit_flag(sizes, fill_ref, piece_index, unit, panel):
    block = (piece_index * sizes.per_piece + unit) // sizes.per_block
    return fill_ref[block * 2 + panel] != 0


def pool_pieces(sizes, pool_row, pool_col):
    for core in range(2):
        for side in range(2):
            yield core, side, (pool_row * 2 + core) * sizes.cols + pool_col * 2 + side


def pair_flag(sizes, fill_ref, group, index):
    unit = sizes.pair_slab(group) * sizes.tiles + sizes.pair_start(group) + index // 2
    return fill_ref[unit // sizes.per_block * 2 + index % 2] != 0


def fits_kernel(sizes, cap, column_cap, fill_ref, out_ref):
    over = jnp.int32(0)
    for pool_row in range(sizes.rows // 2):
        for pool_col in range(sizes.groups):
            count = jnp.int32(0)
            for _, _, piece in pool_pieces(sizes, pool_row, pool_col):
                for u in range(sizes.per_piece):
                    for p in range(2):
                        count = count + unit_flag(sizes, fill_ref, piece, u, p).astype(jnp.int32)
            over = jnp.maximum(over, count - cap)
    for group in range(sizes.groups):
        for side in range(2):
            count = jnp.int32(0)
            for i in range(sizes.column_units):
                flag = pair_flag(sizes, fill_ref, group, side * sizes.column_units + i)
                count = count + flag.astype(jnp.int32)
            over = jnp.maximum(over, count - column_cap)
    out_ref[0] = (over <= 0).astype(jnp.int32)


def fits(sizes, cap, column_cap, fill):
    return pl.pallas_call(
        functools.partial(fits_kernel, sizes, cap, column_cap),
        out_shape=jax.ShapeDtypeStruct((1,), jnp.int32),
        in_specs=[SMEM],
        out_specs=SMEM,
    )(fill)


def pack_kernel(sizes, cap, where_ref, fill_ref, panel_ref, core_ref, side_ref, out_ref, pool):
    c, r = where_ref[0], where_ref[1]
    side, core = c % 2, r % 2
    quarter = sizes.unit // 4
    own_at = pl.multiple_of((side * 2 + core) * quarter, quarter)
    for u in range(sizes.per_piece):
        pool[core, side, u] = panel_ref[u, pl.ds(own_at, quarter), :]
        pool[1 - core, side, u] = core_ref[u, side]
        pool[core, 1 - side, u] = side_ref[0, u]
        pool[1 - core, 1 - side, u] = side_ref[1, u]
    slot = jnp.int32(0)
    for core_at, side_at, piece in pool_pieces(sizes, r // 2, c // 2):
        for u in range(sizes.per_piece):
            for p in range(2):
                flag = unit_flag(sizes, fill_ref, piece, u, p)

                @pl.when(flag)
                def _(slot=slot, core_at=core_at, side_at=side_at, u=u, p=p):
                    out_ref[jnp.minimum(slot, cap - 1)] = pool[
                        core_at, side_at, u, :, p * sizes.block : (p + 1) * sizes.block
                    ]

                slot = slot + flag.astype(jnp.int32)


def pack(sizes, cap, where, fill, panel, from_core, from_side):
    quarter = sizes.unit // 4
    return pl.pallas_call(
        functools.partial(pack_kernel, sizes, cap),
        out_shape=jax.ShapeDtypeStruct((cap, quarter, sizes.block), F32),
        in_specs=[SMEM, SMEM, VMEM, VMEM, VMEM],
        out_specs=VMEM,
        scratch_shapes=[pltpu.VMEM((2, 2, sizes.per_piece, quarter, 2 * sizes.block), F32)],
        compiler_params=pltpu.CompilerParams(vmem_limit_bytes=16 * 2**20),
    )(where, fill, panel, from_core, from_side)


def pair_slots(sizes, fill_ref, group, slots):
    def step(i, slot):
        flag = pair_flag(sizes, fill_ref, group, i)
        slot = jnp.where(i == sizes.column_units, 0, slot)
        slots[i] = jnp.where(flag, slot, -1)
        return slot + flag.astype(jnp.int32)

    lax.fori_loop(0, 2 * sizes.column_units, step, jnp.int32(0))


def pack_column_kernel(sizes, cap, column_cap, where_ref, fill_ref, *refs):
    lists, (out_ref, slots) = refs[:-2], refs[-2:]
    own = where_ref[0] // 2
    slab, start = sizes.pair_slab(own), sizes.pair_start(own)
    pair_slots(sizes, fill_ref, own, slots)
    for shift, list_ref in zip(sizes.needed, lists):
        group = lax.rem(own + shift, sizes.groups)
        slot = jnp.int32(0)
        for core, side, piece in pool_pieces(sizes, slab // 2, group):
            for u in range(sizes.per_piece):
                for p in range(2):
                    flag = unit_flag(sizes, fill_ref, piece, u, p)
                    index = (((group * 2 + side) * sizes.per_piece + u) - start) * 2 + p
                    inside = jnp.logical_and(index >= 0, index < 2 * sizes.column_units)
                    wanted = jnp.logical_and(jnp.logical_and(flag, inside), slab % 2 == core)

                    @pl.when(wanted)
                    def _(slot=slot, index=index, list_ref=list_ref):
                        index = jnp.clip(index, 0, 2 * sizes.column_units - 1)
                        target = jnp.clip(slots[index], 0, column_cap - 1)
                        out_ref[index // sizes.column_units, target] = list_ref[jnp.minimum(slot, cap - 1)]

                    slot = slot + flag.astype(jnp.int32)


def pack_column(sizes, cap, column_cap, where, fill, lists):
    return pl.pallas_call(
        functools.partial(pack_column_kernel, sizes, cap, column_cap),
        out_shape=jax.ShapeDtypeStruct((2, column_cap, sizes.unit // 4, sizes.block), F32),
        in_specs=[SMEM, SMEM] + [VMEM] * len(lists),
        out_specs=VMEM,
        scratch_shapes=[pltpu.SMEM((2 * sizes.column_units,), jnp.int32)],
        compiler_params=pltpu.CompilerParams(vmem_limit_bytes=20 * 2**20),
    )(where, fill, *lists)


def own_factor_kernel(sizes, where_ref, fill_ref, w_ref, panel_ref, x_ref, masked, sem):
    own = where_ref[1] * sizes.cols + where_ref[0]
    for u in range(sizes.per_piece):
        for p in range(2):
            at = (pl.ds(u * sizes.unit, sizes.unit), pl.ds(p * sizes.block, sizes.block))
            masked[at] = jnp.where(unit_flag(sizes, fill_ref, own, u, p), panel_ref[at], 0.0)
    masked[...] = dot3(halves(masked[...]), halves(w_ref[...]), NT)
    copy_out = pltpu.make_async_copy(masked, x_ref, sem)
    copy_out.start()
    copy_out.wait()


def own_factor(sizes, where, fill, w, panel):
    return pl.pallas_call(
        functools.partial(own_factor_kernel, sizes),
        out_shape=pltpu.HBM(panel.shape, F32),
        in_specs=[SMEM, SMEM, VMEM, VMEM],
        out_specs=HBM,
        scratch_shapes=[pltpu.VMEM(panel.shape, F32), pltpu.SemaphoreType.DMA],
        compiler_params=pltpu.CompilerParams(vmem_limit_bytes=20 * 2**20),
    )(where, fill, w, panel)


def list_slots_kernel(sizes, where_ref, fill_ref, slot_ref):
    c, r = where_ref[0], where_ref[1]

    @pl.loop(0, sizes.groups)
    def _(shift):
        group = lax.rem(c // 2 + shift, sizes.groups)
        slot = jnp.int32(0)
        for core, side, piece in pool_pieces(sizes, r // 2, group):
            for u in range(sizes.per_piece):
                for p in range(2):
                    flag = unit_flag(sizes, fill_ref, piece, u, p)

                    @pl.when(core == r % 2)
                    def _(slot=slot, flag=flag, side=side, u=u, p=p):
                        at = ((shift * 2 + side) * sizes.per_piece + u) * 2 + p
                        slot_ref[at] = jnp.where(flag, slot, -1)

                    slot = slot + flag.astype(jnp.int32)


def list_slots(sizes, where, fill):
    return pl.pallas_call(
        functools.partial(list_slots_kernel, sizes),
        out_shape=jax.ShapeDtypeStruct((2 * sizes.tiles,), jnp.int32),
        in_specs=[SMEM, SMEM],
        out_specs=SMEM,
        cost_estimate=pl.CostEstimate(flops=2 * 10**10, bytes_accessed=6 * 10**7, transcendentals=0),
    )(where, fill)


def column_factor_kernel(sizes, where_ref, fill_ref, w_ref, *refs):
    lists, (out_ref, column, slots) = refs[:4], refs[4:]
    c, r = where_ref[0], where_ref[1]
    side, core = c % 2, r % 2
    quarter = sizes.unit // 4
    pair_slots(sizes, fill_ref, c // 2, slots)
    column[...] = jnp.zeros_like(column)

    @pl.loop(0, sizes.column_units // 2)
    def _(unit):
        for p in range(2):
            slot = slots[side * sizes.column_units + unit * 2 + p]

            @pl.when(slot >= 0)
            def _(slot=slot, p=p):
                for flip in range(4):
                    from_side = jnp.bitwise_xor(side, flip // 2)
                    from_core = jnp.bitwise_xor(core, flip % 2)
                    at = pl.multiple_of(unit * sizes.unit + (from_side * 2 + from_core) * quarter, quarter)
                    column[pl.ds(at, quarter), pl.ds(p * sizes.block, sizes.block)] = lists[flip][slot]

    w = halves(w_ref[...])
    solved = dot3(w, halves(column[...]), NT)
    out_ref[...] = dot3(w, halves(solved), TN)


def column_factor(sizes, where, fill, w, lists):
    n = w.shape[0]
    return pl.pallas_call(
        functools.partial(column_factor_kernel, sizes),
        out_shape=jax.ShapeDtypeStruct((n, sizes.width), F32),
        in_specs=[SMEM, SMEM, VMEM] + [VMEM] * 4,
        out_specs=VMEM,
        scratch_shapes=[pltpu.VMEM((sizes.width, n), F32), pltpu.SMEM((2 * sizes.column_units,), jnp.int32)],
        compiler_params=pltpu.CompilerParams(vmem_limit_bytes=20 * 2**20),
    )(where, fill, w, *lists)


def update_kernel(sizes, where_ref, slot_ref, column_ref, window_ref, *refs):
    groups, merge = sizes.groups, sizes.merge
    lists, (out_ref, tiles, data, right, out_sems) = refs[: 4 * groups], refs[4 * groups :]
    c, r = where_ref[0], where_ref[1]
    side, core = c % 2, r % 2
    per_group = 2 * sizes.per_piece // merge
    rows = merge * sizes.unit
    quarter = sizes.unit // 4

    def rows_of(t):
        group = lax.rem(c // 2 + t // per_group, groups)
        return pl.ds(pl.multiple_of((group * per_group + t % per_group) * rows, rows), rows)

    def tile_out(t, source):
        return pltpu.make_async_copy(source, out_ref.at[rows_of(t)], out_sems.at[t])

    def slot_of(t, p, part):
        return slot_ref[(t * merge + part) * 2 + p]

    def active(t):
        return jnp.logical_or(slot_of(t, 0, 0) >= 0, slot_of(t, 1, 0) >= 0)

    @pl.loop(0, per_group * groups)
    def _(t):
        pl.when(jnp.logical_not(active(t)))(tile_out(t, window_ref.at[rows_of(t)]).start)

    for p in range(2):
        high, low = halves(column_ref[p * sizes.block : (p + 1) * sizes.block, :])
        for i, part in enumerate((high, low, high)):
            right[p, i * sizes.block : (i + 1) * sizes.block, :] = part

    for group in range(groups):

        @pl.loop(group * per_group, (group + 1) * per_group)
        def _(t, group=group):
            @pl.when(active(t))
            def _():
                tiles[t] = window_ref[rows_of(t), :]
                for p in range(2):

                    @pl.when(slot_of(t, p, 0) >= 0)
                    def _(p=p):
                        for part in range(merge):
                            slot = slot_of(t, p, part)
                            for flip in range(4):
                                from_side = jnp.bitwise_xor(side, flip // 2)
                                from_core = jnp.bitwise_xor(core, flip % 2)
                                at = pl.multiple_of((part * 4 + from_side * 2 + from_core) * quarter, quarter)
                                data[pl.ds(at, quarter), :] = lists[4 * group + flip][slot]
                        high, low = halves(data[...])
                        left = jnp.concatenate([high, high, low], axis=1)
                        tiles[t] = tiles[t] - dot(left, right[p], NN)

                tile_out(t, tiles.at[t]).start()

    @pl.loop(0, per_group * groups)
    def _(t):
        tile_out(t, tiles.at[t]).wait()


def update(sizes, where, slots, column, window, lists):
    rows = sizes.merge * sizes.unit
    tiles = sizes.slab // rows
    return pl.pallas_call(
        functools.partial(update_kernel, sizes),
        out_shape=pltpu.HBM(window.shape, F32),
        in_specs=[SMEM, SMEM, VMEM, VMEM] + [VMEM] * len(lists),
        out_specs=HBM,
        scratch_shapes=[
            pltpu.VMEM((tiles, rows, sizes.width), F32),
            pltpu.VMEM((rows, sizes.block), F32),
            pltpu.VMEM((2, 3 * sizes.block, sizes.width), BF16),
            pltpu.SemaphoreType.DMA((tiles,)),
        ],
        compiler_params=pltpu.CompilerParams(vmem_limit_bytes=36 * 2**20),
    )(where, slots, column, window, *lists)


def swap(value, axis, step):
    size = lax.axis_size(axis)
    return lax.ppermute(value, axis, [(i, i ^ step) for i in range(size)])


def join(index, step, own, other):
    second = (index & step) != 0
    return jnp.where(second, jnp.concatenate([other, own], 0), jnp.concatenate([own, other], 0))


def after(value, *earlier):
    return lax.optimization_barrier((value, *earlier))[0]


def bring(sizes, value, shift):
    pairs = [(i, (i - 2 * shift) % sizes.cols) for i in range(sizes.cols)]
    return lax.ppermute(value, "col", pairs)


def spread_column(sizes, value, step):
    r, c = lax.axis_index("row"), lax.axis_index("col")
    pairs = []
    for at in range(sizes.cols):
        slab = sizes.pair_slab(at // 2)
        for row in range(sizes.rows):
            if (row // 2 ^ slab // 2) % step == 0:
                pairs.append((at * sizes.rows + row, at * sizes.rows + (row ^ step)))
    other = lax.ppermute(value, ("col", "row"), pairs)
    return jnp.where(((r ^ sizes.pair_slab(c // 2)) & step) != 0, other, value)


def per_device(trailing, panel_rows, pivot_block, panel_fill):
    sizes = Sizes(trailing, panel_rows, panel_fill)
    fill = panel_fill.reshape(-1)
    r, c = lax.axis_index("row"), lax.axis_index("col")
    where = jnp.stack([c, r]).astype(jnp.int32)
    side, core = c % 2, r % 2
    quarter = sizes.unit // 4
    split = min(4, pivot_block.shape[0] // 8)
    share = pivot_block.shape[0] // split
    most, column_most = 8 * sizes.per_piece, sizes.column_units
    cap, column_cap = most * 5 // 12, column_most * 3 // 4

    units = panel_rows.reshape(sizes.per_piece, sizes.unit, -1)
    quarters = panel_rows.reshape(sizes.per_piece, 2, 2, quarter, -1)

    def at_core(which):
        return lax.dynamic_index_in_dim(quarters, which, 2, keepdims=False)

    pivot = lax.dynamic_slice_in_dim(pivot_block, r % split * share, share, 0)[None]
    pivot = join(c, 1, pivot, swap(pivot, "col", 1))
    from_core = swap(at_core(1 - core), "row", 1)
    from_core, pivot = lax.optimization_barrier((from_core, pivot))
    both = jnp.stack([at_core(core), from_core])
    from_side = swap(lax.dynamic_index_in_dim(both, 1 - side, 2, keepdims=False), "col", 1)
    pivot = join(c, 2, pivot, swap(pivot, "col", 2))

    def run(cap, column_cap, trailing, panel_rows, fill, units, from_core, from_side, pivot):
        own = pack(sizes, cap, where, fill, units, from_core, from_side)
        lists = {0: own}
        first = [s for s in range(1, sizes.groups) if s in sizes.needed]
        later = [s for s in range(1, sizes.groups) if s not in sizes.needed]
        lists |= {s: bring(sizes, own, s) for s in first}
        sides = {0: swap(own, "col", 1)}
        pivot = lax.optimization_barrier((pivot, own))[0]
        step = 4
        while step < sizes.cols:
            pivot = join(c, step, pivot, swap(pivot, "col", step))
            step *= 2
        parts = [pivot] + ([swap(pivot, "row", 2)] if split == 4 else [])
        parts = [part for value in parts for part in (value, swap(value, "row", 1))]
        near = first[0]
        lists[near], sides[0] = lax.optimization_barrier((lists[near], sides[0]))
        sides[near] = swap(lists[near], "col", 1)
        count = len(parts)
        held = lax.optimization_barrier((*parts, sides[0], sides[near], *lists.values()))
        parts, sides[0], sides[near] = held[:count], held[count], held[count + 1]
        lists = dict(zip(lists, held[count + 2 :]))

        column = pack_column(sizes, cap, column_cap, where, fill, [lists[s] for s in sizes.needed])
        lists |= {s: bring(sizes, lists[0], s) for s in later}
        sides |= {s: swap(lists[s], "col", 1) for s in first[1:]}
        step = sizes.rows // 2
        while step > 1:
            column = spread_column(sizes, column, step)
            step //= 2
        w = inverse_factor(where, parts)
        held = lax.optimization_barrier((fill, w, *(lists[s] for s in later), *(sides[s] for s in first[1:])))
        lists |= dict(zip(later, held[2:]))
        sides |= dict(zip(first[1:], held[2 + len(later) :]))
        slots = list_slots(sizes, where, held[0])
        w, column, slots, *late = lax.optimization_barrier((held[1], column, slots, *(lists[s] for s in later)))
        lists |= dict(zip(later, late))

        across = swap(lax.dynamic_index_in_dim(column, 1 - side, 0, keepdims=False), "col", 1)
        column = lax.dynamic_index_in_dim(column, side, 0, keepdims=False)
        columns = [column, swap(column, "row", 1), across, swap(across, "row", 1)]
        sides |= {s: swap(lists[s], "col", 1) for s in later}
        panel_factor = own_factor(sizes, where, fill, w, panel_rows)
        column = column_factor(sizes, where, fill, w, columns)
        for s in later:
            sides[s], column, panel_factor = lax.optimization_barrier((sides[s], column, panel_factor))
        ordered = []
        for s in range(sizes.groups):
            value, other = lists[s], sides[s]
            ordered += [value, swap(value, "row", 1), other, swap(other, "row", 1)]
        return update(sizes, where, slots, column, trailing, ordered), panel_factor

    operands = (trailing, panel_rows, fill, units, from_core, from_side, pivot)
    return lax.cond(
        fits(sizes, cap, column_cap, fill)[0] != 0,
        functools.partial(run, cap, column_cap),
        functools.partial(run, most, column_most),
        *operands,
    )


def solution(mesh):
    in_specs = (P("row", "col"), P(("row", "col"), None), P("col", None), P())
    out_specs = (P("row", "col"), P(("row", "col"), None))
    return jax.shard_map(
        per_device, mesh=mesh, in_specs=in_specs, out_specs=out_specs, check_vma=False
    )
```

```python
import functools
import math

import jax
import jax.numpy as jnp
from jax import lax
from jax.experimental import pallas as pl
from jax.experimental.pallas import tpu as pltpu
from jax.sharding import PartitionSpec as P

F32, BF16 = jnp.float32, jnp.bfloat16
VMEM = pl.BlockSpec(memory_space=pltpu.VMEM)
SMEM = pl.BlockSpec(memory_space=pltpu.SMEM)
HBM = pl.BlockSpec(memory_space=pltpu.HBM)
COARSE_STEPS = 2
FINE_STEPS = 16
RESIDUAL = 5e-4


def halves(value):
    high = value.astype(BF16)
    return high, (value - high.astype(F32)).astype(BF16)


def dot(a, b, dims):
    return lax.dot_general(a, b, (dims, ((), ())), preferred_element_type=F32)


NN, NT, TN = ((1,), (0,)), ((1,), (1,)), ((0,), (0,))


def dot3(a, b, dims):
    (ah, al), (bh, bl) = a, b
    return dot(ah, bh, dims) + (dot(ah, bl, dims) + dot(al, bh, dims))


def inverse_factor_kernel(where_ref, *refs):
    parts, (w_ref, s_ref) = refs[:-2], refs[-2:]
    n = w_ref.shape[0]
    pieces, share = parts[0].shape[0], parts[0].shape[1]
    own = where_ref[1] % len(parts)
    for flip, ref in enumerate(parts):
        at = jnp.bitwise_xor(own, flip) * share
        for i in range(pieces):
            s_ref[pl.ds(pl.multiple_of(i * len(parts) * share + at, share), share), :] = ref[i]
    rows = lax.broadcasted_iota(jnp.int32, (n, n), 0)
    cols = lax.broadcasted_iota(jnp.int32, (n, n), 1)
    eye = (rows == cols).astype(F32)
    take = jnp.where(rows > cols, 1.0, 0.5 * eye)
    a = s_ref[...]
    diag_row = jnp.sum(a * eye, axis=0, keepdims=True)
    diag_col = jnp.sum(a * eye, axis=1, keepdims=True)
    scale_row, scale_col = lax.rsqrt(diag_row), lax.rsqrt(diag_col)
    scaled = jnp.where(rows == cols, 1.0, a * scale_row * scale_col)
    s_ref[...] = scaled
    scaled_parts = halves(scaled)
    w = eye - take * (scaled - eye)
    for _ in range(COARSE_STEPS):
        wh = w.astype(BF16)
        t = dot(wh, scaled_parts[0], NN).astype(BF16)
        change = take * (dot(t, wh, NT) - eye)
        w = w - dot(change.astype(BF16), wh, NN)
    w_ref[...] = w

    def fine(state):
        step, _ = state
        w = w_ref[...]
        parts = halves(w)
        t = halves(dot3(parts, halves(s_ref[...]), NN))
        residual = dot3(t, parts, NT) - eye
        w_ref[...] = w - dot((take * residual).astype(BF16), parts[0], NN)
        return step + 1, jnp.sum(residual * residual)

    _, left = lax.while_loop(
        lambda state: jnp.logical_and(state[0] < FINE_STEPS, jnp.logical_not(state[1] < RESIDUAL**2)),
        fine,
        (jnp.int32(0), jnp.float32(1.0)),
    )
    done = left < RESIDUAL**2

    @pl.when(jnp.logical_not(done))
    def _():
        w_ref[...] = eye

        def eliminate(j, carry):
            row = s_ref[pl.ds(j, 1), :]
            pick = lax.broadcasted_iota(jnp.int32, (1, n), 1) == j
            pivot = jnp.sum(jnp.where(pick, row, 0.0), axis=1, keepdims=True)
            column = jnp.sum(jnp.where(pick, s_ref[...], 0.0), axis=1, keepdims=True)
            below = lax.broadcasted_iota(jnp.int32, (n, 1), 0) > j
            ratio = jnp.where(below, column / pivot, 0.0)
            s_ref[...] = s_ref[...] - ratio * row
            w_ref[...] = w_ref[...] - ratio * w_ref[pl.ds(j, 1), :]
            return carry

        lax.fori_loop(0, n, eliminate, 0)
        pivots = jnp.sum(s_ref[...] * eye, axis=1, keepdims=True)
        w_ref[...] = w_ref[...] * lax.rsqrt(pivots)

    w_ref[...] = w_ref[...] * scale_row


def inverse_factor(where, parts):
    n = parts[0].shape[-1]
    return pl.pallas_call(
        inverse_factor_kernel,
        out_shape=jax.ShapeDtypeStruct((n, n), F32),
        in_specs=[SMEM] + [VMEM] * len(parts),
        out_specs=VMEM,
        scratch_shapes=[pltpu.VMEM((n, n), F32)],
        compiler_params=pltpu.CompilerParams(vmem_limit_bytes=16 * 2**20),
    )(where, *parts)


class Sizes:
    def __init__(self, trailing, panel_rows, panel_fill):
        self.cols, self.rows = lax.axis_size("col"), lax.axis_size("row")
        self.block = panel_rows.shape[1] // 2
        self.piece = panel_rows.shape[0]
        self.unit = math.gcd(self.piece, self.block)
        self.per_piece = self.piece // self.unit
        self.per_block = self.block // self.unit
        self.slab = self.piece * self.cols
        self.merge = self.per_block if 2 * self.piece % self.block == 0 else 1
        self.width = trailing.shape[1]
        self.tiles = self.cols * self.per_piece

        self.groups = self.cols // 2
        self.column_units = 2 * self.width // self.unit
        self.needed = sorted({s for g in range(self.groups) for s in self.shifts(g)})

    def pair_slab(self, group):
        return 2 * group * self.width // self.slab

    def pair_start(self, group):
        return (2 * group * self.width - self.pair_slab(group) * self.slab) // self.unit

    def shifts(self, group):
        start = self.pair_start(group) * self.unit
        first, last = start // (2 * self.piece), (start + 2 * self.width - 1) // (2 * self.piece)
        return [(g - group) % self.groups for g in range(first, last + 1)]


def unit_flag(sizes, fill_ref, piece_index, unit, panel):
    block = (piece_index * sizes.per_piece + unit) // sizes.per_block
    return fill_ref[block * 2 + panel] != 0


def pool_pieces(sizes, pool_row, pool_col):
    for core in range(2):
        for side in range(2):
            yield core, side, (pool_row * 2 + core) * sizes.cols + pool_col * 2 + side


def pair_flag(sizes, fill_ref, group, index):
    unit = sizes.pair_slab(group) * sizes.tiles + sizes.pair_start(group) + index // 2
    return fill_ref[unit // sizes.per_block * 2 + index % 2] != 0


def fits_kernel(sizes, cap, column_cap, fill_ref, out_ref):
    over = jnp.int32(0)
    for pool_row in range(sizes.rows // 2):
        for pool_col in range(sizes.groups):
            count = jnp.int32(0)
            for _, _, piece in pool_pieces(sizes, pool_row, pool_col):
                for u in range(sizes.per_piece):
                    for p in range(2):
                        count = count + unit_flag(sizes, fill_ref, piece, u, p).astype(jnp.int32)
            over = jnp.maximum(over, count - cap)
    for group in range(sizes.groups):
        for side in range(2):
            count = jnp.int32(0)
            for i in range(sizes.column_units):
                flag = pair_flag(sizes, fill_ref, group, side * sizes.column_units + i)
                count = count + flag.astype(jnp.int32)
            over = jnp.maximum(over, count - column_cap)
    out_ref[0] = (over <= 0).astype(jnp.int32)


def fits(sizes, cap, column_cap, fill):
    return pl.pallas_call(
        functools.partial(fits_kernel, sizes, cap, column_cap),
        out_shape=jax.ShapeDtypeStruct((1,), jnp.int32),
        in_specs=[SMEM],
        out_specs=SMEM,
    )(fill)


def pack_kernel(sizes, cap, where_ref, fill_ref, panel_ref, core_ref, side_ref, out_ref, pool):
    c, r = where_ref[0], where_ref[1]
    side, core = c % 2, r % 2
    quarter = sizes.unit // 4
    own_at = pl.multiple_of((side * 2 + core) * quarter, quarter)
    for u in range(sizes.per_piece):
        pool[core, side, u] = panel_ref[u, pl.ds(own_at, quarter), :]
        pool[1 - core, side, u] = core_ref[u, side]
        pool[core, 1 - side, u] = side_ref[0, u]
        pool[1 - core, 1 - side, u] = side_ref[1, u]
    slot = jnp.int32(0)
    for core_at, side_at, piece in pool_pieces(sizes, r // 2, c // 2):
        for u in range(sizes.per_piece):
            for p in range(2):
                flag = unit_flag(sizes, fill_ref, piece, u, p)

                @pl.when(flag)
                def _(slot=slot, core_at=core_at, side_at=side_at, u=u, p=p):
                    out_ref[jnp.minimum(slot, cap - 1)] = pool[
                        core_at, side_at, u, :, p * sizes.block : (p + 1) * sizes.block
                    ]

                slot = slot + flag.astype(jnp.int32)


def pack(sizes, cap, where, fill, panel, from_core, from_side):
    quarter = sizes.unit // 4
    return pl.pallas_call(
        functools.partial(pack_kernel, sizes, cap),
        out_shape=jax.ShapeDtypeStruct((cap, quarter, sizes.block), F32),
        in_specs=[SMEM, SMEM, VMEM, VMEM, VMEM],
        out_specs=VMEM,
        scratch_shapes=[pltpu.VMEM((2, 2, sizes.per_piece, quarter, 2 * sizes.block), F32)],
        compiler_params=pltpu.CompilerParams(vmem_limit_bytes=16 * 2**20),
    )(where, fill, panel, from_core, from_side)


def pair_slots(sizes, fill_ref, group, slots):
    def step(i, slot):
        flag = pair_flag(sizes, fill_ref, group, i)
        slot = jnp.where(i == sizes.column_units, 0, slot)
        slots[i] = jnp.where(flag, slot, -1)
        return slot + flag.astype(jnp.int32)

    lax.fori_loop(0, 2 * sizes.column_units, step, jnp.int32(0))


def pack_column_kernel(sizes, cap, column_cap, where_ref, fill_ref, *refs):
    lists, (out_ref, slots) = refs[:-2], refs[-2:]
    own = where_ref[0] // 2
    slab, start = sizes.pair_slab(own), sizes.pair_start(own)
    pair_slots(sizes, fill_ref, own, slots)
    for shift, list_ref in zip(sizes.needed, lists):
        group = lax.rem(own + shift, sizes.groups)
        slot = jnp.int32(0)
        for core, side, piece in pool_pieces(sizes, slab // 2, group):
            for u in range(sizes.per_piece):
                for p in range(2):
                    flag = unit_flag(sizes, fill_ref, piece, u, p)
                    index = (((group * 2 + side) * sizes.per_piece + u) - start) * 2 + p
                    inside = jnp.logical_and(index >= 0, index < 2 * sizes.column_units)
                    wanted = jnp.logical_and(jnp.logical_and(flag, inside), slab % 2 == core)

                    @pl.when(wanted)
                    def _(slot=slot, index=index, list_ref=list_ref):
                        index = jnp.clip(index, 0, 2 * sizes.column_units - 1)
                        target = jnp.clip(slots[index], 0, column_cap - 1)
                        out_ref[index // sizes.column_units, target] = list_ref[jnp.minimum(slot, cap - 1)]

                    slot = slot + flag.astype(jnp.int32)


def pack_column(sizes, cap, column_cap, where, fill, lists):
    return pl.pallas_call(
        functools.partial(pack_column_kernel, sizes, cap, column_cap),
        out_shape=jax.ShapeDtypeStruct((2, column_cap, sizes.unit // 4, sizes.block), F32),
        in_specs=[SMEM, SMEM] + [VMEM] * len(lists),
        out_specs=VMEM,
        scratch_shapes=[pltpu.SMEM((2 * sizes.column_units,), jnp.int32)],
        compiler_params=pltpu.CompilerParams(vmem_limit_bytes=16 * 2**20),
    )(where, fill, *lists)


def own_factor_kernel(sizes, where_ref, fill_ref, w_ref, panel_ref, x_ref, masked, sem):
    own = where_ref[1] * sizes.cols + where_ref[0]
    for u in range(sizes.per_piece):
        for p in range(2):
            at = (pl.ds(u * sizes.unit, sizes.unit), pl.ds(p * sizes.block, sizes.block))
            masked[at] = jnp.where(unit_flag(sizes, fill_ref, own, u, p), panel_ref[at], 0.0)
    masked[...] = dot3(halves(masked[...]), halves(w_ref[...]), NT)
    copy_out = pltpu.make_async_copy(masked, x_ref, sem)
    copy_out.start()
    copy_out.wait()


def own_factor(sizes, where, fill, w, panel):
    return pl.pallas_call(
        functools.partial(own_factor_kernel, sizes),
        out_shape=pltpu.HBM(panel.shape, F32),
        in_specs=[SMEM, SMEM, VMEM, VMEM],
        out_specs=HBM,
        scratch_shapes=[pltpu.VMEM(panel.shape, F32), pltpu.SemaphoreType.DMA],
        compiler_params=pltpu.CompilerParams(vmem_limit_bytes=16 * 2**20),
    )(where, fill, w, panel)


def list_slots_kernel(sizes, where_ref, fill_ref, slot_ref):
    c, r = where_ref[0], where_ref[1]

    @pl.loop(0, sizes.groups)
    def _(shift):
        group = lax.rem(c // 2 + shift, sizes.groups)
        slot = jnp.int32(0)
        for core, side, piece in pool_pieces(sizes, r // 2, group):
            for u in range(sizes.per_piece):
                for p in range(2):
                    flag = unit_flag(sizes, fill_ref, piece, u, p)

                    @pl.when(core == r % 2)
                    def _(slot=slot, flag=flag, side=side, u=u, p=p):
                        at = ((shift * 2 + side) * sizes.per_piece + u) * 2 + p
                        slot_ref[at] = jnp.where(flag, slot, -1)

                    slot = slot + flag.astype(jnp.int32)


def list_slots(sizes, where, fill):
    return pl.pallas_call(
        functools.partial(list_slots_kernel, sizes),
        out_shape=jax.ShapeDtypeStruct((2 * sizes.tiles,), jnp.int32),
        in_specs=[SMEM, SMEM],
        out_specs=SMEM,
        cost_estimate=pl.CostEstimate(flops=2 * 10**10, bytes_accessed=6 * 10**7, transcendentals=0),
    )(where, fill)


def column_factor_kernel(sizes, where_ref, fill_ref, w_ref, *refs):
    lists, (out_ref, column, slots) = refs[:4], refs[4:]
    c, r = where_ref[0], where_ref[1]
    side, core = c % 2, r % 2
    quarter = sizes.unit // 4
    pair_slots(sizes, fill_ref, c // 2, slots)
    column[...] = jnp.zeros_like(column)

    @pl.loop(0, sizes.column_units // 2)
    def _(unit):
        for p in range(2):
            slot = slots[side * sizes.column_units + unit * 2 + p]

            @pl.when(slot >= 0)
            def _(slot=slot, p=p):
                for flip in range(4):
                    from_side = jnp.bitwise_xor(side, flip // 2)
                    from_core = jnp.bitwise_xor(core, flip % 2)
                    at = pl.multiple_of(unit * sizes.unit + (from_side * 2 + from_core) * quarter, quarter)
                    column[pl.ds(at, quarter), pl.ds(p * sizes.block, sizes.block)] = lists[flip][slot]

    w = halves(w_ref[...])
    solved = dot3(w, halves(column[...]), NT)
    out_ref[...] = dot3(w, halves(solved), TN)


def column_factor(sizes, where, fill, w, lists):
    n = w.shape[0]
    return pl.pallas_call(
        functools.partial(column_factor_kernel, sizes),
        out_shape=jax.ShapeDtypeStruct((n, sizes.width), F32),
        in_specs=[SMEM, SMEM, VMEM] + [VMEM] * 4,
        out_specs=VMEM,
        scratch_shapes=[pltpu.VMEM((sizes.width, n), F32), pltpu.SMEM((2 * sizes.column_units,), jnp.int32)],
        compiler_params=pltpu.CompilerParams(vmem_limit_bytes=16 * 2**20),
    )(where, fill, w, *lists)


def update_kernel(sizes, where_ref, slot_ref, column_ref, window_ref, *refs):
    groups, merge = sizes.groups, sizes.merge
    lists, (out_ref, tiles, data, right, out_sems) = refs[: 4 * groups], refs[4 * groups :]
    c, r = where_ref[0], where_ref[1]
    side, core = c % 2, r % 2
    per_group = 2 * sizes.per_piece // merge
    rows = merge * sizes.unit
    quarter = sizes.unit // 4

    def rows_of(t):
        group = lax.rem(c // 2 + t // per_group, groups)
        return pl.ds(pl.multiple_of((group * per_group + t % per_group) * rows, rows), rows)

    def tile_out(t, source):
        return pltpu.make_async_copy(source, out_ref.at[rows_of(t)], out_sems.at[t])

    def slot_of(t, p, part):
        return slot_ref[(t * merge + part) * 2 + p]

    def active(t):
        return jnp.logical_or(slot_of(t, 0, 0) >= 0, slot_of(t, 1, 0) >= 0)

    @pl.loop(0, per_group * groups)
    def _(t):
        pl.when(jnp.logical_not(active(t)))(tile_out(t, window_ref.at[rows_of(t)]).start)

    for p in range(2):
        high, low = halves(column_ref[p * sizes.block : (p + 1) * sizes.block, :])
        for i, part in enumerate((high, low, high)):
            right[p, i * sizes.block : (i + 1) * sizes.block, :] = part

    for group in range(groups):

        @pl.loop(group * per_group, (group + 1) * per_group)
        def _(t, group=group):
            @pl.when(active(t))
            def _():
                tiles[t] = window_ref[rows_of(t), :]
                for p in range(2):

                    @pl.when(slot_of(t, p, 0) >= 0)
                    def _(p=p):
                        for part in range(merge):
                            slot = slot_of(t, p, part)
                            for flip in range(4):
                                from_side = jnp.bitwise_xor(side, flip // 2)
                                from_core = jnp.bitwise_xor(core, flip % 2)
                                at = pl.multiple_of((part * 4 + from_side * 2 + from_core) * quarter, quarter)
                                data[pl.ds(at, quarter), :] = lists[4 * group + flip][slot]
                        high, low = halves(data[...])
                        left = jnp.concatenate([high, high, low], axis=1)
                        tiles[t] = tiles[t] - dot(left, right[p], NN)

                tile_out(t, tiles.at[t]).start()

    @pl.loop(0, per_group * groups)
    def _(t):
        tile_out(t, tiles.at[t]).wait()


def update(sizes, where, slots, column, window, lists):
    rows = sizes.merge * sizes.unit
    tiles = sizes.slab // rows
    return pl.pallas_call(
        functools.partial(update_kernel, sizes),
        out_shape=pltpu.HBM(window.shape, F32),
        in_specs=[SMEM, SMEM, VMEM, VMEM] + [VMEM] * len(lists),
        out_specs=HBM,
        scratch_shapes=[
            pltpu.VMEM((tiles, rows, sizes.width), F32),
            pltpu.VMEM((rows, sizes.block), F32),
            pltpu.VMEM((2, 3 * sizes.block, sizes.width), BF16),
            pltpu.SemaphoreType.DMA((tiles,)),
        ],
        compiler_params=pltpu.CompilerParams(vmem_limit_bytes=30 * 2**20),
    )(where, slots, column, window, *lists)


def swap(value, axis, step):
    size = lax.axis_size(axis)
    return lax.ppermute(value, axis, [(i, i ^ step) for i in range(size)])


def join(index, step, own, other):
    second = (index & step) != 0
    return jnp.where(second, jnp.concatenate([other, own], 0), jnp.concatenate([own, other], 0))


def after(value, *earlier):
    return lax.optimization_barrier((value, *earlier))[0]


def bring(sizes, value, shift):
    pairs = [(i, (i - 2 * shift) % sizes.cols) for i in range(sizes.cols)]
    return lax.ppermute(value, "col", pairs)


def spread_column(sizes, value, step):
    r, c = lax.axis_index("row"), lax.axis_index("col")
    pairs = []
    for at in range(sizes.cols):
        slab = sizes.pair_slab(at // 2)
        for row in range(sizes.rows):
            if (row // 2 ^ slab // 2) % step == 0:
                pairs.append((at * sizes.rows + row, at * sizes.rows + (row ^ step)))
    other = lax.ppermute(value, ("col", "row"), pairs)
    return jnp.where(((r ^ sizes.pair_slab(c // 2)) & step) != 0, other, value)


def per_device(trailing, panel_rows, pivot_block, panel_fill):
    sizes = Sizes(trailing, panel_rows, panel_fill)
    fill = panel_fill.reshape(-1)
    r, c = lax.axis_index("row"), lax.axis_index("col")
    where = jnp.stack([c, r]).astype(jnp.int32)
    side, core = c % 2, r % 2
    quarter = sizes.unit // 4
    split = min(4, pivot_block.shape[0] // 8)
    share = pivot_block.shape[0] // split
    most, column_most = 8 * sizes.per_piece, sizes.column_units
    cap, column_cap = most * 5 // 12, column_most * 3 // 4

    units = panel_rows.reshape(sizes.per_piece, sizes.unit, -1)
    quarters = panel_rows.reshape(sizes.per_piece, 2, 2, quarter, -1)

    def at_core(which):
        return lax.dynamic_index_in_dim(quarters, which, 2, keepdims=False)

    pivot = lax.dynamic_slice_in_dim(pivot_block, r % split * share, share, 0)[None]
    pivot = join(c, 1, pivot, swap(pivot, "col", 1))
    from_core = swap(at_core(1 - core), "row", 1)
    from_core, pivot = lax.optimization_barrier((from_core, pivot))
    both = jnp.stack([at_core(core), from_core])
    from_side = swap(lax.dynamic_index_in_dim(both, 1 - side, 2, keepdims=False), "col", 1)
    step = 2
    while step < sizes.cols:
        pivot = join(c, step, pivot, swap(pivot, "col", step))
        step *= 2

    def run(cap, column_cap, trailing, panel_rows, fill, units, from_core, from_side, pivot):
        own = pack(sizes, cap, where, fill, units, from_core, from_side)
        lists = {0: own}
        first = [s for s in range(1, sizes.groups) if s in sizes.needed]
        later = [s for s in range(1, sizes.groups) if s not in sizes.needed]
        lists |= {s: bring(sizes, own, s) for s in first}
        sides = {0: swap(own, "col", 1)}
        pivot = lax.optimization_barrier((pivot, own))[0]
        parts = [pivot] + ([swap(pivot, "row", 2)] if split == 4 else [])
        parts = [part for value in parts for part in (value, swap(value, "row", 1))]
        near = first[0]
        lists[near], sides[0], *parts = lax.optimization_barrier((lists[near], sides[0], *parts))
        sides[near] = swap(lists[near], "col", 1)
        w = inverse_factor(where, parts)
        held = lax.optimization_barrier((w, sides[0], sides[near], *lists.values()))
        w, sides[0], sides[near] = held[:3]
        lists = dict(zip(lists, held[3:]))

        column = pack_column(sizes, cap, column_cap, where, fill, [lists[s] for s in sizes.needed])
        lists |= {s: bring(sizes, lists[0], s) for s in later}
        sides |= {s: swap(lists[s], "col", 1) for s in first[1:]}
        step = sizes.rows // 2
        while step > 1:
            column = spread_column(sizes, column, step)
            step //= 2
        held = lax.optimization_barrier((fill, w, *(lists[s] for s in later), *(sides[s] for s in first[1:])))
        lists |= dict(zip(later, held[2:]))
        sides |= dict(zip(first[1:], held[2 + len(later) :]))
        slots = list_slots(sizes, where, held[0])
        w, column, slots, *late = lax.optimization_barrier((held[1], column, slots, *(lists[s] for s in later)))
        lists |= dict(zip(later, late))

        across = swap(lax.dynamic_index_in_dim(column, 1 - side, 0, keepdims=False), "col", 1)
        column = lax.dynamic_index_in_dim(column, side, 0, keepdims=False)
        columns = [column, swap(column, "row", 1), across, swap(across, "row", 1)]
        sides |= {s: swap(lists[s], "col", 1) for s in later}
        panel_factor = own_factor(sizes, where, fill, w, panel_rows)
        column = column_factor(sizes, where, fill, w, columns)
        for s in later:
            sides[s], column, panel_factor = lax.optimization_barrier((sides[s], column, panel_factor))
        ordered = []
        for s in range(sizes.groups):
            value, other = lists[s], sides[s]
            ordered += [value, swap(value, "row", 1), other, swap(other, "row", 1)]
        return update(sizes, where, slots, column, trailing, ordered), panel_factor

    operands = (trailing, panel_rows, fill, units, from_core, from_side, pivot)
    return lax.cond(
        fits(sizes, cap, column_cap, fill)[0] != 0,
        functools.partial(run, cap, column_cap),
        functools.partial(run, most, column_most),
        *operands,
    )


def solution(mesh):
    in_specs = (P("row", "col"), P(("row", "col"), None), P("col", None), P())
    out_specs = (P("row", "col"), P(("row", "col"), None))
    return jax.shard_map(
        per_device, mesh=mesh, in_specs=in_specs, out_specs=out_specs, check_vma=False
    )
```

```python
import functools
import math

import jax
import jax.numpy as jnp
from jax import lax
from jax.experimental import pallas as pl
from jax.experimental.pallas import tpu as pltpu
from jax.sharding import PartitionSpec as P

F32, BF16 = jnp.float32, jnp.bfloat16
VMEM = pl.BlockSpec(memory_space=pltpu.VMEM)
SMEM = pl.BlockSpec(memory_space=pltpu.SMEM)
HBM = pl.BlockSpec(memory_space=pltpu.HBM)
COARSE_STEPS = 2
FINE_STEPS = 16
RESIDUAL = 5e-4


def halves(value):
    high = value.astype(BF16)
    return high, (value - high.astype(F32)).astype(BF16)


def dot(a, b, dims):
    return lax.dot_general(a, b, (dims, ((), ())), preferred_element_type=F32)


NN, NT, TN = ((1,), (0,)), ((1,), (1,)), ((0,), (0,))


def dot3(a, b, dims):
    (ah, al), (bh, bl) = a, b
    return dot(ah, bh, dims) + (dot(ah, bl, dims) + dot(al, bh, dims))


def inverse_factor_kernel(where_ref, *refs):
    parts, (w_ref, s_ref) = refs[:-2], refs[-2:]
    n = w_ref.shape[0]
    pieces, share = parts[0].shape[0], parts[0].shape[1]
    own = where_ref[1] % len(parts)
    for flip, ref in enumerate(parts):
        at = jnp.bitwise_xor(own, flip) * share
        for i in range(pieces):
            s_ref[pl.ds(pl.multiple_of(i * len(parts) * share + at, share), share), :] = ref[i]
    rows = lax.broadcasted_iota(jnp.int32, (n, n), 0)
    cols = lax.broadcasted_iota(jnp.int32, (n, n), 1)
    eye = (rows == cols).astype(F32)
    take = jnp.where(rows > cols, 1.0, 0.5 * eye)
    a = s_ref[...]
    diag_row = jnp.sum(a * eye, axis=0, keepdims=True)
    diag_col = jnp.sum(a * eye, axis=1, keepdims=True)
    scale_row, scale_col = lax.rsqrt(diag_row), lax.rsqrt(diag_col)
    scaled = jnp.where(rows == cols, 1.0, a * scale_row * scale_col)
    s_ref[...] = scaled
    scaled_parts = halves(scaled)
    w = eye - take * (scaled - eye)
    for _ in range(COARSE_STEPS):
        wh = w.astype(BF16)
        t = dot(wh, scaled_parts[0], NN).astype(BF16)
        change = take * (dot(t, wh, NT) - eye)
        w = w - dot(change.astype(BF16), wh, NN)
    w_ref[...] = w

    def fine(state):
        step, _ = state
        w = w_ref[...]
        parts = halves(w)
        t = halves(dot3(parts, halves(s_ref[...]), NN))
        residual = dot3(t, parts, NT) - eye
        w_ref[...] = w - dot((take * residual).astype(BF16), parts[0], NN)
        return step + 1, jnp.sum(residual * residual)

    _, left = lax.while_loop(
        lambda state: jnp.logical_and(state[0] < FINE_STEPS, jnp.logical_not(state[1] < RESIDUAL**2)),
        fine,
        (jnp.int32(0), jnp.float32(1.0)),
    )
    done = left < RESIDUAL**2

    @pl.when(jnp.logical_not(done))
    def _():
        w_ref[...] = eye

        def eliminate(j, carry):
            row = s_ref[pl.ds(j, 1), :]
            pick = lax.broadcasted_iota(jnp.int32, (1, n), 1) == j
            pivot = jnp.sum(jnp.where(pick, row, 0.0), axis=1, keepdims=True)
            column = jnp.sum(jnp.where(pick, s_ref[...], 0.0), axis=1, keepdims=True)
            below = lax.broadcasted_iota(jnp.int32, (n, 1), 0) > j
            ratio = jnp.where(below, column / pivot, 0.0)
            s_ref[...] = s_ref[...] - ratio * row
            w_ref[...] = w_ref[...] - ratio * w_ref[pl.ds(j, 1), :]
            return carry

        lax.fori_loop(0, n, eliminate, 0)
        pivots = jnp.sum(s_ref[...] * eye, axis=1, keepdims=True)
        w_ref[...] = w_ref[...] * lax.rsqrt(pivots)

    w_ref[...] = w_ref[...] * scale_row


def inverse_factor(where, parts):
    n = parts[0].shape[-1]
    return pl.pallas_call(
        inverse_factor_kernel,
        out_shape=jax.ShapeDtypeStruct((n, n), F32),
        in_specs=[SMEM] + [VMEM] * len(parts),
        out_specs=VMEM,
        scratch_shapes=[pltpu.VMEM((n, n), F32)],
        compiler_params=pltpu.CompilerParams(vmem_limit_bytes=20 * 2**20),
    )(where, *parts)


class Sizes:
    def __init__(self, trailing, panel_rows, panel_fill):
        self.cols, self.rows = lax.axis_size("col"), lax.axis_size("row")
        self.block = panel_rows.shape[1] // 2
        self.piece = panel_rows.shape[0]
        self.unit = math.gcd(self.piece, self.block)
        self.per_piece = self.piece // self.unit
        self.per_block = self.block // self.unit
        self.slab = self.piece * self.cols
        self.merge = self.per_block if 2 * self.piece % self.block == 0 else 1
        self.width = trailing.shape[1]
        self.tiles = self.cols * self.per_piece

        self.groups = self.cols // 2
        self.column_units = 2 * self.width // self.unit
        self.needed = sorted({s for g in range(self.groups) for s in self.shifts(g)})

    def pair_slab(self, group):
        return 2 * group * self.width // self.slab

    def pair_start(self, group):
        return (2 * group * self.width - self.pair_slab(group) * self.slab) // self.unit

    def shifts(self, group):
        start = self.pair_start(group) * self.unit
        first, last = start // (2 * self.piece), (start + 2 * self.width - 1) // (2 * self.piece)
        return [(g - group) % self.groups for g in range(first, last + 1)]


def unit_flag(sizes, fill_ref, piece_index, unit, panel):
    block = (piece_index * sizes.per_piece + unit) // sizes.per_block
    return fill_ref[block * 2 + panel] != 0


def pool_pieces(sizes, pool_row, pool_col):
    for core in range(2):
        for side in range(2):
            yield core, side, (pool_row * 2 + core) * sizes.cols + pool_col * 2 + side


def pair_flag(sizes, fill_ref, group, index):
    unit = sizes.pair_slab(group) * sizes.tiles + sizes.pair_start(group) + index // 2
    return fill_ref[unit // sizes.per_block * 2 + index % 2] != 0


def fits_kernel(sizes, cap, column_cap, fill_ref, out_ref):
    over = jnp.int32(0)
    for pool_row in range(sizes.rows // 2):
        for pool_col in range(sizes.groups):
            count = jnp.int32(0)
            for _, _, piece in pool_pieces(sizes, pool_row, pool_col):
                for u in range(sizes.per_piece):
                    for p in range(2):
                        count = count + unit_flag(sizes, fill_ref, piece, u, p).astype(jnp.int32)
            over = jnp.maximum(over, count - cap)
    for group in range(sizes.groups):
        for side in range(2):
            count = jnp.int32(0)
            for i in range(sizes.column_units):
                flag = pair_flag(sizes, fill_ref, group, side * sizes.column_units + i)
                count = count + flag.astype(jnp.int32)
            over = jnp.maximum(over, count - column_cap)
    out_ref[0] = (over <= 0).astype(jnp.int32)


def fits(sizes, cap, column_cap, fill):
    return pl.pallas_call(
        functools.partial(fits_kernel, sizes, cap, column_cap),
        out_shape=jax.ShapeDtypeStruct((1,), jnp.int32),
        in_specs=[SMEM],
        out_specs=SMEM,
    )(fill)


def pack_kernel(sizes, cap, where_ref, fill_ref, panel_ref, core_ref, side_ref, out_ref, pool):
    c, r = where_ref[0], where_ref[1]
    side, core = c % 2, r % 2
    quarter = sizes.unit // 4
    own_at = pl.multiple_of((side * 2 + core) * quarter, quarter)
    for u in range(sizes.per_piece):
        pool[core, side, u] = panel_ref[u, pl.ds(own_at, quarter), :]
        pool[1 - core, side, u] = core_ref[u, side]
        pool[core, 1 - side, u] = side_ref[0, u]
        pool[1 - core, 1 - side, u] = side_ref[1, u]
    slot = jnp.int32(0)
    for core_at, side_at, piece in pool_pieces(sizes, r // 2, c // 2):
        for u in range(sizes.per_piece):
            for p in range(2):
                flag = unit_flag(sizes, fill_ref, piece, u, p)

                @pl.when(flag)
                def _(slot=slot, core_at=core_at, side_at=side_at, u=u, p=p):
                    out_ref[jnp.minimum(slot, cap - 1)] = pool[
                        core_at, side_at, u, :, p * sizes.block : (p + 1) * sizes.block
                    ]

                slot = slot + flag.astype(jnp.int32)


def pack(sizes, cap, where, fill, panel, from_core, from_side):
    quarter = sizes.unit // 4
    return pl.pallas_call(
        functools.partial(pack_kernel, sizes, cap),
        out_shape=jax.ShapeDtypeStruct((cap, quarter, sizes.block), F32),
        in_specs=[SMEM, SMEM, VMEM, VMEM, VMEM],
        out_specs=VMEM,
        scratch_shapes=[pltpu.VMEM((2, 2, sizes.per_piece, quarter, 2 * sizes.block), F32)],
        compiler_params=pltpu.CompilerParams(vmem_limit_bytes=16 * 2**20),
    )(where, fill, panel, from_core, from_side)


def pair_slots(sizes, fill_ref, group, slots):
    def step(i, slot):
        flag = pair_flag(sizes, fill_ref, group, i)
        slot = jnp.where(i == sizes.column_units, 0, slot)
        slots[i] = jnp.where(flag, slot, -1)
        return slot + flag.astype(jnp.int32)

    lax.fori_loop(0, 2 * sizes.column_units, step, jnp.int32(0))


def pack_column_kernel(sizes, cap, column_cap, where_ref, fill_ref, *refs):
    lists, (out_ref, slots) = refs[:-2], refs[-2:]
    own = where_ref[0] // 2
    slab, start = sizes.pair_slab(own), sizes.pair_start(own)
    pair_slots(sizes, fill_ref, own, slots)
    for shift, list_ref in zip(sizes.needed, lists):
        group = lax.rem(own + shift, sizes.groups)
        slot = jnp.int32(0)
        for core, side, piece in pool_pieces(sizes, slab // 2, group):
            for u in range(sizes.per_piece):
                for p in range(2):
                    flag = unit_flag(sizes, fill_ref, piece, u, p)
                    index = (((group * 2 + side) * sizes.per_piece + u) - start) * 2 + p
                    inside = jnp.logical_and(index >= 0, index < 2 * sizes.column_units)
                    wanted = jnp.logical_and(jnp.logical_and(flag, inside), slab % 2 == core)

                    @pl.when(wanted)
                    def _(slot=slot, index=index, list_ref=list_ref):
                        index = jnp.clip(index, 0, 2 * sizes.column_units - 1)
                        target = jnp.clip(slots[index], 0, column_cap - 1)
                        out_ref[index // sizes.column_units, target] = list_ref[jnp.minimum(slot, cap - 1)]

                    slot = slot + flag.astype(jnp.int32)


def pack_column(sizes, cap, column_cap, where, fill, lists):
    return pl.pallas_call(
        functools.partial(pack_column_kernel, sizes, cap, column_cap),
        out_shape=jax.ShapeDtypeStruct((2, column_cap, sizes.unit // 4, sizes.block), F32),
        in_specs=[SMEM, SMEM] + [VMEM] * len(lists),
        out_specs=VMEM,
        scratch_shapes=[pltpu.SMEM((2 * sizes.column_units,), jnp.int32)],
        compiler_params=pltpu.CompilerParams(vmem_limit_bytes=20 * 2**20),
    )(where, fill, *lists)


def own_factor_kernel(sizes, where_ref, fill_ref, w_ref, panel_ref, x_ref, slot_ref, masked, sem):
    c, r = where_ref[0], where_ref[1]
    own = r * sizes.cols + c
    for u in range(sizes.per_piece):
        for p in range(2):
            at = (pl.ds(u * sizes.unit, sizes.unit), pl.ds(p * sizes.block, sizes.block))
            masked[at] = jnp.where(unit_flag(sizes, fill_ref, own, u, p), panel_ref[at], 0.0)
    masked[...] = dot3(halves(masked[...]), halves(w_ref[...]), NT)
    copy_out = pltpu.make_async_copy(masked, x_ref, sem)
    copy_out.start()

    @pl.loop(0, sizes.groups)
    def _(shift):
        group = lax.rem(c // 2 + shift, sizes.groups)
        slot = jnp.int32(0)
        for core, side, piece in pool_pieces(sizes, r // 2, group):
            for u in range(sizes.per_piece):
                for p in range(2):
                    flag = unit_flag(sizes, fill_ref, piece, u, p)

                    @pl.when(core == r % 2)
                    def _(slot=slot, flag=flag, side=side, u=u, p=p):
                        at = ((shift * 2 + side) * sizes.per_piece + u) * 2 + p
                        slot_ref[at] = jnp.where(flag, slot, -1)

                    slot = slot + flag.astype(jnp.int32)

    copy_out.wait()


def own_factor(sizes, where, fill, w, panel):
    return pl.pallas_call(
        functools.partial(own_factor_kernel, sizes),
        out_shape=(
            pltpu.HBM(panel.shape, F32),
            jax.ShapeDtypeStruct((2 * sizes.tiles,), jnp.int32),
        ),
        in_specs=[SMEM, SMEM, VMEM, VMEM],
        out_specs=(HBM, SMEM),
        scratch_shapes=[pltpu.VMEM(panel.shape, F32), pltpu.SemaphoreType.DMA],
        compiler_params=pltpu.CompilerParams(vmem_limit_bytes=20 * 2**20),
    )(where, fill, w, panel)


def column_factor_kernel(sizes, where_ref, fill_ref, w_ref, *refs):
    lists, (out_ref, column, slots) = refs[:4], refs[4:]
    c, r = where_ref[0], where_ref[1]
    side, core = c % 2, r % 2
    quarter = sizes.unit // 4
    pair_slots(sizes, fill_ref, c // 2, slots)
    column[...] = jnp.zeros_like(column)

    @pl.loop(0, sizes.column_units // 2)
    def _(unit):
        for p in range(2):
            slot = slots[side * sizes.column_units + unit * 2 + p]

            @pl.when(slot >= 0)
            def _(slot=slot, p=p):
                for flip in range(4):
                    from_side = jnp.bitwise_xor(side, flip // 2)
                    from_core = jnp.bitwise_xor(core, flip % 2)
                    at = pl.multiple_of(unit * sizes.unit + (from_side * 2 + from_core) * quarter, quarter)
                    column[pl.ds(at, quarter), pl.ds(p * sizes.block, sizes.block)] = lists[flip][slot]

    w = halves(w_ref[...])
    solved = dot3(w, halves(column[...]), NT)
    out_ref[...] = dot3(w, halves(solved), TN)


def column_factor(sizes, where, fill, w, lists):
    n = w.shape[0]
    return pl.pallas_call(
        functools.partial(column_factor_kernel, sizes),
        out_shape=jax.ShapeDtypeStruct((n, sizes.width), F32),
        in_specs=[SMEM, SMEM, VMEM] + [VMEM] * 4,
        out_specs=VMEM,
        scratch_shapes=[pltpu.VMEM((sizes.width, n), F32), pltpu.SMEM((2 * sizes.column_units,), jnp.int32)],
        compiler_params=pltpu.CompilerParams(vmem_limit_bytes=20 * 2**20),
    )(where, fill, w, *lists)


def update_kernel(sizes, where_ref, slot_ref, column_ref, window_ref, *refs):
    groups, merge = sizes.groups, sizes.merge
    lists, (out_ref, tiles, data, right, out_sems) = refs[: 4 * groups], refs[4 * groups :]
    c, r = where_ref[0], where_ref[1]
    side, core = c % 2, r % 2
    per_group = 2 * sizes.per_piece // merge
    rows = merge * sizes.unit
    quarter = sizes.unit // 4

    def rows_of(t):
        group = lax.rem(c // 2 + t // per_group, groups)
        return pl.ds(pl.multiple_of((group * per_group + t % per_group) * rows, rows), rows)

    def tile_out(t, source):
        return pltpu.make_async_copy(source, out_ref.at[rows_of(t)], out_sems.at[t])

    def slot_of(t, p, part):
        return slot_ref[(t * merge + part) * 2 + p]

    def active(t):
        return jnp.logical_or(slot_of(t, 0, 0) >= 0, slot_of(t, 1, 0) >= 0)

    @pl.loop(0, per_group * groups)
    def _(t):
        pl.when(jnp.logical_not(active(t)))(tile_out(t, window_ref.at[rows_of(t)]).start)

    for p in range(2):
        high, low = halves(column_ref[p * sizes.block : (p + 1) * sizes.block, :])
        for i, part in enumerate((high, low, high)):
            right[p, i * sizes.block : (i + 1) * sizes.block, :] = part

    for group in range(groups):

        @pl.loop(group * per_group, (group + 1) * per_group)
        def _(t, group=group):
            @pl.when(active(t))
            def _():
                tiles[t] = window_ref[rows_of(t), :]
                for p in range(2):

                    @pl.when(slot_of(t, p, 0) >= 0)
                    def _(p=p):
                        for part in range(merge):
                            slot = slot_of(t, p, part)
                            for flip in range(4):
                                from_side = jnp.bitwise_xor(side, flip // 2)
                                from_core = jnp.bitwise_xor(core, flip % 2)
                                at = pl.multiple_of((part * 4 + from_side * 2 + from_core) * quarter, quarter)
                                data[pl.ds(at, quarter), :] = lists[4 * group + flip][slot]
                        high, low = halves(data[...])
                        left = jnp.concatenate([high, high, low], axis=1)
                        tiles[t] = tiles[t] - dot(left, right[p], NN)

                tile_out(t, tiles.at[t]).start()

    @pl.loop(0, per_group * groups)
    def _(t):
        tile_out(t, tiles.at[t]).wait()


def update(sizes, where, slots, column, window, lists):
    rows = sizes.merge * sizes.unit
    tiles = sizes.slab // rows
    return pl.pallas_call(
        functools.partial(update_kernel, sizes),
        out_shape=pltpu.HBM(window.shape, F32),
        in_specs=[SMEM, SMEM, VMEM, VMEM] + [VMEM] * len(lists),
        out_specs=HBM,
        scratch_shapes=[
            pltpu.VMEM((tiles, rows, sizes.width), F32),
            pltpu.VMEM((rows, sizes.block), F32),
            pltpu.VMEM((2, 3 * sizes.block, sizes.width), BF16),
            pltpu.SemaphoreType.DMA((tiles,)),
        ],
        compiler_params=pltpu.CompilerParams(vmem_limit_bytes=36 * 2**20),
    )(where, slots, column, window, *lists)


def swap(value, axis, step):
    size = lax.axis_size(axis)
    return lax.ppermute(value, axis, [(i, i ^ step) for i in range(size)])


def join(index, step, own, other):
    second = (index & step) != 0
    return jnp.where(second, jnp.concatenate([other, own], 0), jnp.concatenate([own, other], 0))


def after(value, *earlier):
    return lax.optimization_barrier((value, *earlier))[0]


def bring(sizes, value, shift):
    pairs = [(i, (i - 2 * shift) % sizes.cols) for i in range(sizes.cols)]
    return lax.ppermute(value, "col", pairs)


def spread_column(sizes, value, step):
    r, c = lax.axis_index("row"), lax.axis_index("col")
    pairs = []
    for at in range(sizes.cols):
        slab = sizes.pair_slab(at // 2)
        for row in range(sizes.rows):
            if (row // 2 ^ slab // 2) % step == 0:
                pairs.append((at * sizes.rows + row, at * sizes.rows + (row ^ step)))
    other = lax.ppermute(value, ("col", "row"), pairs)
    return jnp.where(((r ^ sizes.pair_slab(c // 2)) & step) != 0, other, value)


def per_device(trailing, panel_rows, pivot_block, panel_fill):
    sizes = Sizes(trailing, panel_rows, panel_fill)
    fill = panel_fill.reshape(-1)
    r, c = lax.axis_index("row"), lax.axis_index("col")
    where = jnp.stack([c, r]).astype(jnp.int32)
    side, core = c % 2, r % 2
    quarter = sizes.unit // 4
    split = min(4, pivot_block.shape[0] // 8)
    share = pivot_block.shape[0] // split
    most, column_most = 8 * sizes.per_piece, sizes.column_units
    cap, column_cap = most * 5 // 12, column_most * 3 // 4

    units = panel_rows.reshape(sizes.per_piece, sizes.unit, -1)
    quarters = panel_rows.reshape(sizes.per_piece, 2, 2, quarter, -1)

    def at_core(which):
        return lax.dynamic_index_in_dim(quarters, which, 2, keepdims=False)

    pivot = lax.dynamic_slice_in_dim(pivot_block, r % split * share, share, 0)[None]
    pivot = join(c, 1, pivot, swap(pivot, "col", 1))
    from_core = swap(at_core(1 - core), "row", 1)
    from_core, pivot = lax.optimization_barrier((from_core, pivot))
    both = jnp.stack([at_core(core), from_core])
    from_side = swap(lax.dynamic_index_in_dim(both, 1 - side, 2, keepdims=False), "col", 1)
    step = 2
    while step < sizes.cols:
        pivot = join(c, step, pivot, swap(pivot, "col", step))
        step *= 2

    def run(cap, column_cap, trailing, panel_rows, fill, units, from_core, from_side, pivot):
        own = pack(sizes, cap, where, fill, units, from_core, from_side)
        lists = {0: own}
        first = [s for s in range(1, sizes.groups) if s in sizes.needed]
        later = [s for s in range(1, sizes.groups) if s not in sizes.needed]
        lists |= {s: bring(sizes, own, s) for s in first}
        sides = {0: swap(own, "col", 1)}
        parts = [pivot] + ([swap(pivot, "row", 2)] if split == 4 else [])
        parts = [part for value in parts for part in (value, swap(value, "row", 1))]
        near = first[0]
        lists[near], sides[0], *parts = lax.optimization_barrier((lists[near], sides[0], *parts))
        sides[near] = swap(lists[near], "col", 1)
        w = inverse_factor(where, parts)
        held = lax.optimization_barrier((w, sides[0], sides[near], *lists.values()))
        w, sides[0], sides[near] = held[:3]
        lists = dict(zip(lists, held[3:]))

        column = pack_column(sizes, cap, column_cap, where, fill, [lists[s] for s in sizes.needed])
        lists |= {s: bring(sizes, lists[0], s) for s in later}
        sides |= {s: swap(lists[s], "col", 1) for s in first[1:]}
        step = sizes.rows // 2
        while step > 1:
            column = spread_column(sizes, column, step)
            step //= 2
        across = swap(lax.dynamic_index_in_dim(column, 1 - side, 0, keepdims=False), "col", 1)
        column = lax.dynamic_index_in_dim(column, side, 0, keepdims=False)
        columns = [column, swap(column, "row", 1), across, swap(across, "row", 1)]
        panel_factor, slots = own_factor(sizes, where, fill, w, panel_rows)
        for s in later:
            lists[s] = lax.optimization_barrier((lists[s], slots, *(sides[j] for j in first)))[0]
            sides[s] = swap(lists[s], "col", 1)
        column = column_factor(sizes, where, fill, w, columns)
        for s in later:
            sides[s], column = lax.optimization_barrier((sides[s], column))
        ordered = []
        for s in range(sizes.groups):
            value, other = lists[s], sides[s]
            ordered += [value, swap(value, "row", 1), other, swap(other, "row", 1)]
        return update(sizes, where, slots, column, trailing, ordered), panel_factor

    operands = (trailing, panel_rows, fill, units, from_core, from_side, pivot)
    return lax.cond(
        fits(sizes, cap, column_cap, fill)[0] != 0,
        functools.partial(run, cap, column_cap),
        functools.partial(run, most, column_most),
        *operands,
    )


def solution(mesh):
    in_specs = (P("row", "col"), P(("row", "col"), None), P("col", None), P())
    out_specs = (P("row", "col"), P(("row", "col"), None))
    return jax.shard_map(
        per_device, mesh=mesh, in_specs=in_specs, out_specs=out_specs, check_vma=False
    )
```

```python
import functools
import math

import jax
import jax.numpy as jnp
from jax import lax
from jax.experimental import pallas as pl
from jax.experimental.pallas import tpu as pltpu
from jax.sharding import PartitionSpec as P

F32, BF16 = jnp.float32, jnp.bfloat16
VMEM = pl.BlockSpec(memory_space=pltpu.VMEM)
SMEM = pl.BlockSpec(memory_space=pltpu.SMEM)
HBM = pl.BlockSpec(memory_space=pltpu.HBM)
COARSE_STEPS = 2
FINE_STEPS = 16
RESIDUAL = 5e-4


def halves(value):
    high = value.astype(BF16)
    return high, (value - high.astype(F32)).astype(BF16)


def dot(a, b, dims):
    return lax.dot_general(a, b, (dims, ((), ())), preferred_element_type=F32)


NN, NT, TN = ((1,), (0,)), ((1,), (1,)), ((0,), (0,))


def dot3(a, b, dims):
    (ah, al), (bh, bl) = a, b
    return dot(ah, bh, dims) + (dot(ah, bl, dims) + dot(al, bh, dims))


def inverse_factor_kernel(where_ref, *refs):
    parts, (w_ref, s_ref) = refs[:-2], refs[-2:]
    n = w_ref.shape[0]
    pieces, share = parts[0].shape[0], parts[0].shape[1]
    own = where_ref[1] % len(parts)
    for flip, ref in enumerate(parts):
        at = jnp.bitwise_xor(own, flip) * share
        for i in range(pieces):
            s_ref[pl.ds(pl.multiple_of(i * len(parts) * share + at, share), share), :] = ref[i]
    rows = lax.broadcasted_iota(jnp.int32, (n, n), 0)
    cols = lax.broadcasted_iota(jnp.int32, (n, n), 1)
    eye = (rows == cols).astype(F32)
    take = jnp.where(rows > cols, 1.0, 0.5 * eye)
    a = s_ref[...]
    diag_row = jnp.sum(a * eye, axis=0, keepdims=True)
    diag_col = jnp.sum(a * eye, axis=1, keepdims=True)
    scale_row, scale_col = lax.rsqrt(diag_row), lax.rsqrt(diag_col)
    scaled = jnp.where(rows == cols, 1.0, a * scale_row * scale_col)
    s_ref[...] = scaled
    scaled_parts = halves(scaled)
    w = eye - take * (scaled - eye)
    for _ in range(COARSE_STEPS):
        wh = w.astype(BF16)
        t = dot(wh, scaled_parts[0], NN).astype(BF16)
        change = take * (dot(t, wh, NT) - eye)
        w = w - dot(change.astype(BF16), wh, NN)
    w_ref[...] = w

    def fine(state):
        step, _ = state
        w = w_ref[...]
        parts = halves(w)
        t = halves(dot3(parts, halves(s_ref[...]), NN))
        residual = dot3(t, parts, NT) - eye
        w_ref[...] = w - dot((take * residual).astype(BF16), parts[0], NN)
        return step + 1, jnp.sum(residual * residual)

    _, left = lax.while_loop(
        lambda state: jnp.logical_and(state[0] < FINE_STEPS, jnp.logical_not(state[1] < RESIDUAL**2)),
        fine,
        (jnp.int32(0), jnp.float32(1.0)),
    )
    done = left < RESIDUAL**2

    @pl.when(jnp.logical_not(done))
    def _():
        w_ref[...] = eye

        def eliminate(j, carry):
            row = s_ref[pl.ds(j, 1), :]
            pick = lax.broadcasted_iota(jnp.int32, (1, n), 1) == j
            pivot = jnp.sum(jnp.where(pick, row, 0.0), axis=1, keepdims=True)
            column = jnp.sum(jnp.where(pick, s_ref[...], 0.0), axis=1, keepdims=True)
            below = lax.broadcasted_iota(jnp.int32, (n, 1), 0) > j
            ratio = jnp.where(below, column / pivot, 0.0)
            s_ref[...] = s_ref[...] - ratio * row
            w_ref[...] = w_ref[...] - ratio * w_ref[pl.ds(j, 1), :]
            return carry

        lax.fori_loop(0, n, eliminate, 0)
        pivots = jnp.sum(s_ref[...] * eye, axis=1, keepdims=True)
        w_ref[...] = w_ref[...] * lax.rsqrt(pivots)

    w_ref[...] = w_ref[...] * scale_row


def inverse_factor(where, parts):
    n = parts[0].shape[-1]
    return pl.pallas_call(
        inverse_factor_kernel,
        out_shape=jax.ShapeDtypeStruct((n, n), F32),
        in_specs=[SMEM] + [VMEM] * len(parts),
        out_specs=VMEM,
        scratch_shapes=[pltpu.VMEM((n, n), F32)],
        compiler_params=pltpu.CompilerParams(vmem_limit_bytes=20 * 2**20),
    )(where, *parts)


class Sizes:
    def __init__(self, trailing, panel_rows, panel_fill):
        self.cols, self.rows = lax.axis_size("col"), lax.axis_size("row")
        self.block = panel_rows.shape[1] // 2
        self.piece = panel_rows.shape[0]
        self.unit = math.gcd(self.piece, self.block)
        self.per_piece = self.piece // self.unit
        self.per_block = self.block // self.unit
        self.slab = self.piece * self.cols
        self.merge = self.per_block if 2 * self.piece % self.block == 0 else 1
        self.width = trailing.shape[1]
        self.tiles = self.cols * self.per_piece

        self.groups = self.cols // 2
        self.column_units = 2 * self.width // self.unit
        self.needed = sorted({s for g in range(self.groups) for s in self.shifts(g)})

    def pair_slab(self, group):
        return 2 * group * self.width // self.slab

    def pair_start(self, group):
        return (2 * group * self.width - self.pair_slab(group) * self.slab) // self.unit

    def shifts(self, group):
        start = self.pair_start(group) * self.unit
        first, last = start // (2 * self.piece), (start + 2 * self.width - 1) // (2 * self.piece)
        return [(g - group) % self.groups for g in range(first, last + 1)]


def unit_flag(sizes, fill_ref, piece_index, unit, panel):
    block = (piece_index * sizes.per_piece + unit) // sizes.per_block
    return fill_ref[block * 2 + panel] != 0


def pool_pieces(sizes, pool_row, pool_col):
    for core in range(2):
        for side in range(2):
            yield core, side, (pool_row * 2 + core) * sizes.cols + pool_col * 2 + side


def pair_flag(sizes, fill_ref, group, index):
    unit = sizes.pair_slab(group) * sizes.tiles + sizes.pair_start(group) + index // 2
    return fill_ref[unit // sizes.per_block * 2 + index % 2] != 0


def level_kernel(sizes, levels, fill_ref, out_ref):
    pool_most, column_most = jnp.int32(0), jnp.int32(0)
    for pool_row in range(sizes.rows // 2):
        for pool_col in range(sizes.groups):
            count = jnp.int32(0)
            for _, _, piece in pool_pieces(sizes, pool_row, pool_col):
                for u in range(sizes.per_piece):
                    for p in range(2):
                        count = count + unit_flag(sizes, fill_ref, piece, u, p).astype(jnp.int32)
            pool_most = jnp.maximum(pool_most, count)
    for group in range(sizes.groups):
        for side in range(2):
            count = jnp.int32(0)
            for i in range(sizes.column_units):
                flag = pair_flag(sizes, fill_ref, group, side * sizes.column_units + i)
                count = count + flag.astype(jnp.int32)
            column_most = jnp.maximum(column_most, count)
    level = jnp.int32(0)
    for cap, column_cap in levels[:-1]:
        fits = jnp.logical_and(pool_most <= cap, column_most <= column_cap)
        level = level + jnp.logical_not(fits).astype(jnp.int32)
    out_ref[0] = level


def level_of(sizes, levels, fill):
    return pl.pallas_call(
        functools.partial(level_kernel, sizes, levels),
        out_shape=jax.ShapeDtypeStruct((1,), jnp.int32),
        in_specs=[SMEM],
        out_specs=SMEM,
    )(fill)


def pack_kernel(sizes, cap, where_ref, fill_ref, panel_ref, core_ref, side_ref, out_ref, pool):
    c, r = where_ref[0], where_ref[1]
    side, core = c % 2, r % 2
    quarter = sizes.unit // 4
    own_at = pl.multiple_of((side * 2 + core) * quarter, quarter)
    for u in range(sizes.per_piece):
        pool[core, side, u] = panel_ref[u, pl.ds(own_at, quarter), :]
        pool[1 - core, side, u] = core_ref[u, side]
        pool[core, 1 - side, u] = side_ref[0, u]
        pool[1 - core, 1 - side, u] = side_ref[1, u]
    slot = jnp.int32(0)
    for core_at, side_at, piece in pool_pieces(sizes, r // 2, c // 2):
        for u in range(sizes.per_piece):
            for p in range(2):
                flag = unit_flag(sizes, fill_ref, piece, u, p)

                @pl.when(flag)
                def _(slot=slot, core_at=core_at, side_at=side_at, u=u, p=p):
                    out_ref[jnp.minimum(slot, cap - 1)] = pool[
                        core_at, side_at, u, :, p * sizes.block : (p + 1) * sizes.block
                    ]

                slot = slot + flag.astype(jnp.int32)


def pack(sizes, cap, where, fill, panel, from_core, from_side):
    quarter = sizes.unit // 4
    return pl.pallas_call(
        functools.partial(pack_kernel, sizes, cap),
        out_shape=jax.ShapeDtypeStruct((cap, quarter, sizes.block), F32),
        in_specs=[SMEM, SMEM, VMEM, VMEM, VMEM],
        out_specs=VMEM,
        scratch_shapes=[pltpu.VMEM((2, 2, sizes.per_piece, quarter, 2 * sizes.block), F32)],
        compiler_params=pltpu.CompilerParams(vmem_limit_bytes=16 * 2**20),
    )(where, fill, panel, from_core, from_side)


def pair_slots(sizes, fill_ref, group, slots):
    def step(i, slot):
        flag = pair_flag(sizes, fill_ref, group, i)
        slot = jnp.where(i == sizes.column_units, 0, slot)
        slots[i] = jnp.where(flag, slot, -1)
        return slot + flag.astype(jnp.int32)

    lax.fori_loop(0, 2 * sizes.column_units, step, jnp.int32(0))


def pack_column_kernel(sizes, cap, column_cap, where_ref, fill_ref, *refs):
    lists, (out_ref, slots) = refs[:-2], refs[-2:]
    own = where_ref[0] // 2
    slab, start = sizes.pair_slab(own), sizes.pair_start(own)
    pair_slots(sizes, fill_ref, own, slots)
    for shift, list_ref in zip(sizes.needed, lists):
        group = lax.rem(own + shift, sizes.groups)
        slot = jnp.int32(0)
        for core, side, piece in pool_pieces(sizes, slab // 2, group):
            for u in range(sizes.per_piece):
                for p in range(2):
                    flag = unit_flag(sizes, fill_ref, piece, u, p)
                    index = (((group * 2 + side) * sizes.per_piece + u) - start) * 2 + p
                    inside = jnp.logical_and(index >= 0, index < 2 * sizes.column_units)
                    wanted = jnp.logical_and(jnp.logical_and(flag, inside), slab % 2 == core)

                    @pl.when(wanted)
                    def _(slot=slot, index=index, list_ref=list_ref):
                        index = jnp.clip(index, 0, 2 * sizes.column_units - 1)
                        target = jnp.clip(slots[index], 0, column_cap - 1)
                        out_ref[index // sizes.column_units, target] = list_ref[jnp.minimum(slot, cap - 1)]

                    slot = slot + flag.astype(jnp.int32)


def pack_column(sizes, cap, column_cap, where, fill, lists):
    return pl.pallas_call(
        functools.partial(pack_column_kernel, sizes, cap, column_cap),
        out_shape=jax.ShapeDtypeStruct((2, column_cap, sizes.unit // 4, sizes.block), F32),
        in_specs=[SMEM, SMEM] + [VMEM] * len(lists),
        out_specs=VMEM,
        scratch_shapes=[pltpu.SMEM((2 * sizes.column_units,), jnp.int32)],
        compiler_params=pltpu.CompilerParams(vmem_limit_bytes=20 * 2**20),
    )(where, fill, *lists)


def own_factor_kernel(sizes, where_ref, fill_ref, w_ref, panel_ref, x_ref, slot_ref, masked, sem):
    c, r = where_ref[0], where_ref[1]
    own = r * sizes.cols + c
    for u in range(sizes.per_piece):
        for p in range(2):
            at = (pl.ds(u * sizes.unit, sizes.unit), pl.ds(p * sizes.block, sizes.block))
            masked[at] = jnp.where(unit_flag(sizes, fill_ref, own, u, p), panel_ref[at], 0.0)
    masked[...] = dot3(halves(masked[...]), halves(w_ref[...]), NT)
    copy_out = pltpu.make_async_copy(masked, x_ref, sem)
    copy_out.start()

    @pl.loop(0, sizes.groups)
    def _(shift):
        group = lax.rem(c // 2 + shift, sizes.groups)
        slot = jnp.int32(0)
        for core, side, piece in pool_pieces(sizes, r // 2, group):
            for u in range(sizes.per_piece):
                for p in range(2):
                    flag = unit_flag(sizes, fill_ref, piece, u, p)

                    @pl.when(core == r % 2)
                    def _(slot=slot, flag=flag, side=side, u=u, p=p):
                        at = ((shift * 2 + side) * sizes.per_piece + u) * 2 + p
                        slot_ref[at] = jnp.where(flag, slot, -1)

                    slot = slot + flag.astype(jnp.int32)

    copy_out.wait()


def own_factor(sizes, where, fill, w, panel):
    return pl.pallas_call(
        functools.partial(own_factor_kernel, sizes),
        out_shape=(
            pltpu.HBM(panel.shape, F32),
            jax.ShapeDtypeStruct((2 * sizes.tiles,), jnp.int32),
        ),
        in_specs=[SMEM, SMEM, VMEM, VMEM],
        out_specs=(HBM, SMEM),
        scratch_shapes=[pltpu.VMEM(panel.shape, F32), pltpu.SemaphoreType.DMA],
        compiler_params=pltpu.CompilerParams(vmem_limit_bytes=20 * 2**20),
    )(where, fill, w, panel)


def column_factor_kernel(sizes, where_ref, fill_ref, w_ref, *refs):
    lists, (out_ref, column, slots) = refs[:4], refs[4:]
    c, r = where_ref[0], where_ref[1]
    side, core = c % 2, r % 2
    quarter = sizes.unit // 4
    pair_slots(sizes, fill_ref, c // 2, slots)
    column[...] = jnp.zeros_like(column)

    @pl.loop(0, sizes.column_units // 2)
    def _(unit):
        for p in range(2):
            slot = slots[side * sizes.column_units + unit * 2 + p]

            @pl.when(slot >= 0)
            def _(slot=slot, p=p):
                for flip in range(4):
                    from_side = jnp.bitwise_xor(side, flip // 2)
                    from_core = jnp.bitwise_xor(core, flip % 2)
                    at = pl.multiple_of(unit * sizes.unit + (from_side * 2 + from_core) * quarter, quarter)
                    column[pl.ds(at, quarter), pl.ds(p * sizes.block, sizes.block)] = lists[flip][slot]

    w = halves(w_ref[...])
    solved = dot3(w, halves(column[...]), NT)
    out_ref[...] = dot3(w, halves(solved), TN)


def column_factor(sizes, where, fill, w, lists):
    n = w.shape[0]
    return pl.pallas_call(
        functools.partial(column_factor_kernel, sizes),
        out_shape=jax.ShapeDtypeStruct((n, sizes.width), F32),
        in_specs=[SMEM, SMEM, VMEM] + [VMEM] * 4,
        out_specs=VMEM,
        scratch_shapes=[pltpu.VMEM((sizes.width, n), F32), pltpu.SMEM((2 * sizes.column_units,), jnp.int32)],
        compiler_params=pltpu.CompilerParams(vmem_limit_bytes=20 * 2**20),
    )(where, fill, w, *lists)


def update_kernel(sizes, where_ref, slot_ref, column_ref, window_ref, *refs):
    groups, merge = sizes.groups, sizes.merge
    lists, (out_ref, tiles, data, right, out_sems) = refs[: 4 * groups], refs[4 * groups :]
    c, r = where_ref[0], where_ref[1]
    side, core = c % 2, r % 2
    per_group = 2 * sizes.per_piece // merge
    rows = merge * sizes.unit
    quarter = sizes.unit // 4

    def rows_of(t):
        group = lax.rem(c // 2 + t // per_group, groups)
        return pl.ds(pl.multiple_of((group * per_group + t % per_group) * rows, rows), rows)

    def tile_out(t, source):
        return pltpu.make_async_copy(source, out_ref.at[rows_of(t)], out_sems.at[t])

    def slot_of(t, p, part):
        return slot_ref[(t * merge + part) * 2 + p]

    def active(t):
        return jnp.logical_or(slot_of(t, 0, 0) >= 0, slot_of(t, 1, 0) >= 0)

    @pl.loop(0, per_group * groups)
    def _(t):
        pl.when(jnp.logical_not(active(t)))(tile_out(t, window_ref.at[rows_of(t)]).start)

    for p in range(2):
        high, low = halves(column_ref[p * sizes.block : (p + 1) * sizes.block, :])
        for i, part in enumerate((high, low, high)):
            right[p, i * sizes.block : (i + 1) * sizes.block, :] = part

    for group in range(groups):

        @pl.loop(group * per_group, (group + 1) * per_group)
        def _(t, group=group):
            @pl.when(active(t))
            def _():
                tiles[t] = window_ref[rows_of(t), :]
                for p in range(2):

                    @pl.when(slot_of(t, p, 0) >= 0)
                    def _(p=p):
                        for part in range(merge):
                            slot = slot_of(t, p, part)
                            for flip in range(4):
                                from_side = jnp.bitwise_xor(side, flip // 2)
                                from_core = jnp.bitwise_xor(core, flip % 2)
                                at = pl.multiple_of((part * 4 + from_side * 2 + from_core) * quarter, quarter)
                                data[pl.ds(at, quarter), :] = lists[4 * group + flip][slot]
                        high, low = halves(data[...])
                        left = jnp.concatenate([high, high, low], axis=1)
                        tiles[t] = tiles[t] - dot(left, right[p], NN)

                tile_out(t, tiles.at[t]).start()

    @pl.loop(0, per_group * groups)
    def _(t):
        tile_out(t, tiles.at[t]).wait()


def update(sizes, where, slots, column, window, lists):
    rows = sizes.merge * sizes.unit
    tiles = sizes.slab // rows
    return pl.pallas_call(
        functools.partial(update_kernel, sizes),
        out_shape=pltpu.HBM(window.shape, F32),
        in_specs=[SMEM, SMEM, VMEM, VMEM] + [VMEM] * len(lists),
        out_specs=HBM,
        scratch_shapes=[
            pltpu.VMEM((tiles, rows, sizes.width), F32),
            pltpu.VMEM((rows, sizes.block), F32),
            pltpu.VMEM((2, 3 * sizes.block, sizes.width), BF16),
            pltpu.SemaphoreType.DMA((tiles,)),
        ],
        compiler_params=pltpu.CompilerParams(vmem_limit_bytes=36 * 2**20),
    )(where, slots, column, window, *lists)


def swap(value, axis, step):
    size = lax.axis_size(axis)
    return lax.ppermute(value, axis, [(i, i ^ step) for i in range(size)])


def join(index, step, own, other):
    second = (index & step) != 0
    return jnp.where(second, jnp.concatenate([other, own], 0), jnp.concatenate([own, other], 0))


def after(value, *earlier):
    return lax.optimization_barrier((value, *earlier))[0]


def bring(sizes, value, shift):
    pairs = [(i, (i - 2 * shift) % sizes.cols) for i in range(sizes.cols)]
    return lax.ppermute(value, "col", pairs)


def spread_column(sizes, value, step):
    r, c = lax.axis_index("row"), lax.axis_index("col")
    pairs = []
    for at in range(sizes.cols):
        slab = sizes.pair_slab(at // 2)
        for row in range(sizes.rows):
            if (row // 2 ^ slab // 2) % step == 0:
                pairs.append((at * sizes.rows + row, at * sizes.rows + (row ^ step)))
    other = lax.ppermute(value, ("col", "row"), pairs)
    return jnp.where(((r ^ sizes.pair_slab(c // 2)) & step) != 0, other, value)


def per_device(trailing, panel_rows, pivot_block, panel_fill):
    sizes = Sizes(trailing, panel_rows, panel_fill)
    fill = panel_fill.reshape(-1)
    r, c = lax.axis_index("row"), lax.axis_index("col")
    where = jnp.stack([c, r]).astype(jnp.int32)
    side, core = c % 2, r % 2
    quarter = sizes.unit // 4
    split = min(4, pivot_block.shape[0] // 8)
    share = pivot_block.shape[0] // split
    most, column_most = 8 * sizes.per_piece, sizes.column_units
    levels = [(most // 3, column_most // 2), (most * 5 // 12, column_most * 3 // 4), (most, column_most)]

    units = panel_rows.reshape(sizes.per_piece, sizes.unit, -1)
    quarters = panel_rows.reshape(sizes.per_piece, 2, 2, quarter, -1)

    def at_core(which):
        return lax.dynamic_index_in_dim(quarters, which, 2, keepdims=False)

    pivot = lax.dynamic_slice_in_dim(pivot_block, r % split * share, share, 0)[None]
    pivot = join(c, 1, pivot, swap(pivot, "col", 1))
    from_core = swap(at_core(1 - core), "row", 1)
    from_core, pivot = lax.optimization_barrier((from_core, pivot))
    both = jnp.stack([at_core(core), from_core])
    from_side = swap(lax.dynamic_index_in_dim(both, 1 - side, 2, keepdims=False), "col", 1)
    step = 2
    while step < sizes.cols:
        pivot = join(c, step, pivot, swap(pivot, "col", step))
        step *= 2

    def run(cap, column_cap, trailing, panel_rows, fill, units, from_core, from_side, pivot):
        own = pack(sizes, cap, where, fill, units, from_core, from_side)
        lists = {0: own}
        first = [s for s in range(1, sizes.groups) if s in sizes.needed]
        later = [s for s in range(1, sizes.groups) if s not in sizes.needed]
        lists |= {s: bring(sizes, own, s) for s in first}
        sides = {0: swap(own, "col", 1)}
        parts = [pivot] + ([swap(pivot, "row", 2)] if split == 4 else [])
        parts = [part for value in parts for part in (value, swap(value, "row", 1))]
        near = first[0]
        lists[near], sides[0], *parts = lax.optimization_barrier((lists[near], sides[0], *parts))
        sides[near] = swap(lists[near], "col", 1)
        w = inverse_factor(where, parts)
        held = lax.optimization_barrier((w, sides[0], sides[near], *lists.values()))
        w, sides[0], sides[near] = held[:3]
        lists = dict(zip(lists, held[3:]))

        column = pack_column(sizes, cap, column_cap, where, fill, [lists[s] for s in sizes.needed])
        lists |= {s: bring(sizes, lists[0], s) for s in later}
        sides |= {s: swap(lists[s], "col", 1) for s in first[1:]}
        step = sizes.rows // 2
        while step > 1:
            column = spread_column(sizes, column, step)
            step //= 2
        panel_factor, slots = own_factor(sizes, where, fill, w, panel_rows)
        column, slots = lax.optimization_barrier((column, slots))
        across = swap(lax.dynamic_index_in_dim(column, 1 - side, 0, keepdims=False), "col", 1)
        column = lax.dynamic_index_in_dim(column, side, 0, keepdims=False)
        columns = [column, swap(column, "row", 1), across, swap(across, "row", 1)]
        for s in later:
            lists[s] = lax.optimization_barrier((lists[s], slots, *(sides[j] for j in first)))[0]
            sides[s] = swap(lists[s], "col", 1)
        column = column_factor(sizes, where, fill, w, columns)
        for s in later:
            sides[s], column = lax.optimization_barrier((sides[s], column))
        ordered = []
        for s in range(sizes.groups):
            value, other = lists[s], sides[s]
            ordered += [value, swap(value, "row", 1), other, swap(other, "row", 1)]
        return update(sizes, where, slots, column, trailing, ordered), panel_factor

    operands = (trailing, panel_rows, fill, units, from_core, from_side, pivot)
    branches = [functools.partial(run, *level) for level in levels]
    return lax.switch(level_of(sizes, levels, fill)[0], branches, *operands)


def solution(mesh):
    in_specs = (P("row", "col"), P(("row", "col"), None), P("col", None), P())
    out_specs = (P("row", "col"), P(("row", "col"), None))
    return jax.shard_map(
        per_device, mesh=mesh, in_specs=in_specs, out_specs=out_specs, check_vma=False
    )
```

```python
import functools
import math

import jax
import jax.numpy as jnp
from jax import lax
from jax.experimental import pallas as pl
from jax.experimental.pallas import tpu as pltpu
from jax.sharding import PartitionSpec as P

F32, BF16 = jnp.float32, jnp.bfloat16
VMEM = pl.BlockSpec(memory_space=pltpu.VMEM)
SMEM = pl.BlockSpec(memory_space=pltpu.SMEM)
HBM = pl.BlockSpec(memory_space=pltpu.HBM)
COARSE_STEPS = 2
FINE_STEPS = 16
RESIDUAL = 5e-4
STAGES = 16


def halves(value):
    high = value.astype(BF16)
    return high, (value - high.astype(F32)).astype(BF16)


def dot(a, b, dims):
    return lax.dot_general(a, b, (dims, ((), ())), preferred_element_type=F32)


NN, NT, TN = ((1,), (0,)), ((1,), (1,)), ((0,), (0,))


def dot3(a, b, dims):
    (ah, al), (bh, bl) = a, b
    return dot(ah, bh, dims) + (dot(ah, bl, dims) + dot(al, bh, dims))


def inverse_factor_kernel(where_ref, window_ref, *refs):
    parts, (w_ref, staged_ref, s_ref, sems) = refs[:-4], refs[-4:]
    n = w_ref.shape[0]
    rows_each = window_ref.shape[0] // STAGES
    stages = []
    for i in range(STAGES):
        at = pl.ds(i * rows_each, rows_each)
        stages.append(pltpu.make_async_copy(window_ref.at[at], staged_ref.at[at], sems.at[i]))
        stages[i].start()
    pieces, share = parts[0].shape[0], parts[0].shape[1]
    own = where_ref[1] % len(parts)
    for flip, ref in enumerate(parts):
        at = jnp.bitwise_xor(own, flip) * share
        for i in range(pieces):
            s_ref[pl.ds(pl.multiple_of(i * len(parts) * share + at, share), share), :] = ref[i]
    rows = lax.broadcasted_iota(jnp.int32, (n, n), 0)
    cols = lax.broadcasted_iota(jnp.int32, (n, n), 1)
    eye = (rows == cols).astype(F32)
    take = jnp.where(rows > cols, 1.0, 0.5 * eye)
    a = s_ref[...]
    diag_row = jnp.sum(a * eye, axis=0, keepdims=True)
    diag_col = jnp.sum(a * eye, axis=1, keepdims=True)
    scale_row, scale_col = lax.rsqrt(diag_row), lax.rsqrt(diag_col)
    scaled = jnp.where(rows == cols, 1.0, a * scale_row * scale_col)
    s_ref[...] = scaled
    scaled_parts = halves(scaled)
    w = eye - take * (scaled - eye)
    for _ in range(COARSE_STEPS):
        wh = w.astype(BF16)
        t = dot(wh, scaled_parts[0], NN).astype(BF16)
        change = take * (dot(t, wh, NT) - eye)
        w = w - dot(change.astype(BF16), wh, NN)
    w_ref[...] = w

    def fine(state):
        step, _ = state
        w = w_ref[...]
        parts = halves(w)
        t = halves(dot3(parts, halves(s_ref[...]), NN))
        residual = dot3(t, parts, NT) - eye
        w_ref[...] = w - dot((take * residual).astype(BF16), parts[0], NN)
        return step + 1, jnp.sum(residual * residual)

    _, left = lax.while_loop(
        lambda state: jnp.logical_and(state[0] < FINE_STEPS, jnp.logical_not(state[1] < RESIDUAL**2)),
        fine,
        (jnp.int32(0), jnp.float32(1.0)),
    )
    done = left < RESIDUAL**2

    @pl.when(jnp.logical_not(done))
    def _():
        w_ref[...] = eye

        def eliminate(j, carry):
            row = s_ref[pl.ds(j, 1), :]
            pick = lax.broadcasted_iota(jnp.int32, (1, n), 1) == j
            pivot = jnp.sum(jnp.where(pick, row, 0.0), axis=1, keepdims=True)
            column = jnp.sum(jnp.where(pick, s_ref[...], 0.0), axis=1, keepdims=True)
            below = lax.broadcasted_iota(jnp.int32, (n, 1), 0) > j
            ratio = jnp.where(below, column / pivot, 0.0)
            s_ref[...] = s_ref[...] - ratio * row
            w_ref[...] = w_ref[...] - ratio * w_ref[pl.ds(j, 1), :]
            return carry

        lax.fori_loop(0, n, eliminate, 0)
        pivots = jnp.sum(s_ref[...] * eye, axis=1, keepdims=True)
        w_ref[...] = w_ref[...] * lax.rsqrt(pivots)

    w_ref[...] = w_ref[...] * scale_row
    for stage in stages:
        stage.wait()


def inverse_factor(where, window, parts):
    n = parts[0].shape[-1]
    return pl.pallas_call(
        inverse_factor_kernel,
        out_shape=(jax.ShapeDtypeStruct((n, n), F32), pltpu.HBM(window.shape, F32)),
        in_specs=[SMEM, HBM] + [VMEM] * len(parts),
        out_specs=(VMEM, HBM),
        scratch_shapes=[pltpu.VMEM((n, n), F32), pltpu.SemaphoreType.DMA((STAGES,))],
        compiler_params=pltpu.CompilerParams(vmem_limit_bytes=20 * 2**20),
    )(where, window, *parts)


class Sizes:
    def __init__(self, trailing, panel_rows, panel_fill):
        self.cols, self.rows = lax.axis_size("col"), lax.axis_size("row")
        self.block = panel_rows.shape[1] // 2
        self.piece = panel_rows.shape[0]
        self.unit = math.gcd(self.piece, self.block)
        self.per_piece = self.piece // self.unit
        self.per_block = self.block // self.unit
        self.slab = self.piece * self.cols
        self.merge = self.per_block if 2 * self.piece % self.block == 0 else 1
        self.width = trailing.shape[1]
        self.tiles = self.cols * self.per_piece

        self.groups = self.cols // 2
        self.column_units = 2 * self.width // self.unit
        self.needed = sorted({s for g in range(self.groups) for s in self.shifts(g)})

    def pair_slab(self, group):
        return 2 * group * self.width // self.slab

    def pair_start(self, group):
        return (2 * group * self.width - self.pair_slab(group) * self.slab) // self.unit

    def shifts(self, group):
        start = self.pair_start(group) * self.unit
        first, last = start // (2 * self.piece), (start + 2 * self.width - 1) // (2 * self.piece)
        return [(g - group) % self.groups for g in range(first, last + 1)]


def unit_flag(sizes, fill_ref, piece_index, unit, panel):
    block = (piece_index * sizes.per_piece + unit) // sizes.per_block
    return fill_ref[block * 2 + panel] != 0


def pool_pieces(sizes, pool_row, pool_col):
    for core in range(2):
        for side in range(2):
            yield core, side, (pool_row * 2 + core) * sizes.cols + pool_col * 2 + side


def pair_flag(sizes, fill_ref, group, index):
    unit = sizes.pair_slab(group) * sizes.tiles + sizes.pair_start(group) + index // 2
    return fill_ref[unit // sizes.per_block * 2 + index % 2] != 0


def level_kernel(sizes, levels, fill_ref, out_ref):
    pool_most, column_most = jnp.int32(0), jnp.int32(0)
    for pool_row in range(sizes.rows // 2):
        for pool_col in range(sizes.groups):
            count = jnp.int32(0)
            for _, _, piece in pool_pieces(sizes, pool_row, pool_col):
                for u in range(sizes.per_piece):
                    for p in range(2):
                        count = count + unit_flag(sizes, fill_ref, piece, u, p).astype(jnp.int32)
            pool_most = jnp.maximum(pool_most, count)
    for group in range(sizes.groups):
        for side in range(2):
            count = jnp.int32(0)
            for i in range(sizes.column_units):
                flag = pair_flag(sizes, fill_ref, group, side * sizes.column_units + i)
                count = count + flag.astype(jnp.int32)
            column_most = jnp.maximum(column_most, count)
    level = jnp.int32(0)
    for cap, column_cap in levels[:-1]:
        fits = jnp.logical_and(pool_most <= cap, column_most <= column_cap)
        level = level + jnp.logical_not(fits).astype(jnp.int32)
    out_ref[0] = level


def level_of(sizes, levels, fill):
    return pl.pallas_call(
        functools.partial(level_kernel, sizes, levels),
        out_shape=jax.ShapeDtypeStruct((1,), jnp.int32),
        in_specs=[SMEM],
        out_specs=SMEM,
    )(fill)


def pack_kernel(sizes, cap, where_ref, fill_ref, panel_ref, core_ref, side_ref, out_ref, pool):
    c, r = where_ref[0], where_ref[1]
    side, core = c % 2, r % 2
    quarter = sizes.unit // 4
    own_at = pl.multiple_of((side * 2 + core) * quarter, quarter)
    for u in range(sizes.per_piece):
        pool[core, side, u] = panel_ref[u, pl.ds(own_at, quarter), :]
        pool[1 - core, side, u] = core_ref[u, side]
        pool[core, 1 - side, u] = side_ref[0, u]
        pool[1 - core, 1 - side, u] = side_ref[1, u]
    slot = jnp.int32(0)
    for core_at, side_at, piece in pool_pieces(sizes, r // 2, c // 2):
        for u in range(sizes.per_piece):
            for p in range(2):
                flag = unit_flag(sizes, fill_ref, piece, u, p)

                @pl.when(flag)
                def _(slot=slot, core_at=core_at, side_at=side_at, u=u, p=p):
                    out_ref[jnp.minimum(slot, cap - 1)] = pool[
                        core_at, side_at, u, :, p * sizes.block : (p + 1) * sizes.block
                    ]

                slot = slot + flag.astype(jnp.int32)


def pack(sizes, cap, where, fill, panel, from_core, from_side):
    quarter = sizes.unit // 4
    return pl.pallas_call(
        functools.partial(pack_kernel, sizes, cap),
        out_shape=jax.ShapeDtypeStruct((cap, quarter, sizes.block), F32),
        in_specs=[SMEM, SMEM, VMEM, VMEM, VMEM],
        out_specs=VMEM,
        scratch_shapes=[pltpu.VMEM((2, 2, sizes.per_piece, quarter, 2 * sizes.block), F32)],
        compiler_params=pltpu.CompilerParams(vmem_limit_bytes=16 * 2**20),
    )(where, fill, panel, from_core, from_side)


def pair_slots(sizes, fill_ref, group, slots):
    def step(i, slot):
        flag = pair_flag(sizes, fill_ref, group, i)
        slot = jnp.where(i == sizes.column_units, 0, slot)
        slots[i] = jnp.where(flag, slot, -1)
        return slot + flag.astype(jnp.int32)

    lax.fori_loop(0, 2 * sizes.column_units, step, jnp.int32(0))


def pack_column_kernel(sizes, cap, column_cap, where_ref, fill_ref, *refs):
    lists, (out_ref, slots) = refs[:-2], refs[-2:]
    own = where_ref[0] // 2
    slab, start = sizes.pair_slab(own), sizes.pair_start(own)
    pair_slots(sizes, fill_ref, own, slots)
    for shift, list_ref in zip(sizes.needed, lists):
        group = lax.rem(own + shift, sizes.groups)
        slot = jnp.int32(0)
        for core, side, piece in pool_pieces(sizes, slab // 2, group):
            for u in range(sizes.per_piece):
                for p in range(2):
                    flag = unit_flag(sizes, fill_ref, piece, u, p)
                    index = (((group * 2 + side) * sizes.per_piece + u) - start) * 2 + p
                    inside = jnp.logical_and(index >= 0, index < 2 * sizes.column_units)
                    wanted = jnp.logical_and(jnp.logical_and(flag, inside), slab % 2 == core)

                    @pl.when(wanted)
                    def _(slot=slot, index=index, list_ref=list_ref):
                        index = jnp.clip(index, 0, 2 * sizes.column_units - 1)
                        target = jnp.clip(slots[index], 0, column_cap - 1)
                        out_ref[index // sizes.column_units, target] = list_ref[jnp.minimum(slot, cap - 1)]

                    slot = slot + flag.astype(jnp.int32)


def pack_column(sizes, cap, column_cap, where, fill, lists):
    return pl.pallas_call(
        functools.partial(pack_column_kernel, sizes, cap, column_cap),
        out_shape=jax.ShapeDtypeStruct((2, column_cap, sizes.unit // 4, sizes.block), F32),
        in_specs=[SMEM, SMEM] + [VMEM] * len(lists),
        out_specs=VMEM,
        scratch_shapes=[pltpu.SMEM((2 * sizes.column_units,), jnp.int32)],
        compiler_params=pltpu.CompilerParams(vmem_limit_bytes=20 * 2**20),
    )(where, fill, *lists)


def own_factor_kernel(sizes, where_ref, fill_ref, w_ref, panel_ref, x_ref, slot_ref, masked, sem):
    c, r = where_ref[0], where_ref[1]
    own = r * sizes.cols + c
    for u in range(sizes.per_piece):
        for p in range(2):
            at = (pl.ds(u * sizes.unit, sizes.unit), pl.ds(p * sizes.block, sizes.block))
            masked[at] = jnp.where(unit_flag(sizes, fill_ref, own, u, p), panel_ref[at], 0.0)
    masked[...] = dot3(halves(masked[...]), halves(w_ref[...]), NT)
    copy_out = pltpu.make_async_copy(masked, x_ref, sem)
    copy_out.start()

    @pl.loop(0, sizes.groups)
    def _(shift):
        group = lax.rem(c // 2 + shift, sizes.groups)
        slot = jnp.int32(0)
        for core, side, piece in pool_pieces(sizes, r // 2, group):
            for u in range(sizes.per_piece):
                for p in range(2):
                    flag = unit_flag(sizes, fill_ref, piece, u, p)

                    @pl.when(core == r % 2)
                    def _(slot=slot, flag=flag, side=side, u=u, p=p):
                        at = ((shift * 2 + side) * sizes.per_piece + u) * 2 + p
                        slot_ref[at] = jnp.where(flag, slot, -1)

                    slot = slot + flag.astype(jnp.int32)

    copy_out.wait()


def own_factor(sizes, where, fill, w, panel):
    return pl.pallas_call(
        functools.partial(own_factor_kernel, sizes),
        out_shape=(
            pltpu.HBM(panel.shape, F32),
            jax.ShapeDtypeStruct((2 * sizes.tiles,), jnp.int32),
        ),
        in_specs=[SMEM, SMEM, VMEM, VMEM],
        out_specs=(HBM, SMEM),
        scratch_shapes=[pltpu.VMEM(panel.shape, F32), pltpu.SemaphoreType.DMA],
        compiler_params=pltpu.CompilerParams(vmem_limit_bytes=20 * 2**20),
    )(where, fill, w, panel)


def column_factor_kernel(sizes, where_ref, fill_ref, w_ref, *refs):
    lists, (out_ref, column, slots) = refs[:4], refs[4:]
    c, r = where_ref[0], where_ref[1]
    side, core = c % 2, r % 2
    quarter = sizes.unit // 4
    pair_slots(sizes, fill_ref, c // 2, slots)
    column[...] = jnp.zeros_like(column)

    @pl.loop(0, sizes.column_units // 2)
    def _(unit):
        for p in range(2):
            slot = slots[side * sizes.column_units + unit * 2 + p]

            @pl.when(slot >= 0)
            def _(slot=slot, p=p):
                for flip in range(4):
                    from_side = jnp.bitwise_xor(side, flip // 2)
                    from_core = jnp.bitwise_xor(core, flip % 2)
                    at = pl.multiple_of(unit * sizes.unit + (from_side * 2 + from_core) * quarter, quarter)
                    column[pl.ds(at, quarter), pl.ds(p * sizes.block, sizes.block)] = lists[flip][slot]

    w = halves(w_ref[...])
    solved = dot3(w, halves(column[...]), NT)
    out_ref[...] = dot3(w, halves(solved), TN)


def column_factor(sizes, where, fill, w, lists):
    n = w.shape[0]
    return pl.pallas_call(
        functools.partial(column_factor_kernel, sizes),
        out_shape=jax.ShapeDtypeStruct((n, sizes.width), F32),
        in_specs=[SMEM, SMEM, VMEM] + [VMEM] * 4,
        out_specs=VMEM,
        scratch_shapes=[pltpu.VMEM((sizes.width, n), F32), pltpu.SMEM((2 * sizes.column_units,), jnp.int32)],
        compiler_params=pltpu.CompilerParams(vmem_limit_bytes=20 * 2**20),
    )(where, fill, w, *lists)


def update_kernel(sizes, where_ref, slot_ref, column_ref, window_ref, *refs):
    groups, merge = sizes.groups, sizes.merge
    lists, (out_ref, tiles, data, right, in_sems, out_sems) = refs[: 4 * groups], refs[4 * groups :]
    c, r = where_ref[0], where_ref[1]
    side, core = c % 2, r % 2
    per_group = 2 * sizes.per_piece // merge
    rows = merge * sizes.unit
    quarter = sizes.unit // 4

    def rows_of(t):
        group = lax.rem(c // 2 + t // per_group, groups)
        return pl.ds(pl.multiple_of((group * per_group + t % per_group) * rows, rows), rows)

    def tile_in(t):
        return pltpu.make_async_copy(window_ref.at[rows_of(t)], tiles.at[t], in_sems.at[t])

    def tile_out(t):
        return pltpu.make_async_copy(tiles.at[t], out_ref.at[rows_of(t)], out_sems.at[t])

    def slot_of(t, p, part):
        return slot_ref[(t * merge + part) * 2 + p]

    def active(t):
        return jnp.logical_or(slot_of(t, 0, 0) >= 0, slot_of(t, 1, 0) >= 0)

    @pl.loop(0, per_group * groups)
    def _(t):
        pl.when(active(t))(tile_in(t).start)

    for p in range(2):
        high, low = halves(column_ref[p * sizes.block : (p + 1) * sizes.block, :])
        for i, part in enumerate((high, low, high)):
            right[p, i * sizes.block : (i + 1) * sizes.block, :] = part

    for group in range(groups):

        @pl.loop(group * per_group, (group + 1) * per_group)
        def _(t, group=group):
            @pl.when(active(t))
            def _():
                tile_in(t).wait()
                for p in range(2):

                    @pl.when(slot_of(t, p, 0) >= 0)
                    def _(p=p):
                        for part in range(merge):
                            slot = slot_of(t, p, part)
                            for flip in range(4):
                                from_side = jnp.bitwise_xor(side, flip // 2)
                                from_core = jnp.bitwise_xor(core, flip % 2)
                                at = pl.multiple_of((part * 4 + from_side * 2 + from_core) * quarter, quarter)
                                data[pl.ds(at, quarter), :] = lists[4 * group + flip][slot]
                        high, low = halves(data[...])
                        left = jnp.concatenate([high, high, low], axis=1)
                        tiles[t] = tiles[t] - dot(left, right[p], NN)

                tile_out(t).start()

    @pl.loop(0, per_group * groups)
    def _(t):
        pl.when(active(t))(tile_out(t).wait)


def update(sizes, where, slots, column, window, lists):
    rows = sizes.merge * sizes.unit
    tiles = sizes.slab // rows
    return pl.pallas_call(
        functools.partial(update_kernel, sizes),
        out_shape=pltpu.HBM(window.shape, F32),
        in_specs=[SMEM, SMEM, VMEM, HBM] + [VMEM] * len(lists),
        out_specs=HBM,
        input_output_aliases={3: 0},
        scratch_shapes=[
            pltpu.VMEM((tiles, rows, sizes.width), F32),
            pltpu.VMEM((rows, sizes.block), F32),
            pltpu.VMEM((2, 3 * sizes.block, sizes.width), BF16),
            pltpu.SemaphoreType.DMA((tiles,)),
            pltpu.SemaphoreType.DMA((tiles,)),
        ],
        compiler_params=pltpu.CompilerParams(vmem_limit_bytes=36 * 2**20),
    )(where, slots, column, window, *lists)


def swap(value, axis, step):
    size = lax.axis_size(axis)
    return lax.ppermute(value, axis, [(i, i ^ step) for i in range(size)])


def join(index, step, own, other):
    second = (index & step) != 0
    return jnp.where(second, jnp.concatenate([other, own], 0), jnp.concatenate([own, other], 0))


def after(value, *earlier):
    return lax.optimization_barrier((value, *earlier))[0]


def bring(sizes, value, shift):
    pairs = [(i, (i - 2 * shift) % sizes.cols) for i in range(sizes.cols)]
    return lax.ppermute(value, "col", pairs)


def spread_column(sizes, value, step):
    r, c = lax.axis_index("row"), lax.axis_index("col")
    pairs = []
    for at in range(sizes.cols):
        slab = sizes.pair_slab(at // 2)
        for row in range(sizes.rows):
            if (row // 2 ^ slab // 2) % step == 0:
                pairs.append((at * sizes.rows + row, at * sizes.rows + (row ^ step)))
    other = lax.ppermute(value, ("col", "row"), pairs)
    return jnp.where(((r ^ sizes.pair_slab(c // 2)) & step) != 0, other, value)


def per_device(trailing, panel_rows, pivot_block, panel_fill):
    sizes = Sizes(trailing, panel_rows, panel_fill)
    fill = panel_fill.reshape(-1)
    r, c = lax.axis_index("row"), lax.axis_index("col")
    where = jnp.stack([c, r]).astype(jnp.int32)
    side, core = c % 2, r % 2
    quarter = sizes.unit // 4
    split = min(4, pivot_block.shape[0] // 8)
    share = pivot_block.shape[0] // split
    most, column_most = 8 * sizes.per_piece, sizes.column_units
    levels = [(most // 3, column_most // 2), (most * 5 // 12, column_most * 3 // 4), (most, column_most)]

    units = panel_rows.reshape(sizes.per_piece, sizes.unit, -1)
    quarters = panel_rows.reshape(sizes.per_piece, 2, 2, quarter, -1)

    def at_core(which):
        return lax.dynamic_index_in_dim(quarters, which, 2, keepdims=False)

    pivot = lax.dynamic_slice_in_dim(pivot_block, r % split * share, share, 0)[None]
    pivot = join(c, 1, pivot, swap(pivot, "col", 1))
    from_core = swap(at_core(1 - core), "row", 1)
    from_core, pivot = lax.optimization_barrier((from_core, pivot))
    both = jnp.stack([at_core(core), from_core])
    from_side = swap(lax.dynamic_index_in_dim(both, 1 - side, 2, keepdims=False), "col", 1)
    step = 2
    while step < sizes.cols:
        pivot = join(c, step, pivot, swap(pivot, "col", step))
        step *= 2

    def run(cap, column_cap, trailing, panel_rows, fill, units, from_core, from_side, pivot):
        own = pack(sizes, cap, where, fill, units, from_core, from_side)
        lists = {0: own}
        first = [s for s in range(1, sizes.groups) if s in sizes.needed]
        later = [s for s in range(1, sizes.groups) if s not in sizes.needed]
        lists |= {s: bring(sizes, own, s) for s in first}
        sides = {0: swap(own, "col", 1)}
        parts = [pivot] + ([swap(pivot, "row", 2)] if split == 4 else [])
        parts = [part for value in parts for part in (value, swap(value, "row", 1))]
        near = first[0]
        lists[near], sides[0], *parts = lax.optimization_barrier((lists[near], sides[0], *parts))
        sides[near] = swap(lists[near], "col", 1)
        w, window = inverse_factor(where, trailing, parts)
        held = lax.optimization_barrier((w, sides[0], sides[near], *lists.values()))
        w, sides[0], sides[near] = held[:3]
        lists = dict(zip(lists, held[3:]))

        column = pack_column(sizes, cap, column_cap, where, fill, [lists[s] for s in sizes.needed])
        lists |= {s: bring(sizes, lists[0], s) for s in later}
        sides |= {s: swap(lists[s], "col", 1) for s in first[1:]}
        step = sizes.rows // 2
        while step > 1:
            column = spread_column(sizes, column, step)
            step //= 2
        panel_factor, slots = own_factor(sizes, where, fill, w, panel_rows)
        column, slots = lax.optimization_barrier((column, slots))
        across = swap(lax.dynamic_index_in_dim(column, 1 - side, 0, keepdims=False), "col", 1)
        column = lax.dynamic_index_in_dim(column, side, 0, keepdims=False)
        columns = [column, swap(column, "row", 1), across, swap(across, "row", 1)]
        for s in later:
            lists[s] = lax.optimization_barrier((lists[s], slots, *(sides[j] for j in first)))[0]
            sides[s] = swap(lists[s], "col", 1)
        column = column_factor(sizes, where, fill, w, columns)
        for s in later:
            sides[s], column = lax.optimization_barrier((sides[s], column))
        ordered = []
        for s in range(sizes.groups):
            value, other = lists[s], sides[s]
            ordered += [value, swap(value, "row", 1), other, swap(other, "row", 1)]
        return update(sizes, where, slots, column, window, ordered), panel_factor

    operands = (trailing, panel_rows, fill, units, from_core, from_side, pivot)
    branches = [functools.partial(run, *level) for level in levels]
    return lax.switch(level_of(sizes, levels, fill)[0], branches, *operands)


def solution(mesh):
    in_specs = (P("row", "col"), P(("row", "col"), None), P("col", None), P())
    out_specs = (P("row", "col"), P(("row", "col"), None))
    return jax.shard_map(
        per_device, mesh=mesh, in_specs=in_specs, out_specs=out_specs, check_vma=False
    )
```

```python
import functools
import math

import jax
import jax.numpy as jnp
from jax import lax
from jax.experimental import pallas as pl
from jax.experimental.pallas import tpu as pltpu
from jax.sharding import PartitionSpec as P

F32, BF16 = jnp.float32, jnp.bfloat16
VMEM = pl.BlockSpec(memory_space=pltpu.VMEM)
SMEM = pl.BlockSpec(memory_space=pltpu.SMEM)
HBM = pl.BlockSpec(memory_space=pltpu.HBM)
COARSE_STEPS = 2
FINE_STEPS = 16
RESIDUAL = 5e-4


def halves(value):
    high = value.astype(BF16)
    return high, (value - high.astype(F32)).astype(BF16)


def dot(a, b, dims):
    return lax.dot_general(a, b, (dims, ((), ())), preferred_element_type=F32)


NN, NT, TN = ((1,), (0,)), ((1,), (1,)), ((0,), (0,))


def dot3(a, b, dims):
    (ah, al), (bh, bl) = a, b
    return dot(ah, bh, dims) + (dot(ah, bl, dims) + dot(al, bh, dims))


def inverse_factor_kernel(where_ref, *refs):
    parts, (w_ref, s_ref) = refs[:-2], refs[-2:]
    n = w_ref.shape[0]
    pieces, share = parts[0].shape[0], parts[0].shape[1]
    own = where_ref[1] % len(parts)
    for flip, ref in enumerate(parts):
        at = jnp.bitwise_xor(own, flip) * share
        for i in range(pieces):
            s_ref[pl.ds(pl.multiple_of(i * len(parts) * share + at, share), share), :] = ref[i]
    rows = lax.broadcasted_iota(jnp.int32, (n, n), 0)
    cols = lax.broadcasted_iota(jnp.int32, (n, n), 1)
    eye = (rows == cols).astype(F32)
    take = jnp.where(rows > cols, 1.0, 0.5 * eye)
    a = s_ref[...]
    diag_row = jnp.sum(a * eye, axis=0, keepdims=True)
    diag_col = jnp.sum(a * eye, axis=1, keepdims=True)
    scale_row, scale_col = lax.rsqrt(diag_row), lax.rsqrt(diag_col)
    scaled = jnp.where(rows == cols, 1.0, a * scale_row * scale_col)
    s_ref[...] = scaled
    scaled_parts = halves(scaled)
    w = eye - take * (scaled - eye)
    for _ in range(COARSE_STEPS):
        wh = w.astype(BF16)
        t = dot(wh, scaled_parts[0], NN).astype(BF16)
        change = take * (dot(t, wh, NT) - eye)
        w = w - dot(change.astype(BF16), wh, NN)
    w_ref[...] = w

    def fine(state):
        step, _ = state
        w = w_ref[...]
        parts = halves(w)
        t = halves(dot3(parts, halves(s_ref[...]), NN))
        residual = dot3(t, parts, NT) - eye
        w_ref[...] = w - dot((take * residual).astype(BF16), parts[0], NN)
        return step + 1, jnp.sum(residual * residual)

    _, left = lax.while_loop(
        lambda state: jnp.logical_and(state[0] < FINE_STEPS, jnp.logical_not(state[1] < RESIDUAL**2)),
        fine,
        (jnp.int32(0), jnp.float32(1.0)),
    )
    done = left < RESIDUAL**2

    @pl.when(jnp.logical_not(done))
    def _():
        w_ref[...] = eye

        def eliminate(j, carry):
            row = s_ref[pl.ds(j, 1), :]
            pick = lax.broadcasted_iota(jnp.int32, (1, n), 1) == j
            pivot = jnp.sum(jnp.where(pick, row, 0.0), axis=1, keepdims=True)
            column = jnp.sum(jnp.where(pick, s_ref[...], 0.0), axis=1, keepdims=True)
            below = lax.broadcasted_iota(jnp.int32, (n, 1), 0) > j
            ratio = jnp.where(below, column / pivot, 0.0)
            s_ref[...] = s_ref[...] - ratio * row
            w_ref[...] = w_ref[...] - ratio * w_ref[pl.ds(j, 1), :]
            return carry

        lax.fori_loop(0, n, eliminate, 0)
        pivots = jnp.sum(s_ref[...] * eye, axis=1, keepdims=True)
        w_ref[...] = w_ref[...] * lax.rsqrt(pivots)

    w_ref[...] = w_ref[...] * scale_row


def inverse_factor(where, parts):
    n = parts[0].shape[-1]
    return pl.pallas_call(
        inverse_factor_kernel,
        out_shape=jax.ShapeDtypeStruct((n, n), F32),
        in_specs=[SMEM] + [VMEM] * len(parts),
        out_specs=VMEM,
        scratch_shapes=[pltpu.VMEM((n, n), F32)],
        compiler_params=pltpu.CompilerParams(vmem_limit_bytes=20 * 2**20),
    )(where, *parts)


class Sizes:
    def __init__(self, trailing, panel_rows, panel_fill):
        self.cols, self.rows = lax.axis_size("col"), lax.axis_size("row")
        self.block = panel_rows.shape[1] // 2
        self.piece = panel_rows.shape[0]
        self.unit = math.gcd(self.piece, self.block)
        self.per_piece = self.piece // self.unit
        self.per_block = self.block // self.unit
        self.slab = self.piece * self.cols
        self.merge = self.per_block if 2 * self.piece % self.block == 0 else 1
        self.width = trailing.shape[1]
        self.tiles = self.cols * self.per_piece

        self.groups = self.cols // 2
        self.column_units = 2 * self.width // self.unit
        self.needed = sorted({s for g in range(self.groups) for s in self.shifts(g)})

    def pair_slab(self, group):
        return 2 * group * self.width // self.slab

    def pair_start(self, group):
        return (2 * group * self.width - self.pair_slab(group) * self.slab) // self.unit

    def shifts(self, group):
        start = self.pair_start(group) * self.unit
        first, last = start // (2 * self.piece), (start + 2 * self.width - 1) // (2 * self.piece)
        return [(g - group) % self.groups for g in range(first, last + 1)]


def unit_flag(sizes, fill_ref, piece_index, unit, panel):
    block = (piece_index * sizes.per_piece + unit) // sizes.per_block
    return fill_ref[block * 2 + panel] != 0


def pool_pieces(sizes, pool_row, pool_col):
    for core in range(2):
        for side in range(2):
            yield core, side, (pool_row * 2 + core) * sizes.cols + pool_col * 2 + side


def pair_flag(sizes, fill_ref, group, index):
    unit = sizes.pair_slab(group) * sizes.tiles + sizes.pair_start(group) + index // 2
    return fill_ref[unit // sizes.per_block * 2 + index % 2] != 0


def level_kernel(sizes, levels, fill_ref, out_ref):
    pool_most, column_most = jnp.int32(0), jnp.int32(0)
    for pool_row in range(sizes.rows // 2):
        for pool_col in range(sizes.groups):
            count = jnp.int32(0)
            for _, _, piece in pool_pieces(sizes, pool_row, pool_col):
                for u in range(sizes.per_piece):
                    for p in range(2):
                        count = count + unit_flag(sizes, fill_ref, piece, u, p).astype(jnp.int32)
            pool_most = jnp.maximum(pool_most, count)
    for group in range(sizes.groups):
        for side in range(2):
            count = jnp.int32(0)
            for i in range(sizes.column_units):
                flag = pair_flag(sizes, fill_ref, group, side * sizes.column_units + i)
                count = count + flag.astype(jnp.int32)
            column_most = jnp.maximum(column_most, count)
    level = jnp.int32(0)
    for cap, column_cap in levels[:-1]:
        fits = jnp.logical_and(pool_most <= cap, column_most <= column_cap)
        level = level + jnp.logical_not(fits).astype(jnp.int32)
    out_ref[0] = level


def level_of(sizes, levels, fill):
    return pl.pallas_call(
        functools.partial(level_kernel, sizes, levels),
        out_shape=jax.ShapeDtypeStruct((1,), jnp.int32),
        in_specs=[SMEM],
        out_specs=SMEM,
    )(fill)


def pack_kernel(sizes, cap, where_ref, fill_ref, panel_ref, core_ref, side_ref, out_ref, pool):
    c, r = where_ref[0], where_ref[1]
    side, core = c % 2, r % 2
    quarter = sizes.unit // 4
    own_at = pl.multiple_of((side * 2 + core) * quarter, quarter)
    for u in range(sizes.per_piece):
        pool[core, side, u] = panel_ref[u, pl.ds(own_at, quarter), :]
        pool[1 - core, side, u] = core_ref[u, side]
        pool[core, 1 - side, u] = side_ref[0, u]
        pool[1 - core, 1 - side, u] = side_ref[1, u]
    slot = jnp.int32(0)
    for core_at, side_at, piece in pool_pieces(sizes, r // 2, c // 2):
        for u in range(sizes.per_piece):
            for p in range(2):
                flag = unit_flag(sizes, fill_ref, piece, u, p)

                @pl.when(flag)
                def _(slot=slot, core_at=core_at, side_at=side_at, u=u, p=p):
                    out_ref[jnp.minimum(slot, cap - 1)] = pool[
                        core_at, side_at, u, :, p * sizes.block : (p + 1) * sizes.block
                    ]

                slot = slot + flag.astype(jnp.int32)


def pack(sizes, cap, where, fill, panel, from_core, from_side):
    quarter = sizes.unit // 4
    return pl.pallas_call(
        functools.partial(pack_kernel, sizes, cap),
        out_shape=jax.ShapeDtypeStruct((cap, quarter, sizes.block), F32),
        in_specs=[SMEM, SMEM, VMEM, VMEM, VMEM],
        out_specs=VMEM,
        scratch_shapes=[pltpu.VMEM((2, 2, sizes.per_piece, quarter, 2 * sizes.block), F32)],
        compiler_params=pltpu.CompilerParams(vmem_limit_bytes=16 * 2**20),
    )(where, fill, panel, from_core, from_side)


def pair_slots(sizes, fill_ref, group, slots):
    def step(i, slot):
        flag = pair_flag(sizes, fill_ref, group, i)
        slot = jnp.where(i == sizes.column_units, 0, slot)
        slots[i] = jnp.where(flag, slot, -1)
        return slot + flag.astype(jnp.int32)

    lax.fori_loop(0, 2 * sizes.column_units, step, jnp.int32(0))


def pack_column_kernel(sizes, cap, column_cap, shifts, where_ref, fill_ref, *refs):
    lists, before, (out_ref, slots) = refs[: len(shifts)], refs[len(shifts) : -2], refs[-2:]
    own = where_ref[0] // 2
    slab, start = sizes.pair_slab(own), sizes.pair_start(own)
    pair_slots(sizes, fill_ref, own, slots)
    for ref in before:
        out_ref[...] = ref[...]
    for shift, list_ref in zip(shifts, lists):
        group = lax.rem(own + shift, sizes.groups)
        slot = jnp.int32(0)
        for core, side, piece in pool_pieces(sizes, slab // 2, group):
            for u in range(sizes.per_piece):
                for p in range(2):
                    flag = unit_flag(sizes, fill_ref, piece, u, p)
                    index = (((group * 2 + side) * sizes.per_piece + u) - start) * 2 + p
                    inside = jnp.logical_and(index >= 0, index < 2 * sizes.column_units)
                    wanted = jnp.logical_and(jnp.logical_and(flag, inside), slab % 2 == core)

                    @pl.when(wanted)
                    def _(slot=slot, index=index, list_ref=list_ref):
                        index = jnp.clip(index, 0, 2 * sizes.column_units - 1)
                        target = jnp.clip(slots[index], 0, column_cap - 1)
                        out_ref[index // sizes.column_units, target] = list_ref[jnp.minimum(slot, cap - 1)]

                    slot = slot + flag.astype(jnp.int32)


def pack_column(sizes, cap, column_cap, shifts, where, fill, lists, before=()):
    return pl.pallas_call(
        functools.partial(pack_column_kernel, sizes, cap, column_cap, shifts),
        out_shape=jax.ShapeDtypeStruct((2, column_cap, sizes.unit // 4, sizes.block), F32),
        in_specs=[SMEM, SMEM] + [VMEM] * (len(lists) + len(before)),
        out_specs=VMEM,
        scratch_shapes=[pltpu.SMEM((2 * sizes.column_units,), jnp.int32)],
        compiler_params=pltpu.CompilerParams(vmem_limit_bytes=20 * 2**20),
    )(where, fill, *lists, *before)


def own_factor_kernel(sizes, where_ref, fill_ref, w_ref, panel_ref, x_ref, slot_ref, masked, sem):
    c, r = where_ref[0], where_ref[1]
    own = r * sizes.cols + c
    for u in range(sizes.per_piece):
        for p in range(2):
            at = (pl.ds(u * sizes.unit, sizes.unit), pl.ds(p * sizes.block, sizes.block))
            masked[at] = jnp.where(unit_flag(sizes, fill_ref, own, u, p), panel_ref[at], 0.0)
    masked[...] = dot3(halves(masked[...]), halves(w_ref[...]), NT)
    copy_out = pltpu.make_async_copy(masked, x_ref, sem)
    copy_out.start()

    @pl.loop(0, sizes.groups)
    def _(shift):
        group = lax.rem(c // 2 + shift, sizes.groups)
        slot = jnp.int32(0)
        for core, side, piece in pool_pieces(sizes, r // 2, group):
            for u in range(sizes.per_piece):
                for p in range(2):
                    flag = unit_flag(sizes, fill_ref, piece, u, p)

                    @pl.when(core == r % 2)
                    def _(slot=slot, flag=flag, side=side, u=u, p=p):
                        at = ((shift * 2 + side) * sizes.per_piece + u) * 2 + p
                        slot_ref[at] = jnp.where(flag, slot, -1)

                    slot = slot + flag.astype(jnp.int32)

    copy_out.wait()


def own_factor(sizes, where, fill, w, panel):
    return pl.pallas_call(
        functools.partial(own_factor_kernel, sizes),
        out_shape=(
            pltpu.HBM(panel.shape, F32),
            jax.ShapeDtypeStruct((2 * sizes.tiles,), jnp.int32),
        ),
        in_specs=[SMEM, SMEM, VMEM, VMEM],
        out_specs=(HBM, SMEM),
        scratch_shapes=[pltpu.VMEM(panel.shape, F32), pltpu.SemaphoreType.DMA],
        compiler_params=pltpu.CompilerParams(vmem_limit_bytes=20 * 2**20),
    )(where, fill, w, panel)


def column_factor_kernel(sizes, where_ref, fill_ref, w_ref, *refs):
    lists, (out_ref, column, slots) = refs[:4], refs[4:]
    c, r = where_ref[0], where_ref[1]
    side, core = c % 2, r % 2
    quarter = sizes.unit // 4
    pair_slots(sizes, fill_ref, c // 2, slots)
    column[...] = jnp.zeros_like(column)

    @pl.loop(0, sizes.column_units // 2)
    def _(unit):
        for p in range(2):
            slot = slots[side * sizes.column_units + unit * 2 + p]

            @pl.when(slot >= 0)
            def _(slot=slot, p=p):
                for flip in range(4):
                    from_side = jnp.bitwise_xor(side, flip // 2)
                    from_core = jnp.bitwise_xor(core, flip % 2)
                    at = pl.multiple_of(unit * sizes.unit + (from_side * 2 + from_core) * quarter, quarter)
                    column[pl.ds(at, quarter), pl.ds(p * sizes.block, sizes.block)] = lists[flip][slot]

    w = halves(w_ref[...])
    solved = dot3(w, halves(column[...]), NT)
    out_ref[...] = dot3(w, halves(solved), TN)


def column_factor(sizes, where, fill, w, lists):
    n = w.shape[0]
    return pl.pallas_call(
        functools.partial(column_factor_kernel, sizes),
        out_shape=jax.ShapeDtypeStruct((n, sizes.width), F32),
        in_specs=[SMEM, SMEM, VMEM] + [VMEM] * 4,
        out_specs=VMEM,
        scratch_shapes=[pltpu.VMEM((sizes.width, n), F32), pltpu.SMEM((2 * sizes.column_units,), jnp.int32)],
        compiler_params=pltpu.CompilerParams(vmem_limit_bytes=20 * 2**20),
    )(where, fill, w, *lists)


def update_kernel(sizes, counts, where_ref, slot_ref, column_ref, window_ref, *refs):
    groups, merge = sizes.groups, sizes.merge
    refs, (out_ref, tiles, data, right, out_sems) = list(refs[:-5]), refs[-5:]
    lists = []
    for count in counts:
        own, other, *cores = [refs.pop(0) for _ in range(count)]
        cores = cores if count == 4 else [cores[0].at[0], cores[0].at[1]]
        lists += [own, cores[0], other, cores[1]]
    c, r = where_ref[0], where_ref[1]
    side, core = c % 2, r % 2
    per_group = 2 * sizes.per_piece // merge
    rows = merge * sizes.unit
    quarter = sizes.unit // 4

    def rows_of(t):
        group = lax.rem(c // 2 + t // per_group, groups)
        return pl.ds(pl.multiple_of((group * per_group + t % per_group) * rows, rows), rows)

    def tile_out(t, source):
        return pltpu.make_async_copy(source, out_ref.at[rows_of(t)], out_sems.at[t])

    def slot_of(t, p, part):
        return slot_ref[(t * merge + part) * 2 + p]

    def active(t):
        return jnp.logical_or(slot_of(t, 0, 0) >= 0, slot_of(t, 1, 0) >= 0)

    @pl.loop(0, per_group * groups)
    def _(t):
        pl.when(jnp.logical_not(active(t)))(tile_out(t, window_ref.at[rows_of(t)]).start)

    for p in range(2):
        high, low = halves(column_ref[p * sizes.block : (p + 1) * sizes.block, :])
        for i, part in enumerate((high, low, high)):
            right[p, i * sizes.block : (i + 1) * sizes.block, :] = part

    for group in range(groups):

        @pl.loop(group * per_group, (group + 1) * per_group)
        def _(t, group=group):
            @pl.when(active(t))
            def _():
                tiles[t] = window_ref[rows_of(t), :]
                for p in range(2):

                    @pl.when(slot_of(t, p, 0) >= 0)
                    def _(p=p):
                        for part in range(merge):
                            slot = slot_of(t, p, part)
                            for flip in range(4):
                                from_side = jnp.bitwise_xor(side, flip // 2)
                                from_core = jnp.bitwise_xor(core, flip % 2)
                                at = pl.multiple_of((part * 4 + from_side * 2 + from_core) * quarter, quarter)
                                data[pl.ds(at, quarter), :] = lists[4 * group + flip][slot]
                        high, low = halves(data[...])
                        left = jnp.concatenate([high, high, low], axis=1)
                        tiles[t] = tiles[t] - dot(left, right[p], NN)

                tile_out(t, tiles.at[t]).start()

    @pl.loop(0, per_group * groups)
    def _(t):
        tile_out(t, tiles.at[t]).wait()


def update(sizes, where, slots, column, window, lists):
    rows = sizes.merge * sizes.unit
    tiles = sizes.slab // rows
    return pl.pallas_call(
        functools.partial(update_kernel, sizes, [len(group) for group in lists]),
        out_shape=pltpu.HBM(window.shape, F32),
        in_specs=[SMEM, SMEM, VMEM, VMEM] + [VMEM] * sum(len(group) for group in lists),
        out_specs=HBM,
        scratch_shapes=[
            pltpu.VMEM((tiles, rows, sizes.width), F32),
            pltpu.VMEM((rows, sizes.block), F32),
            pltpu.VMEM((2, 3 * sizes.block, sizes.width), BF16),
            pltpu.SemaphoreType.DMA((tiles,)),
        ],
        compiler_params=pltpu.CompilerParams(vmem_limit_bytes=36 * 2**20),
    )(where, slots, column, window, *(value for group in lists for value in group))


def swap(value, axis, step):
    size = lax.axis_size(axis)
    return lax.ppermute(value, axis, [(i, i ^ step) for i in range(size)])


def join(index, step, own, other):
    second = (index & step) != 0
    return jnp.where(second, jnp.concatenate([other, own], 0), jnp.concatenate([own, other], 0))


def after(value, *earlier):
    return lax.optimization_barrier((value, *earlier))[0]


def bring(sizes, value, shift):
    pairs = [(i, (i - 2 * shift) % sizes.cols) for i in range(sizes.cols)]
    return lax.ppermute(value, "col", pairs)


def spread_column(sizes, value, step):
    r, c = lax.axis_index("row"), lax.axis_index("col")
    pairs = []
    for at in range(sizes.cols):
        slab = sizes.pair_slab(at // 2)
        for row in range(sizes.rows):
            if (row // 2 ^ slab // 2) % step == 0:
                pairs.append((at * sizes.rows + row, at * sizes.rows + (row ^ step)))
    other = lax.ppermute(value, ("col", "row"), pairs)
    return jnp.where(((r ^ sizes.pair_slab(c // 2)) & step) != 0, other, value)


def per_device(trailing, panel_rows, pivot_block, panel_fill):
    sizes = Sizes(trailing, panel_rows, panel_fill)
    fill = panel_fill.reshape(-1)
    r, c = lax.axis_index("row"), lax.axis_index("col")
    where = jnp.stack([c, r]).astype(jnp.int32)
    side, core = c % 2, r % 2
    quarter = sizes.unit // 4
    split = min(4, pivot_block.shape[0] // 8)
    share = pivot_block.shape[0] // split
    most, column_most = 8 * sizes.per_piece, sizes.column_units
    levels = [(most * 5 // 12, column_most * 3 // 4), (most, column_most)]

    units = panel_rows.reshape(sizes.per_piece, sizes.unit, -1)
    quarters = panel_rows.reshape(sizes.per_piece, 2, 2, quarter, -1)

    def at_core(which):
        return lax.dynamic_index_in_dim(quarters, which, 2, keepdims=False)

    pivot = lax.dynamic_slice_in_dim(pivot_block, r % split * share, share, 0)[None]
    pivot = join(c, 1, pivot, swap(pivot, "col", 1))
    from_core = swap(at_core(1 - core), "row", 1)
    from_core, pivot = lax.optimization_barrier((from_core, pivot))
    both = jnp.stack([at_core(core), from_core])
    from_side = swap(lax.dynamic_index_in_dim(both, 1 - side, 2, keepdims=False), "col", 1)
    step = 2
    while step < sizes.cols:
        pivot = join(c, step, pivot, swap(pivot, "col", step))
        step *= 2

    def run(cap, column_cap, trailing, panel_rows, fill, units, from_core, from_side, pivot):
        own = pack(sizes, cap, where, fill, units, from_core, from_side)
        lists = {0: own}
        first = [s for s in range(1, sizes.groups) if s in sizes.needed]
        later = [s for s in range(1, sizes.groups) if s not in sizes.needed]
        lists |= {s: bring(sizes, own, s) for s in first}
        sides = {0: swap(own, "col", 1)}
        parts = [pivot] + ([swap(pivot, "row", 2)] if split == 4 else [])
        parts = [part for value in parts for part in (value, swap(value, "row", 1))]
        near = first[0]
        lists[near], sides[0], *parts = lax.optimization_barrier((lists[near], sides[0], *parts))
        sides[near] = swap(lists[near], "col", 1)
        w = inverse_factor(where, parts)
        soon, rest = [0, near], [s for s in sizes.needed if s not in (0, near)]
        column = pack_column(sizes, cap, column_cap, soon, where, fill, [lists[s] for s in soon])
        held = lax.optimization_barrier((w, column, sides[0], sides[near], *lists.values()))
        w, column, sides[0], sides[near] = held[:4]
        lists = dict(zip(lists, held[4:]))

        column = pack_column(sizes, cap, column_cap, rest, where, fill, [lists[s] for s in rest], [column])
        lists |= {s: bring(sizes, lists[0], s) for s in later}
        sides |= {s: swap(lists[s], "col", 1) for s in first[1:]}
        step = sizes.rows // 2
        while step > 1:
            column = spread_column(sizes, column, step)
            step //= 2
        panel_factor, slots = own_factor(sizes, where, fill, w, panel_rows)
        column, slots = lax.optimization_barrier((column, slots))
        across = swap(lax.dynamic_index_in_dim(column, 1 - side, 0, keepdims=False), "col", 1)
        column = lax.dynamic_index_in_dim(column, side, 0, keepdims=False)
        columns = [column, swap(column, "row", 1), across, swap(across, "row", 1)]
        for s in later:
            lists[s] = lax.optimization_barrier((lists[s], slots, *(sides[j] for j in first)))[0]
            sides[s] = swap(lists[s], "col", 1)
        column = column_factor(sizes, where, fill, w, columns)
        for s in later:
            sides[s], column = lax.optimization_barrier((sides[s], column))
        ordered = []
        for s in range(sizes.groups):
            value, other = lists[s], sides[s]
            if s in later:
                ordered.append((value, other, swap(value, "row", 1), swap(other, "row", 1)))
            else:
                ordered.append((value, other, swap(jnp.stack([value, other]), "row", 1)))
        return update(sizes, where, slots, column, trailing, ordered), panel_factor

    operands = (trailing, panel_rows, fill, units, from_core, from_side, pivot)
    branches = [functools.partial(run, *level) for level in levels]
    return lax.cond(level_of(sizes, levels, fill)[0] == 0, *branches, *operands)


def solution(mesh):
    in_specs = (P("row", "col"), P(("row", "col"), None), P("col", None), P())
    out_specs = (P("row", "col"), P(("row", "col"), None))
    return jax.shard_map(
        per_device, mesh=mesh, in_specs=in_specs, out_specs=out_specs, check_vma=False
    )
```

```python
import functools
import math

import jax
import jax.numpy as jnp
from jax import lax
from jax.experimental import pallas as pl
from jax.experimental.pallas import tpu as pltpu
from jax.sharding import PartitionSpec as P

F32, BF16 = jnp.float32, jnp.bfloat16
VMEM = pl.BlockSpec(memory_space=pltpu.VMEM)
SMEM = pl.BlockSpec(memory_space=pltpu.SMEM)
HBM = pl.BlockSpec(memory_space=pltpu.HBM)
COARSE_STEPS = 2
FINE_STEPS = 16
RESIDUAL = 5e-4
STAGES = 8


def halves(value):
    high = value.astype(BF16)
    return high, (value - high.astype(F32)).astype(BF16)


def dot(a, b, dims):
    return lax.dot_general(a, b, (dims, ((), ())), preferred_element_type=F32)


NN, NT, TN = ((1,), (0,)), ((1,), (1,)), ((0,), (0,))


def dot3(a, b, dims):
    (ah, al), (bh, bl) = a, b
    return dot(ah, bh, dims) + (dot(ah, bl, dims) + dot(al, bh, dims))


def inverse_factor_kernel(where_ref, *refs):
    parts, (w_ref, s_ref) = refs[:-2], refs[-2:]
    n = w_ref.shape[0]
    pieces, share = parts[0].shape[0], parts[0].shape[1]
    own = where_ref[1] % len(parts)
    for flip, ref in enumerate(parts):
        at = jnp.bitwise_xor(own, flip) * share
        for i in range(pieces):
            s_ref[pl.ds(pl.multiple_of(i * len(parts) * share + at, share), share), :] = ref[i]
    rows = lax.broadcasted_iota(jnp.int32, (n, n), 0)
    cols = lax.broadcasted_iota(jnp.int32, (n, n), 1)
    eye = (rows == cols).astype(F32)
    take = jnp.where(rows > cols, 1.0, 0.5 * eye)
    a = s_ref[...]
    diag_row = jnp.sum(a * eye, axis=0, keepdims=True)
    diag_col = jnp.sum(a * eye, axis=1, keepdims=True)
    scale_row, scale_col = lax.rsqrt(diag_row), lax.rsqrt(diag_col)
    scaled = jnp.where(rows == cols, 1.0, a * scale_row * scale_col)
    s_ref[...] = scaled
    scaled_parts = halves(scaled)
    w = eye - take * (scaled - eye)
    for _ in range(COARSE_STEPS):
        wh = w.astype(BF16)
        t = dot(wh, scaled_parts[0], NN).astype(BF16)
        change = take * (dot(t, wh, NT) - eye)
        w = w - dot(change.astype(BF16), wh, NN)
    w_ref[...] = w

    def fine(state):
        step, _ = state
        w = w_ref[...]
        parts = halves(w)
        t = halves(dot3(parts, halves(s_ref[...]), NN))
        residual = dot3(t, parts, NT) - eye
        w_ref[...] = w - dot((take * residual).astype(BF16), parts[0], NN)
        return step + 1, jnp.sum(residual * residual)

    _, left = lax.while_loop(
        lambda state: jnp.logical_and(state[0] < FINE_STEPS, jnp.logical_not(state[1] < RESIDUAL**2)),
        fine,
        (jnp.int32(0), jnp.float32(1.0)),
    )
    done = left < RESIDUAL**2

    @pl.when(jnp.logical_not(done))
    def _():
        w_ref[...] = eye

        def eliminate(j, carry):
            row = s_ref[pl.ds(j, 1), :]
            pick = lax.broadcasted_iota(jnp.int32, (1, n), 1) == j
            pivot = jnp.sum(jnp.where(pick, row, 0.0), axis=1, keepdims=True)
            column = jnp.sum(jnp.where(pick, s_ref[...], 0.0), axis=1, keepdims=True)
            below = lax.broadcasted_iota(jnp.int32, (n, 1), 0) > j
            ratio = jnp.where(below, column / pivot, 0.0)
            s_ref[...] = s_ref[...] - ratio * row
            w_ref[...] = w_ref[...] - ratio * w_ref[pl.ds(j, 1), :]
            return carry

        lax.fori_loop(0, n, eliminate, 0)
        pivots = jnp.sum(s_ref[...] * eye, axis=1, keepdims=True)
        w_ref[...] = w_ref[...] * lax.rsqrt(pivots)

    w_ref[...] = w_ref[...] * scale_row


def inverse_factor(where, parts):
    n = parts[0].shape[-1]
    return pl.pallas_call(
        inverse_factor_kernel,
        out_shape=jax.ShapeDtypeStruct((n, n), F32),
        in_specs=[SMEM] + [VMEM] * len(parts),
        out_specs=VMEM,
        scratch_shapes=[pltpu.VMEM((n, n), F32)],
        compiler_params=pltpu.CompilerParams(vmem_limit_bytes=20 * 2**20),
    )(where, *parts)


class Sizes:
    def __init__(self, trailing, panel_rows, panel_fill):
        self.cols, self.rows = lax.axis_size("col"), lax.axis_size("row")
        self.block = panel_rows.shape[1] // 2
        self.piece = panel_rows.shape[0]
        self.unit = math.gcd(self.piece, self.block)
        self.per_piece = self.piece // self.unit
        self.per_block = self.block // self.unit
        self.slab = self.piece * self.cols
        self.merge = self.per_block if 2 * self.piece % self.block == 0 else 1
        self.width = trailing.shape[1]
        self.tiles = self.cols * self.per_piece

        self.groups = self.cols // 2
        self.column_units = 2 * self.width // self.unit
        self.needed = sorted({s for g in range(self.groups) for s in self.shifts(g)})

    def pair_slab(self, group):
        return 2 * group * self.width // self.slab

    def pair_start(self, group):
        return (2 * group * self.width - self.pair_slab(group) * self.slab) // self.unit

    def shifts(self, group):
        start = self.pair_start(group) * self.unit
        first, last = start // (2 * self.piece), (start + 2 * self.width - 1) // (2 * self.piece)
        return [(g - group) % self.groups for g in range(first, last + 1)]


def unit_flag(sizes, fill_ref, piece_index, unit, panel):
    block = (piece_index * sizes.per_piece + unit) // sizes.per_block
    return fill_ref[block * 2 + panel] != 0


def pool_pieces(sizes, pool_row, pool_col):
    for core in range(2):
        for side in range(2):
            yield core, side, (pool_row * 2 + core) * sizes.cols + pool_col * 2 + side


def pair_flag(sizes, fill_ref, group, index):
    unit = sizes.pair_slab(group) * sizes.tiles + sizes.pair_start(group) + index // 2
    return fill_ref[unit // sizes.per_block * 2 + index % 2] != 0


def level_kernel(sizes, levels, fill_ref, out_ref):
    pool_most, column_most = jnp.int32(0), jnp.int32(0)
    for pool_row in range(sizes.rows // 2):
        for pool_col in range(sizes.groups):
            count = jnp.int32(0)
            for _, _, piece in pool_pieces(sizes, pool_row, pool_col):
                for u in range(sizes.per_piece):
                    for p in range(2):
                        count = count + unit_flag(sizes, fill_ref, piece, u, p).astype(jnp.int32)
            pool_most = jnp.maximum(pool_most, count)
    for group in range(sizes.groups):
        for side in range(2):
            count = jnp.int32(0)
            for i in range(sizes.column_units):
                flag = pair_flag(sizes, fill_ref, group, side * sizes.column_units + i)
                count = count + flag.astype(jnp.int32)
            column_most = jnp.maximum(column_most, count)
    level = jnp.int32(0)
    for cap, column_cap in levels[:-1]:
        fits = jnp.logical_and(pool_most <= cap, column_most <= column_cap)
        level = level + jnp.logical_not(fits).astype(jnp.int32)
    out_ref[0] = level


def level_of(sizes, levels, fill):
    return pl.pallas_call(
        functools.partial(level_kernel, sizes, levels),
        out_shape=jax.ShapeDtypeStruct((1,), jnp.int32),
        in_specs=[SMEM],
        out_specs=SMEM,
    )(fill)


def pack_kernel(sizes, cap, where_ref, fill_ref, panel_ref, core_ref, side_ref, out_ref, pool):
    c, r = where_ref[0], where_ref[1]
    side, core = c % 2, r % 2
    quarter = sizes.unit // 4
    own_at = pl.multiple_of((side * 2 + core) * quarter, quarter)
    for u in range(sizes.per_piece):
        pool[core, side, u] = panel_ref[u, pl.ds(own_at, quarter), :]
        pool[1 - core, side, u] = core_ref[u, side]
        pool[core, 1 - side, u] = side_ref[0, u]
        pool[1 - core, 1 - side, u] = side_ref[1, u]
    slot = jnp.int32(0)
    for core_at, side_at, piece in pool_pieces(sizes, r // 2, c // 2):
        for u in range(sizes.per_piece):
            for p in range(2):
                flag = unit_flag(sizes, fill_ref, piece, u, p)

                @pl.when(flag)
                def _(slot=slot, core_at=core_at, side_at=side_at, u=u, p=p):
                    out_ref[jnp.minimum(slot, cap - 1)] = pool[
                        core_at, side_at, u, :, p * sizes.block : (p + 1) * sizes.block
                    ]

                slot = slot + flag.astype(jnp.int32)


def pack(sizes, cap, where, fill, panel, from_core, from_side):
    quarter = sizes.unit // 4
    return pl.pallas_call(
        functools.partial(pack_kernel, sizes, cap),
        out_shape=jax.ShapeDtypeStruct((cap, quarter, sizes.block), F32),
        in_specs=[SMEM, SMEM, VMEM, VMEM, VMEM],
        out_specs=VMEM,
        scratch_shapes=[pltpu.VMEM((2, 2, sizes.per_piece, quarter, 2 * sizes.block), F32)],
        compiler_params=pltpu.CompilerParams(vmem_limit_bytes=16 * 2**20),
    )(where, fill, panel, from_core, from_side)


def pair_slots(sizes, fill_ref, group, slots):
    def step(i, slot):
        flag = pair_flag(sizes, fill_ref, group, i)
        slot = jnp.where(i == sizes.column_units, 0, slot)
        slots[i] = jnp.where(flag, slot, -1)
        return slot + flag.astype(jnp.int32)

    lax.fori_loop(0, 2 * sizes.column_units, step, jnp.int32(0))


def pack_column_kernel(sizes, cap, column_cap, shifts, where_ref, fill_ref, *refs):
    lists, before, (out_ref, slots) = refs[: len(shifts)], refs[len(shifts) : -2], refs[-2:]
    own = where_ref[0] // 2
    slab, start = sizes.pair_slab(own), sizes.pair_start(own)
    pair_slots(sizes, fill_ref, own, slots)
    for ref in before:
        out_ref[...] = ref[...]
    for shift, list_ref in zip(shifts, lists):
        group = lax.rem(own + shift, sizes.groups)
        slot = jnp.int32(0)
        for core, side, piece in pool_pieces(sizes, slab // 2, group):
            for u in range(sizes.per_piece):
                for p in range(2):
                    flag = unit_flag(sizes, fill_ref, piece, u, p)
                    index = (((group * 2 + side) * sizes.per_piece + u) - start) * 2 + p
                    inside = jnp.logical_and(index >= 0, index < 2 * sizes.column_units)
                    wanted = jnp.logical_and(jnp.logical_and(flag, inside), slab % 2 == core)

                    @pl.when(wanted)
                    def _(slot=slot, index=index, list_ref=list_ref):
                        index = jnp.clip(index, 0, 2 * sizes.column_units - 1)
                        target = jnp.clip(slots[index], 0, column_cap - 1)
                        out_ref[index // sizes.column_units, target] = list_ref[jnp.minimum(slot, cap - 1)]

                    slot = slot + flag.astype(jnp.int32)


def pack_column(sizes, cap, column_cap, shifts, where, fill, lists, before=()):
    return pl.pallas_call(
        functools.partial(pack_column_kernel, sizes, cap, column_cap, shifts),
        out_shape=jax.ShapeDtypeStruct((2, column_cap, sizes.unit // 4, sizes.block), F32),
        in_specs=[SMEM, SMEM] + [VMEM] * (len(lists) + len(before)),
        out_specs=VMEM,
        scratch_shapes=[pltpu.SMEM((2 * sizes.column_units,), jnp.int32)],
        compiler_params=pltpu.CompilerParams(vmem_limit_bytes=20 * 2**20),
    )(where, fill, *lists, *before)


def own_factor_kernel(sizes, where_ref, fill_ref, w_ref, panel_ref, window_ref, x_ref, slot_ref, near_ref, masked, sem, sems):
    c, r = where_ref[0], where_ref[1]
    rows = window_ref.shape[0] // STAGES
    stages = []
    for i in range(STAGES):
        at = pl.ds(i * rows, rows)
        stages.append(pltpu.make_async_copy(window_ref.at[at], near_ref.at[at], sems.at[i]))
        stages[i].start()
    own = r * sizes.cols + c
    for u in range(sizes.per_piece):
        for p in range(2):
            at = (pl.ds(u * sizes.unit, sizes.unit), pl.ds(p * sizes.block, sizes.block))
            masked[at] = jnp.where(unit_flag(sizes, fill_ref, own, u, p), panel_ref[at], 0.0)
    masked[...] = dot3(halves(masked[...]), halves(w_ref[...]), NT)
    copy_out = pltpu.make_async_copy(masked, x_ref, sem)
    copy_out.start()

    @pl.loop(0, sizes.groups)
    def _(shift):
        group = lax.rem(c // 2 + shift, sizes.groups)
        slot = jnp.int32(0)
        for core, side, piece in pool_pieces(sizes, r // 2, group):
            for u in range(sizes.per_piece):
                for p in range(2):
                    flag = unit_flag(sizes, fill_ref, piece, u, p)

                    @pl.when(core == r % 2)
                    def _(slot=slot, flag=flag, side=side, u=u, p=p):
                        at = ((shift * 2 + side) * sizes.per_piece + u) * 2 + p
                        slot_ref[at] = jnp.where(flag, slot, -1)

                    slot = slot + flag.astype(jnp.int32)

    copy_out.wait()
    for stage in stages:
        stage.wait()


def own_factor(sizes, where, fill, w, panel, window):
    return pl.pallas_call(
        functools.partial(own_factor_kernel, sizes),
        out_shape=(
            pltpu.HBM(panel.shape, F32),
            jax.ShapeDtypeStruct((2 * sizes.tiles,), jnp.int32),
            pltpu.VMEM(window.shape, F32),
        ),
        in_specs=[SMEM, SMEM, VMEM, VMEM, HBM],
        out_specs=(HBM, SMEM, VMEM),
        scratch_shapes=[
            pltpu.VMEM(panel.shape, F32),
            pltpu.SemaphoreType.DMA,
            pltpu.SemaphoreType.DMA((STAGES,)),
        ],
        compiler_params=pltpu.CompilerParams(vmem_limit_bytes=20 * 2**20),
    )(where, fill, w, panel, window)


def column_factor_kernel(sizes, where_ref, fill_ref, w_ref, *refs):
    lists, (out_ref, column, slots) = refs[:4], refs[4:]
    c, r = where_ref[0], where_ref[1]
    side, core = c % 2, r % 2
    quarter = sizes.unit // 4
    pair_slots(sizes, fill_ref, c // 2, slots)
    column[...] = jnp.zeros_like(column)

    @pl.loop(0, sizes.column_units // 2)
    def _(unit):
        for p in range(2):
            slot = slots[side * sizes.column_units + unit * 2 + p]

            @pl.when(slot >= 0)
            def _(slot=slot, p=p):
                for flip in range(4):
                    from_side = jnp.bitwise_xor(side, flip // 2)
                    from_core = jnp.bitwise_xor(core, flip % 2)
                    at = pl.multiple_of(unit * sizes.unit + (from_side * 2 + from_core) * quarter, quarter)
                    column[pl.ds(at, quarter), pl.ds(p * sizes.block, sizes.block)] = lists[flip][slot]

    w = halves(w_ref[...])
    solved = dot3(w, halves(column[...]), NT)
    out_ref[...] = dot3(w, halves(solved), TN)


def column_factor(sizes, where, fill, w, lists):
    n = w.shape[0]
    return pl.pallas_call(
        functools.partial(column_factor_kernel, sizes),
        out_shape=jax.ShapeDtypeStruct((n, sizes.width), F32),
        in_specs=[SMEM, SMEM, VMEM] + [VMEM] * 4,
        out_specs=VMEM,
        scratch_shapes=[pltpu.VMEM((sizes.width, n), F32), pltpu.SMEM((2 * sizes.column_units,), jnp.int32)],
        compiler_params=pltpu.CompilerParams(vmem_limit_bytes=20 * 2**20),
    )(where, fill, w, *lists)


def update_kernel(sizes, counts, where_ref, slot_ref, column_ref, window_ref, *refs):
    groups, merge = sizes.groups, sizes.merge
    refs, (out_ref, tiles, data, right, out_sems) = list(refs[:-5]), refs[-5:]
    lists = []
    for count in counts:
        own, other, *cores = [refs.pop(0) for _ in range(count)]
        cores = cores if count == 4 else [cores[0].at[0], cores[0].at[1]]
        lists += [own, cores[0], other, cores[1]]
    c, r = where_ref[0], where_ref[1]
    side, core = c % 2, r % 2
    per_group = 2 * sizes.per_piece // merge
    rows = merge * sizes.unit
    quarter = sizes.unit // 4

    def rows_of(t):
        group = lax.rem(c // 2 + t // per_group, groups)
        return pl.ds(pl.multiple_of((group * per_group + t % per_group) * rows, rows), rows)

    def tile_out(t, source):
        return pltpu.make_async_copy(source, out_ref.at[rows_of(t)], out_sems.at[t])

    def slot_of(t, p, part):
        return slot_ref[(t * merge + part) * 2 + p]

    def active(t):
        return jnp.logical_or(slot_of(t, 0, 0) >= 0, slot_of(t, 1, 0) >= 0)

    @pl.loop(0, per_group * groups)
    def _(t):
        pl.when(jnp.logical_not(active(t)))(tile_out(t, window_ref.at[rows_of(t)]).start)

    for p in range(2):
        high, low = halves(column_ref[p * sizes.block : (p + 1) * sizes.block, :])
        for i, part in enumerate((high, low, high)):
            right[p, i * sizes.block : (i + 1) * sizes.block, :] = part

    for group in range(groups):

        @pl.loop(group * per_group, (group + 1) * per_group)
        def _(t, group=group):
            @pl.when(active(t))
            def _():
                tiles[t] = window_ref[rows_of(t), :]
                for p in range(2):

                    @pl.when(slot_of(t, p, 0) >= 0)
                    def _(p=p):
                        for part in range(merge):
                            slot = slot_of(t, p, part)
                            for flip in range(4):
                                from_side = jnp.bitwise_xor(side, flip // 2)
                                from_core = jnp.bitwise_xor(core, flip % 2)
                                at = pl.multiple_of((part * 4 + from_side * 2 + from_core) * quarter, quarter)
                                data[pl.ds(at, quarter), :] = lists[4 * group + flip][slot]
                        high, low = halves(data[...])
                        left = jnp.concatenate([high, high, low], axis=1)
                        tiles[t] = tiles[t] - dot(left, right[p], NN)

                tile_out(t, tiles.at[t]).start()

    @pl.loop(0, per_group * groups)
    def _(t):
        tile_out(t, tiles.at[t]).wait()


def update(sizes, where, slots, column, window, lists):
    rows = sizes.merge * sizes.unit
    tiles = sizes.slab // rows
    list_bytes = 4 * sum(value.size for group in lists for value in group)
    return pl.pallas_call(
        functools.partial(update_kernel, sizes, [len(group) for group in lists]),
        out_shape=pltpu.HBM(window.shape, F32),
        in_specs=[SMEM, SMEM, VMEM, VMEM] + [VMEM] * sum(len(group) for group in lists),
        out_specs=HBM,
        scratch_shapes=[
            pltpu.VMEM((tiles, rows, sizes.width), F32),
            pltpu.VMEM((rows, sizes.block), F32),
            pltpu.VMEM((2, 3 * sizes.block, sizes.width), BF16),
            pltpu.SemaphoreType.DMA((tiles,)),
        ],
        compiler_params=pltpu.CompilerParams(vmem_limit_bytes=14 * 2**20 + list_bytes),
    )(where, slots, column, window, *(value for group in lists for value in group))


def swap(value, axis, step):
    size = lax.axis_size(axis)
    return lax.ppermute(value, axis, [(i, i ^ step) for i in range(size)])


def join(index, step, own, other):
    second = (index & step) != 0
    return jnp.where(second, jnp.concatenate([other, own], 0), jnp.concatenate([own, other], 0))


def after(value, *earlier):
    return lax.optimization_barrier((value, *earlier))[0]


def bring(sizes, value, shift):
    pairs = [(i, (i - 2 * shift) % sizes.cols) for i in range(sizes.cols)]
    return lax.ppermute(value, "col", pairs)


def spread_column(sizes, value, step):
    r, c = lax.axis_index("row"), lax.axis_index("col")
    pairs = []
    for at in range(sizes.cols):
        slab = sizes.pair_slab(at // 2)
        for row in range(sizes.rows):
            if (row // 2 ^ slab // 2) % step == 0:
                pairs.append((at * sizes.rows + row, at * sizes.rows + (row ^ step)))
    other = lax.ppermute(value, ("col", "row"), pairs)
    return jnp.where(((r ^ sizes.pair_slab(c // 2)) & step) != 0, other, value)


def per_device(trailing, panel_rows, pivot_block, panel_fill):
    sizes = Sizes(trailing, panel_rows, panel_fill)
    fill = panel_fill.reshape(-1)
    r, c = lax.axis_index("row"), lax.axis_index("col")
    where = jnp.stack([c, r]).astype(jnp.int32)
    side, core = c % 2, r % 2
    quarter = sizes.unit // 4
    split = min(4, pivot_block.shape[0] // 8)
    share = pivot_block.shape[0] // split
    most, column_most = 8 * sizes.per_piece, sizes.column_units
    levels = [(most * 5 // 12, column_most * 3 // 4), (most, column_most)]

    units = panel_rows.reshape(sizes.per_piece, sizes.unit, -1)
    quarters = panel_rows.reshape(sizes.per_piece, 2, 2, quarter, -1)

    def at_core(which):
        return lax.dynamic_index_in_dim(quarters, which, 2, keepdims=False)

    pivot = lax.dynamic_slice_in_dim(pivot_block, r % split * share, share, 0)[None]
    pivot = join(c, 1, pivot, swap(pivot, "col", 1))
    from_core = swap(at_core(1 - core), "row", 1)
    from_core, pivot = lax.optimization_barrier((from_core, pivot))
    both = jnp.stack([at_core(core), from_core])
    from_side = swap(lax.dynamic_index_in_dim(both, 1 - side, 2, keepdims=False), "col", 1)
    step = 2
    while step < sizes.cols:
        pivot = join(c, step, pivot, swap(pivot, "col", step))
        step *= 2

    def run(cap, column_cap, trailing, panel_rows, fill, units, from_core, from_side, pivot):
        own = pack(sizes, cap, where, fill, units, from_core, from_side)
        lists = {0: own}
        first = [s for s in range(1, sizes.groups) if s in sizes.needed]
        later = [s for s in range(1, sizes.groups) if s not in sizes.needed]
        lists |= {s: bring(sizes, own, s) for s in first}
        sides = {0: swap(own, "col", 1)}
        parts = [pivot] + ([swap(pivot, "row", 2)] if split == 4 else [])
        parts = [part for value in parts for part in (value, swap(value, "row", 1))]
        near = first[0]
        lists[near], sides[0], *parts = lax.optimization_barrier((lists[near], sides[0], *parts))
        sides[near] = swap(lists[near], "col", 1)
        w = inverse_factor(where, parts)
        soon, rest = [0, near], [s for s in sizes.needed if s not in (0, near)]
        column = pack_column(sizes, cap, column_cap, soon, where, fill, [lists[s] for s in soon])
        held = lax.optimization_barrier((w, column, sides[0], sides[near], *lists.values()))
        w, column, sides[0], sides[near] = held[:4]
        lists = dict(zip(lists, held[4:]))

        column = pack_column(sizes, cap, column_cap, rest, where, fill, [lists[s] for s in rest], [column])
        lists |= {s: bring(sizes, lists[0], s) for s in later}
        sides |= {s: swap(lists[s], "col", 1) for s in first[1:]}
        step = sizes.rows // 2
        while step > 1:
            column = spread_column(sizes, column, step)
            step //= 2
        panel_factor, slots, window = own_factor(sizes, where, fill, w, panel_rows, trailing)
        column, slots = lax.optimization_barrier((column, slots))
        across = swap(lax.dynamic_index_in_dim(column, 1 - side, 0, keepdims=False), "col", 1)
        column = lax.dynamic_index_in_dim(column, side, 0, keepdims=False)
        columns = [column, swap(column, "row", 1), across, swap(across, "row", 1)]
        for s in later:
            lists[s] = lax.optimization_barrier((lists[s], slots, *(sides[j] for j in first)))[0]
            sides[s] = swap(lists[s], "col", 1)
        column = column_factor(sizes, where, fill, w, columns)
        for s in later:
            sides[s], column = lax.optimization_barrier((sides[s], column))
        ordered = []
        for s in range(sizes.groups):
            value, other = lists[s], sides[s]
            if s in later:
                ordered.append((value, other, swap(value, "row", 1), swap(other, "row", 1)))
            else:
                ordered.append((value, other, swap(jnp.stack([value, other]), "row", 1)))
        return update(sizes, where, slots, column, window, ordered), panel_factor

    operands = (trailing, panel_rows, fill, units, from_core, from_side, pivot)
    branches = [functools.partial(run, *level) for level in levels]
    return lax.cond(level_of(sizes, levels, fill)[0] == 0, *branches, *operands)


def solution(mesh):
    in_specs = (P("row", "col"), P(("row", "col"), None), P("col", None), P())
    out_specs = (P("row", "col"), P(("row", "col"), None))
    return jax.shard_map(
        per_device, mesh=mesh, in_specs=in_specs, out_specs=out_specs, check_vma=False
    )
```

```python
import functools
import math

import jax
import jax.numpy as jnp
from jax import lax
from jax.experimental import pallas as pl
from jax.experimental.pallas import tpu as pltpu
from jax.sharding import PartitionSpec as P

F32, BF16 = jnp.float32, jnp.bfloat16
VMEM = pl.BlockSpec(memory_space=pltpu.VMEM)
SMEM = pl.BlockSpec(memory_space=pltpu.SMEM)
HBM = pl.BlockSpec(memory_space=pltpu.HBM)
COARSE_STEPS = 2
FINE_STEPS = 16
RESIDUAL = 5e-4
STAGES = 8


def halves(value):
    high = value.astype(BF16)
    return high, (value - high.astype(F32)).astype(BF16)


def dot(a, b, dims):
    return lax.dot_general(a, b, (dims, ((), ())), preferred_element_type=F32)


NN, NT, TN = ((1,), (0,)), ((1,), (1,)), ((0,), (0,))


def dot3(a, b, dims):
    (ah, al), (bh, bl) = a, b
    return dot(ah, bh, dims) + (dot(ah, bl, dims) + dot(al, bh, dims))


def inverse_factor_kernel(where_ref, *refs):
    parts, (w_ref, s_ref) = refs[:-2], refs[-2:]
    n = w_ref.shape[0]
    pieces, share = parts[0].shape[0], parts[0].shape[1]
    own = where_ref[1] % len(parts)
    for flip, ref in enumerate(parts):
        at = jnp.bitwise_xor(own, flip) * share
        for i in range(pieces):
            s_ref[pl.ds(pl.multiple_of(i * len(parts) * share + at, share), share), :] = ref[i]
    rows = lax.broadcasted_iota(jnp.int32, (n, n), 0)
    cols = lax.broadcasted_iota(jnp.int32, (n, n), 1)
    eye = (rows == cols).astype(F32)
    take = jnp.where(rows > cols, 1.0, 0.5 * eye)
    a = s_ref[...]
    diag_row = jnp.sum(a * eye, axis=0, keepdims=True)
    diag_col = jnp.sum(a * eye, axis=1, keepdims=True)
    scale_row, scale_col = lax.rsqrt(diag_row), lax.rsqrt(diag_col)
    scaled = jnp.where(rows == cols, 1.0, a * scale_row * scale_col)
    s_ref[...] = scaled
    scaled_parts = halves(scaled)
    w = eye - take * (scaled - eye)
    for _ in range(COARSE_STEPS):
        wh = w.astype(BF16)
        t = dot(wh, scaled_parts[0], NN).astype(BF16)
        change = take * (dot(t, wh, NT) - eye)
        w = w - dot(change.astype(BF16), wh, NN)
    w_ref[...] = w

    def fine(state):
        step, _ = state
        w = w_ref[...]
        parts = halves(w)
        t = halves(dot3(parts, halves(s_ref[...]), NN))
        residual = dot3(t, parts, NT) - eye
        w_ref[...] = w - dot((take * residual).astype(BF16), parts[0], NN)
        return step + 1, jnp.sum(residual * residual)

    _, left = lax.while_loop(
        lambda state: jnp.logical_and(state[0] < FINE_STEPS, jnp.logical_not(state[1] < RESIDUAL**2)),
        fine,
        (jnp.int32(0), jnp.float32(1.0)),
    )
    done = left < RESIDUAL**2

    @pl.when(jnp.logical_not(done))
    def _():
        w_ref[...] = eye

        def eliminate(j, carry):
            row = s_ref[pl.ds(j, 1), :]
            pick = lax.broadcasted_iota(jnp.int32, (1, n), 1) == j
            pivot = jnp.sum(jnp.where(pick, row, 0.0), axis=1, keepdims=True)
            column = jnp.sum(jnp.where(pick, s_ref[...], 0.0), axis=1, keepdims=True)
            below = lax.broadcasted_iota(jnp.int32, (n, 1), 0) > j
            ratio = jnp.where(below, column / pivot, 0.0)
            s_ref[...] = s_ref[...] - ratio * row
            w_ref[...] = w_ref[...] - ratio * w_ref[pl.ds(j, 1), :]
            return carry

        lax.fori_loop(0, n, eliminate, 0)
        pivots = jnp.sum(s_ref[...] * eye, axis=1, keepdims=True)
        w_ref[...] = w_ref[...] * lax.rsqrt(pivots)

    w_ref[...] = w_ref[...] * scale_row


def inverse_factor(where, parts):
    n = parts[0].shape[-1]
    return pl.pallas_call(
        inverse_factor_kernel,
        out_shape=jax.ShapeDtypeStruct((n, n), F32),
        in_specs=[SMEM] + [VMEM] * len(parts),
        out_specs=VMEM,
        scratch_shapes=[pltpu.VMEM((n, n), F32)],
        compiler_params=pltpu.CompilerParams(vmem_limit_bytes=20 * 2**20),
    )(where, *parts)


class Sizes:
    def __init__(self, trailing, panel_rows, panel_fill):
        self.cols, self.rows = lax.axis_size("col"), lax.axis_size("row")
        self.block = panel_rows.shape[1] // 2
        self.piece = panel_rows.shape[0]
        self.unit = math.gcd(self.piece, self.block)
        self.per_piece = self.piece // self.unit
        self.per_block = self.block // self.unit
        self.slab = self.piece * self.cols
        self.merge = self.per_block if 2 * self.piece % self.block == 0 else 1
        self.width = trailing.shape[1]
        self.tiles = self.cols * self.per_piece

        self.groups = self.cols // 2
        self.column_units = 2 * self.width // self.unit
        self.needed = sorted({s for g in range(self.groups) for s in self.shifts(g)})

    def pair_slab(self, group):
        return 2 * group * self.width // self.slab

    def pair_start(self, group):
        return (2 * group * self.width - self.pair_slab(group) * self.slab) // self.unit

    def shifts(self, group):
        start = self.pair_start(group) * self.unit
        first, last = start // (2 * self.piece), (start + 2 * self.width - 1) // (2 * self.piece)
        return [(g - group) % self.groups for g in range(first, last + 1)]


def unit_flag(sizes, fill_ref, piece_index, unit, panel):
    block = (piece_index * sizes.per_piece + unit) // sizes.per_block
    return fill_ref[block * 2 + panel] != 0


def pool_pieces(sizes, pool_row, pool_col):
    for core in range(2):
        for side in range(2):
            yield core, side, (pool_row * 2 + core) * sizes.cols + pool_col * 2 + side


def pair_flag(sizes, fill_ref, group, index):
    unit = sizes.pair_slab(group) * sizes.tiles + sizes.pair_start(group) + index // 2
    return fill_ref[unit // sizes.per_block * 2 + index % 2] != 0


def level_kernel(sizes, levels, fill_ref, out_ref):
    pool_most, column_most = jnp.int32(0), jnp.int32(0)
    for pool_row in range(sizes.rows // 2):
        for pool_col in range(sizes.groups):
            count = jnp.int32(0)
            for _, _, piece in pool_pieces(sizes, pool_row, pool_col):
                for u in range(sizes.per_piece):
                    for p in range(2):
                        count = count + unit_flag(sizes, fill_ref, piece, u, p).astype(jnp.int32)
            pool_most = jnp.maximum(pool_most, count)
    for group in range(sizes.groups):
        for side in range(2):
            count = jnp.int32(0)
            for i in range(sizes.column_units):
                flag = pair_flag(sizes, fill_ref, group, side * sizes.column_units + i)
                count = count + flag.astype(jnp.int32)
            column_most = jnp.maximum(column_most, count)
    level = jnp.int32(0)
    for cap, column_cap in levels[:-1]:
        fits = jnp.logical_and(pool_most <= cap, column_most <= column_cap)
        level = level + jnp.logical_not(fits).astype(jnp.int32)
    out_ref[0] = level


def level_of(sizes, levels, fill):
    return pl.pallas_call(
        functools.partial(level_kernel, sizes, levels),
        out_shape=jax.ShapeDtypeStruct((1,), jnp.int32),
        in_specs=[SMEM],
        out_specs=SMEM,
    )(fill)


def pack_kernel(sizes, cap, where_ref, fill_ref, panel_ref, core_ref, side_ref, out_ref, pool):
    c, r = where_ref[0], where_ref[1]
    side, core = c % 2, r % 2
    quarter = sizes.unit // 4
    own_at = pl.multiple_of((side * 2 + core) * quarter, quarter)
    for u in range(sizes.per_piece):
        pool[core, side, u] = panel_ref[u, pl.ds(own_at, quarter), :]
        pool[1 - core, side, u] = core_ref[u, side]
        pool[core, 1 - side, u] = side_ref[0, u]
        pool[1 - core, 1 - side, u] = side_ref[1, u]
    slot = jnp.int32(0)
    for core_at, side_at, piece in pool_pieces(sizes, r // 2, c // 2):
        for u in range(sizes.per_piece):
            for p in range(2):
                flag = unit_flag(sizes, fill_ref, piece, u, p)

                @pl.when(flag)
                def _(slot=slot, core_at=core_at, side_at=side_at, u=u, p=p):
                    out_ref[jnp.minimum(slot, cap - 1)] = pool[
                        core_at, side_at, u, :, p * sizes.block : (p + 1) * sizes.block
                    ]

                slot = slot + flag.astype(jnp.int32)


def pack(sizes, cap, where, fill, panel, from_core, from_side):
    quarter = sizes.unit // 4
    return pl.pallas_call(
        functools.partial(pack_kernel, sizes, cap),
        out_shape=jax.ShapeDtypeStruct((cap, quarter, sizes.block), F32),
        in_specs=[SMEM, SMEM, VMEM, VMEM, VMEM],
        out_specs=VMEM,
        scratch_shapes=[pltpu.VMEM((2, 2, sizes.per_piece, quarter, 2 * sizes.block), F32)],
        compiler_params=pltpu.CompilerParams(vmem_limit_bytes=16 * 2**20),
    )(where, fill, panel, from_core, from_side)


def pair_slots(sizes, fill_ref, group, slots):
    def step(i, slot):
        flag = pair_flag(sizes, fill_ref, group, i)
        slot = jnp.where(i == sizes.column_units, 0, slot)
        slots[i] = jnp.where(flag, slot, -1)
        return slot + flag.astype(jnp.int32)

    lax.fori_loop(0, 2 * sizes.column_units, step, jnp.int32(0))


def pack_column_kernel(sizes, cap, column_cap, shifts, where_ref, fill_ref, *refs):
    lists, before, (out_ref, slots) = refs[: len(shifts)], refs[len(shifts) : -2], refs[-2:]
    own = where_ref[0] // 2
    slab, start = sizes.pair_slab(own), sizes.pair_start(own)
    pair_slots(sizes, fill_ref, own, slots)
    for ref in before:
        out_ref[...] = ref[...]
    for shift, list_ref in zip(shifts, lists):
        group = lax.rem(own + shift, sizes.groups)
        slot = jnp.int32(0)
        for core, side, piece in pool_pieces(sizes, slab // 2, group):
            for u in range(sizes.per_piece):
                for p in range(2):
                    flag = unit_flag(sizes, fill_ref, piece, u, p)
                    index = (((group * 2 + side) * sizes.per_piece + u) - start) * 2 + p
                    inside = jnp.logical_and(index >= 0, index < 2 * sizes.column_units)
                    wanted = jnp.logical_and(jnp.logical_and(flag, inside), slab % 2 == core)

                    @pl.when(wanted)
                    def _(slot=slot, index=index, list_ref=list_ref):
                        index = jnp.clip(index, 0, 2 * sizes.column_units - 1)
                        target = jnp.clip(slots[index], 0, column_cap - 1)
                        out_ref[index // sizes.column_units, target] = list_ref[jnp.minimum(slot, cap - 1)]

                    slot = slot + flag.astype(jnp.int32)


def pack_column(sizes, cap, column_cap, shifts, where, fill, lists, before=()):
    return pl.pallas_call(
        functools.partial(pack_column_kernel, sizes, cap, column_cap, shifts),
        out_shape=jax.ShapeDtypeStruct((2, column_cap, sizes.unit // 4, sizes.block), F32),
        in_specs=[SMEM, SMEM] + [VMEM] * (len(lists) + len(before)),
        out_specs=VMEM,
        scratch_shapes=[pltpu.SMEM((2 * sizes.column_units,), jnp.int32)],
        compiler_params=pltpu.CompilerParams(vmem_limit_bytes=20 * 2**20),
    )(where, fill, *lists, *before)


def own_factor_kernel(sizes, where_ref, fill_ref, w_ref, panel_ref, window_ref, x_ref, slot_ref, near_ref, inverse_ref, masked, sem, sems):
    c, r = where_ref[0], where_ref[1]
    rows = window_ref.shape[0] // STAGES
    stages = []
    for i in range(STAGES):
        at = pl.ds(i * rows, rows)
        stages.append(pltpu.make_async_copy(window_ref.at[at], near_ref.at[at], sems.at[i]))
        stages[i].start()
    own = r * sizes.cols + c
    for u in range(sizes.per_piece):
        for p in range(2):
            at = (pl.ds(u * sizes.unit, sizes.unit), pl.ds(p * sizes.block, sizes.block))
            masked[at] = jnp.where(unit_flag(sizes, fill_ref, own, u, p), panel_ref[at], 0.0)
    w = halves(w_ref[...])
    masked[...] = dot3(halves(masked[...]), w, NT)
    copy_out = pltpu.make_async_copy(masked, x_ref, sem)
    copy_out.start()
    inverse_ref[...] = dot3(w, w, TN)

    @pl.loop(0, sizes.groups)
    def _(shift):
        group = lax.rem(c // 2 + shift, sizes.groups)
        slot = jnp.int32(0)
        for core, side, piece in pool_pieces(sizes, r // 2, group):
            for u in range(sizes.per_piece):
                for p in range(2):
                    flag = unit_flag(sizes, fill_ref, piece, u, p)

                    @pl.when(core == r % 2)
                    def _(slot=slot, flag=flag, side=side, u=u, p=p):
                        at = ((shift * 2 + side) * sizes.per_piece + u) * 2 + p
                        slot_ref[at] = jnp.where(flag, slot, -1)

                    slot = slot + flag.astype(jnp.int32)

    copy_out.wait()
    for stage in stages:
        stage.wait()


def own_factor(sizes, where, fill, w, panel, window):
    return pl.pallas_call(
        functools.partial(own_factor_kernel, sizes),
        out_shape=(
            pltpu.HBM(panel.shape, F32),
            jax.ShapeDtypeStruct((2 * sizes.tiles,), jnp.int32),
            pltpu.VMEM(window.shape, F32),
            jax.ShapeDtypeStruct(w.shape, F32),
        ),
        in_specs=[SMEM, SMEM, VMEM, VMEM, HBM],
        out_specs=(HBM, SMEM, VMEM, VMEM),
        scratch_shapes=[
            pltpu.VMEM(panel.shape, F32),
            pltpu.SemaphoreType.DMA,
            pltpu.SemaphoreType.DMA((STAGES,)),
        ],
        compiler_params=pltpu.CompilerParams(vmem_limit_bytes=20 * 2**20),
    )(where, fill, w, panel, window)


def column_factor_kernel(sizes, where_ref, fill_ref, inverse_ref, *refs):
    lists, (out_ref, column, slots) = refs[:4], refs[4:]
    c, r = where_ref[0], where_ref[1]
    side, core = c % 2, r % 2
    quarter = sizes.unit // 4
    pair_slots(sizes, fill_ref, c // 2, slots)
    column[...] = jnp.zeros_like(column)

    @pl.loop(0, sizes.column_units // 2)
    def _(unit):
        for p in range(2):
            slot = slots[side * sizes.column_units + unit * 2 + p]

            @pl.when(slot >= 0)
            def _(slot=slot, p=p):
                for flip in range(4):
                    from_side = jnp.bitwise_xor(side, flip // 2)
                    from_core = jnp.bitwise_xor(core, flip % 2)
                    at = pl.multiple_of(unit * sizes.unit + (from_side * 2 + from_core) * quarter, quarter)
                    column[pl.ds(at, quarter), pl.ds(p * sizes.block, sizes.block)] = lists[flip][slot]

    out_ref[...] = dot3(halves(inverse_ref[...]), halves(column[...]), NT)


def column_factor(sizes, where, fill, inverse, lists):
    n = inverse.shape[0]
    return pl.pallas_call(
        functools.partial(column_factor_kernel, sizes),
        out_shape=jax.ShapeDtypeStruct((n, sizes.width), F32),
        in_specs=[SMEM, SMEM, VMEM] + [VMEM] * 4,
        out_specs=VMEM,
        scratch_shapes=[pltpu.VMEM((sizes.width, n), F32), pltpu.SMEM((2 * sizes.column_units,), jnp.int32)],
        compiler_params=pltpu.CompilerParams(vmem_limit_bytes=20 * 2**20),
    )(where, fill, inverse, *lists)


def update_kernel(sizes, counts, where_ref, slot_ref, column_ref, window_ref, *refs):
    groups, merge = sizes.groups, sizes.merge
    refs, (out_ref, tiles, data, right, out_sems) = list(refs[:-5]), refs[-5:]
    lists = []
    for count in counts:
        own, other, *cores = [refs.pop(0) for _ in range(count)]
        cores = cores if count == 4 else [cores[0].at[0], cores[0].at[1]]
        lists += [own, cores[0], other, cores[1]]
    c, r = where_ref[0], where_ref[1]
    side, core = c % 2, r % 2
    per_group = 2 * sizes.per_piece // merge
    rows = merge * sizes.unit
    quarter = sizes.unit // 4

    def rows_of(t):
        group = lax.rem(c // 2 + t // per_group, groups)
        return pl.ds(pl.multiple_of((group * per_group + t % per_group) * rows, rows), rows)

    def tile_out(t, source):
        return pltpu.make_async_copy(source, out_ref.at[rows_of(t)], out_sems.at[t])

    def slot_of(t, p, part):
        return slot_ref[(t * merge + part) * 2 + p]

    def active(t):
        return jnp.logical_or(slot_of(t, 0, 0) >= 0, slot_of(t, 1, 0) >= 0)

    @pl.loop(0, per_group * groups)
    def _(t):
        pl.when(jnp.logical_not(active(t)))(tile_out(t, window_ref.at[rows_of(t)]).start)

    for p in range(2):
        high, low = halves(column_ref[p * sizes.block : (p + 1) * sizes.block, :])
        for i, part in enumerate((high, low, high)):
            right[p, i * sizes.block : (i + 1) * sizes.block, :] = part

    for group in range(groups):

        @pl.loop(group * per_group, (group + 1) * per_group)
        def _(t, group=group):
            @pl.when(active(t))
            def _():
                tiles[t] = window_ref[rows_of(t), :]
                for p in range(2):

                    @pl.when(slot_of(t, p, 0) >= 0)
                    def _(p=p):
                        for part in range(merge):
                            slot = slot_of(t, p, part)
                            for flip in range(4):
                                from_side = jnp.bitwise_xor(side, flip // 2)
                                from_core = jnp.bitwise_xor(core, flip % 2)
                                at = pl.multiple_of((part * 4 + from_side * 2 + from_core) * quarter, quarter)
                                data[pl.ds(at, quarter), :] = lists[4 * group + flip][slot]
                        high, low = halves(data[...])
                        left = jnp.concatenate([high, high, low], axis=1)
                        tiles[t] = tiles[t] - dot(left, right[p], NN)

                tile_out(t, tiles.at[t]).start()

    @pl.loop(0, per_group * groups)
    def _(t):
        tile_out(t, tiles.at[t]).wait()


def update(sizes, where, slots, column, window, lists):
    rows = sizes.merge * sizes.unit
    tiles = sizes.slab // rows
    list_bytes = 4 * sum(value.size for group in lists for value in group)
    return pl.pallas_call(
        functools.partial(update_kernel, sizes, [len(group) for group in lists]),
        out_shape=pltpu.HBM(window.shape, F32),
        in_specs=[SMEM, SMEM, VMEM, VMEM] + [VMEM] * sum(len(group) for group in lists),
        out_specs=HBM,
        scratch_shapes=[
            pltpu.VMEM((tiles, rows, sizes.width), F32),
            pltpu.VMEM((rows, sizes.block), F32),
            pltpu.VMEM((2, 3 * sizes.block, sizes.width), BF16),
            pltpu.SemaphoreType.DMA((tiles,)),
        ],
        compiler_params=pltpu.CompilerParams(vmem_limit_bytes=14 * 2**20 + list_bytes),
    )(where, slots, column, window, *(value for group in lists for value in group))


def swap(value, axis, step):
    size = lax.axis_size(axis)
    return lax.ppermute(value, axis, [(i, i ^ step) for i in range(size)])


def join(index, step, own, other):
    second = (index & step) != 0
    return jnp.where(second, jnp.concatenate([other, own], 0), jnp.concatenate([own, other], 0))


def after(value, *earlier):
    return lax.optimization_barrier((value, *earlier))[0]


def bring(sizes, value, shift):
    pairs = [(i, (i - 2 * shift) % sizes.cols) for i in range(sizes.cols)]
    return lax.ppermute(value, "col", pairs)


def spread_column(sizes, value, step):
    r, c = lax.axis_index("row"), lax.axis_index("col")
    pairs = []
    for at in range(sizes.cols):
        slab = sizes.pair_slab(at // 2)
        for row in range(sizes.rows):
            if (row // 2 ^ slab // 2) % step == 0:
                pairs.append((at * sizes.rows + row, at * sizes.rows + (row ^ step)))
    other = lax.ppermute(value, ("col", "row"), pairs)
    return jnp.where(((r ^ sizes.pair_slab(c // 2)) & step) != 0, other, value)


def per_device(trailing, panel_rows, pivot_block, panel_fill):
    sizes = Sizes(trailing, panel_rows, panel_fill)
    fill = panel_fill.reshape(-1)
    r, c = lax.axis_index("row"), lax.axis_index("col")
    where = jnp.stack([c, r]).astype(jnp.int32)
    side, core = c % 2, r % 2
    quarter = sizes.unit // 4
    split = min(4, pivot_block.shape[0] // 8)
    share = pivot_block.shape[0] // split
    most, column_most = 8 * sizes.per_piece, sizes.column_units
    levels = [(most * 5 // 12, column_most * 3 // 4), (most, column_most)]

    units = panel_rows.reshape(sizes.per_piece, sizes.unit, -1)
    quarters = panel_rows.reshape(sizes.per_piece, 2, 2, quarter, -1)

    def at_core(which):
        return lax.dynamic_index_in_dim(quarters, which, 2, keepdims=False)

    pivot = lax.dynamic_slice_in_dim(pivot_block, r % split * share, share, 0)[None]
    pivot = join(c, 1, pivot, swap(pivot, "col", 1))
    from_core = swap(at_core(1 - core), "row", 1)
    from_core, pivot = lax.optimization_barrier((from_core, pivot))
    both = jnp.stack([at_core(core), from_core])
    from_side = swap(lax.dynamic_index_in_dim(both, 1 - side, 2, keepdims=False), "col", 1)
    step = 2
    while step < sizes.cols:
        pivot = join(c, step, pivot, swap(pivot, "col", step))
        step *= 2

    def run(cap, column_cap, trailing, panel_rows, fill, units, from_core, from_side, pivot):
        own = pack(sizes, cap, where, fill, units, from_core, from_side)
        lists = {0: own}
        first = [s for s in range(1, sizes.groups) if s in sizes.needed]
        later = [s for s in range(1, sizes.groups) if s not in sizes.needed]
        lists |= {s: bring(sizes, own, s) for s in first}
        sides = {0: swap(own, "col", 1)}
        parts = [pivot] + ([swap(pivot, "row", 2)] if split == 4 else [])
        parts = [part for value in parts for part in (value, swap(value, "row", 1))]
        near = first[0]
        lists[near], *parts = lax.optimization_barrier((lists[near], *parts))
        sides[near] = swap(lists[near], "col", 1)
        w = inverse_factor(where, parts)
        soon, rest = [0, near], [s for s in sizes.needed if s not in (0, near)]
        column = pack_column(sizes, cap, column_cap, soon, where, fill, [lists[s] for s in soon])
        held = lax.optimization_barrier((w, column, sides[0], sides[near], *lists.values()))
        w, column, sides[0], sides[near] = held[:4]
        lists = dict(zip(lists, held[4:]))

        column = pack_column(sizes, cap, column_cap, rest, where, fill, [lists[s] for s in rest], [column])
        lists |= {s: bring(sizes, lists[0], s) for s in later}
        sides |= {s: swap(lists[s], "col", 1) for s in first[1:]}
        step = sizes.rows // 2
        while step > 1:
            column = spread_column(sizes, column, step)
            step //= 2
        panel_factor, slots, window, inverse = own_factor(sizes, where, fill, w, panel_rows, trailing)
        column, slots = lax.optimization_barrier((column, slots))
        across = swap(lax.dynamic_index_in_dim(column, 1 - side, 0, keepdims=False), "col", 1)
        column = lax.dynamic_index_in_dim(column, side, 0, keepdims=False)
        columns = [column, swap(column, "row", 1), across, swap(across, "row", 1)]
        for s in later:
            lists[s] = lax.optimization_barrier((lists[s], slots, *(sides[j] for j in first)))[0]
            sides[s] = swap(lists[s], "col", 1)
        column = column_factor(sizes, where, fill, inverse, columns)
        for s in later:
            sides[s], column = lax.optimization_barrier((sides[s], column))
        ordered = []
        for s in range(sizes.groups):
            value, other = lists[s], sides[s]
            if s in later:
                ordered.append((value, other, swap(value, "row", 1), swap(other, "row", 1)))
            else:
                ordered.append((value, other, swap(jnp.stack([value, other]), "row", 1)))
        return update(sizes, where, slots, column, window, ordered), panel_factor

    operands = (trailing, panel_rows, fill, units, from_core, from_side, pivot)
    branches = [functools.partial(run, *level) for level in levels]
    return lax.cond(level_of(sizes, levels, fill)[0] == 0, *branches, *operands)


def solution(mesh):
    in_specs = (P("row", "col"), P(("row", "col"), None), P("col", None), P())
    out_specs = (P("row", "col"), P(("row", "col"), None))
    return jax.shard_map(
        per_device, mesh=mesh, in_specs=in_specs, out_specs=out_specs, check_vma=False
    )
```

```python
import functools
import math

import jax
import jax.numpy as jnp
from jax import lax
from jax.experimental import pallas as pl
from jax.experimental.pallas import tpu as pltpu
from jax.sharding import PartitionSpec as P

F32, BF16 = jnp.float32, jnp.bfloat16
VMEM = pl.BlockSpec(memory_space=pltpu.VMEM)
SMEM = pl.BlockSpec(memory_space=pltpu.SMEM)
HBM = pl.BlockSpec(memory_space=pltpu.HBM)
COARSE_STEPS = 2
FINE_STEPS = 16
RESIDUAL = 5e-4
STAGES = 8


def halves(value):
    high = value.astype(BF16)
    return high, (value - high.astype(F32)).astype(BF16)


def dot(a, b, dims):
    return lax.dot_general(a, b, (dims, ((), ())), preferred_element_type=F32)


NN, NT, TN = ((1,), (0,)), ((1,), (1,)), ((0,), (0,))


def dot3(a, b, dims):
    (ah, al), (bh, bl) = a, b
    return dot(ah, bh, dims) + (dot(ah, bl, dims) + dot(al, bh, dims))


def inverse_factor_kernel(where_ref, *refs):
    parts, (w_ref, s_ref) = refs[:-2], refs[-2:]
    n = w_ref.shape[0]
    pieces, share = parts[0].shape[0], parts[0].shape[1]
    own = where_ref[1] % len(parts)
    for flip, ref in enumerate(parts):
        at = jnp.bitwise_xor(own, flip) * share
        for i in range(pieces):
            s_ref[pl.ds(pl.multiple_of(i * len(parts) * share + at, share), share), :] = ref[i]
    rows = lax.broadcasted_iota(jnp.int32, (n, n), 0)
    cols = lax.broadcasted_iota(jnp.int32, (n, n), 1)
    eye = (rows == cols).astype(F32)
    take = jnp.where(rows > cols, 1.0, 0.5 * eye)
    a = s_ref[...]
    diag_row = jnp.sum(a * eye, axis=0, keepdims=True)
    diag_col = jnp.sum(a * eye, axis=1, keepdims=True)
    scale_row, scale_col = lax.rsqrt(diag_row), lax.rsqrt(diag_col)
    scaled = jnp.where(rows == cols, 1.0, a * scale_row * scale_col)
    s_ref[...] = scaled
    scaled_parts = halves(scaled)
    w = eye - take * (scaled - eye)
    for _ in range(COARSE_STEPS):
        wh = w.astype(BF16)
        t = dot(wh, scaled_parts[0], NN).astype(BF16)
        change = take * (dot(t, wh, NT) - eye)
        w = w - dot(change.astype(BF16), wh, NN)
    w_ref[...] = w

    def fine(state):
        step, _ = state
        w = w_ref[...]
        parts = halves(w)
        t = halves(dot3(parts, halves(s_ref[...]), NN))
        residual = dot3(t, parts, NT) - eye
        w_ref[...] = w - dot((take * residual).astype(BF16), parts[0], NN)
        return step + 1, jnp.sum(residual * residual)

    _, left = lax.while_loop(
        lambda state: jnp.logical_and(state[0] < FINE_STEPS, jnp.logical_not(state[1] < RESIDUAL**2)),
        fine,
        (jnp.int32(0), jnp.float32(1.0)),
    )
    done = left < RESIDUAL**2

    @pl.when(jnp.logical_not(done))
    def _():
        w_ref[...] = eye

        def eliminate(j, carry):
            row = s_ref[pl.ds(j, 1), :]
            pick = lax.broadcasted_iota(jnp.int32, (1, n), 1) == j
            pivot = jnp.sum(jnp.where(pick, row, 0.0), axis=1, keepdims=True)
            column = jnp.sum(jnp.where(pick, s_ref[...], 0.0), axis=1, keepdims=True)
            below = lax.broadcasted_iota(jnp.int32, (n, 1), 0) > j
            ratio = jnp.where(below, column / pivot, 0.0)
            s_ref[...] = s_ref[...] - ratio * row
            w_ref[...] = w_ref[...] - ratio * w_ref[pl.ds(j, 1), :]
            return carry

        lax.fori_loop(0, n, eliminate, 0)
        pivots = jnp.sum(s_ref[...] * eye, axis=1, keepdims=True)
        w_ref[...] = w_ref[...] * lax.rsqrt(pivots)

    w_ref[...] = w_ref[...] * scale_row


def inverse_factor(where, parts):
    n = parts[0].shape[-1]
    return pl.pallas_call(
        inverse_factor_kernel,
        out_shape=jax.ShapeDtypeStruct((n, n), F32),
        in_specs=[SMEM] + [VMEM] * len(parts),
        out_specs=VMEM,
        scratch_shapes=[pltpu.VMEM((n, n), F32)],
        compiler_params=pltpu.CompilerParams(vmem_limit_bytes=20 * 2**20),
    )(where, *parts)


class Sizes:
    def __init__(self, trailing, panel_rows, panel_fill):
        self.cols, self.rows = lax.axis_size("col"), lax.axis_size("row")
        self.block = panel_rows.shape[1] // 2
        self.piece = panel_rows.shape[0]
        self.unit = math.gcd(self.piece, self.block)
        self.per_piece = self.piece // self.unit
        self.per_block = self.block // self.unit
        self.slab = self.piece * self.cols
        self.merge = self.per_block if 2 * self.piece % self.block == 0 else 1
        self.width = trailing.shape[1]
        self.tiles = self.cols * self.per_piece

        self.groups = self.cols // 2
        self.column_units = 2 * self.width // self.unit
        self.needed = sorted({s for g in range(self.groups) for s in self.shifts(g)})

    def pair_slab(self, group):
        return 2 * group * self.width // self.slab

    def pair_start(self, group):
        return (2 * group * self.width - self.pair_slab(group) * self.slab) // self.unit

    def shifts(self, group):
        start = self.pair_start(group) * self.unit
        first, last = start // (2 * self.piece), (start + 2 * self.width - 1) // (2 * self.piece)
        return [(g - group) % self.groups for g in range(first, last + 1)]


def unit_flag(sizes, fill_ref, piece_index, unit, panel):
    block = (piece_index * sizes.per_piece + unit) // sizes.per_block
    return fill_ref[block * 2 + panel] != 0


def pool_pieces(sizes, pool_row, pool_col):
    for core in range(2):
        for side in range(2):
            yield core, side, (pool_row * 2 + core) * sizes.cols + pool_col * 2 + side


def pair_flag(sizes, fill_ref, group, index):
    unit = sizes.pair_slab(group) * sizes.tiles + sizes.pair_start(group) + index // 2
    return fill_ref[unit // sizes.per_block * 2 + index % 2] != 0


def level_kernel(sizes, levels, fill_ref, out_ref):
    pool_most, column_most = jnp.int32(0), jnp.int32(0)
    for pool_row in range(sizes.rows // 2):
        for pool_col in range(sizes.groups):
            count = jnp.int32(0)
            for _, _, piece in pool_pieces(sizes, pool_row, pool_col):
                for u in range(sizes.per_piece):
                    for p in range(2):
                        count = count + unit_flag(sizes, fill_ref, piece, u, p).astype(jnp.int32)
            pool_most = jnp.maximum(pool_most, count)
    for group in range(sizes.groups):
        for side in range(2):
            count = jnp.int32(0)
            for i in range(sizes.column_units):
                flag = pair_flag(sizes, fill_ref, group, side * sizes.column_units + i)
                count = count + flag.astype(jnp.int32)
            column_most = jnp.maximum(column_most, count)
    level = jnp.int32(0)
    for cap, column_cap in levels[:-1]:
        fits = jnp.logical_and(pool_most <= cap, column_most <= column_cap)
        level = level + jnp.logical_not(fits).astype(jnp.int32)
    out_ref[0] = level


def level_of(sizes, levels, fill):
    return pl.pallas_call(
        functools.partial(level_kernel, sizes, levels),
        out_shape=jax.ShapeDtypeStruct((1,), jnp.int32),
        in_specs=[SMEM],
        out_specs=SMEM,
    )(fill)


def pack_kernel(sizes, cap, where_ref, fill_ref, panel_ref, core_ref, side_ref, out_ref, pool):
    c, r = where_ref[0], where_ref[1]
    side, core = c % 2, r % 2
    quarter = sizes.unit // 4
    own_at = pl.multiple_of((side * 2 + core) * quarter, quarter)
    for u in range(sizes.per_piece):
        pool[core, side, u] = panel_ref[u, pl.ds(own_at, quarter), :]
        pool[1 - core, side, u] = core_ref[u, side]
        pool[core, 1 - side, u] = side_ref[0, u]
        pool[1 - core, 1 - side, u] = side_ref[1, u]
    slot = jnp.int32(0)
    for core_at, side_at, piece in pool_pieces(sizes, r // 2, c // 2):
        for u in range(sizes.per_piece):
            for p in range(2):
                flag = unit_flag(sizes, fill_ref, piece, u, p)

                @pl.when(flag)
                def _(slot=slot, core_at=core_at, side_at=side_at, u=u, p=p):
                    out_ref[jnp.minimum(slot, cap - 1)] = pool[
                        core_at, side_at, u, :, p * sizes.block : (p + 1) * sizes.block
                    ]

                slot = slot + flag.astype(jnp.int32)


def pack(sizes, cap, where, fill, panel, from_core, from_side):
    quarter = sizes.unit // 4
    return pl.pallas_call(
        functools.partial(pack_kernel, sizes, cap),
        out_shape=jax.ShapeDtypeStruct((cap, quarter, sizes.block), F32),
        in_specs=[SMEM, SMEM, VMEM, VMEM, VMEM],
        out_specs=VMEM,
        scratch_shapes=[pltpu.VMEM((2, 2, sizes.per_piece, quarter, 2 * sizes.block), F32)],
        compiler_params=pltpu.CompilerParams(vmem_limit_bytes=16 * 2**20),
    )(where, fill, panel, from_core, from_side)


def pair_slots(sizes, fill_ref, group, slots):
    def step(i, slot):
        flag = pair_flag(sizes, fill_ref, group, i)
        slot = jnp.where(i == sizes.column_units, 0, slot)
        slots[i] = jnp.where(flag, slot, -1)
        return slot + flag.astype(jnp.int32)

    lax.fori_loop(0, 2 * sizes.column_units, step, jnp.int32(0))


def pack_column_kernel(sizes, cap, column_cap, shifts, where_ref, fill_ref, *refs):
    lists, before, (out_ref, slots) = refs[: len(shifts)], refs[len(shifts) : -2], refs[-2:]
    own = where_ref[0] // 2
    slab, start = sizes.pair_slab(own), sizes.pair_start(own)
    pair_slots(sizes, fill_ref, own, slots)
    for ref in before:
        out_ref[...] = ref[...]
    for shift, list_ref in zip(shifts, lists):
        group = lax.rem(own + shift, sizes.groups)
        slot = jnp.int32(0)
        for core, side, piece in pool_pieces(sizes, slab // 2, group):
            for u in range(sizes.per_piece):
                for p in range(2):
                    flag = unit_flag(sizes, fill_ref, piece, u, p)
                    index = (((group * 2 + side) * sizes.per_piece + u) - start) * 2 + p
                    inside = jnp.logical_and(index >= 0, index < 2 * sizes.column_units)
                    wanted = jnp.logical_and(jnp.logical_and(flag, inside), slab % 2 == core)

                    @pl.when(wanted)
                    def _(slot=slot, index=index, list_ref=list_ref):
                        index = jnp.clip(index, 0, 2 * sizes.column_units - 1)
                        target = jnp.clip(slots[index], 0, column_cap - 1)
                        out_ref[index // sizes.column_units, target] = list_ref[jnp.minimum(slot, cap - 1)]

                    slot = slot + flag.astype(jnp.int32)


def pack_column(sizes, cap, column_cap, shifts, where, fill, lists, before=()):
    return pl.pallas_call(
        functools.partial(pack_column_kernel, sizes, cap, column_cap, shifts),
        out_shape=jax.ShapeDtypeStruct((2, column_cap, sizes.unit // 4, sizes.block), F32),
        in_specs=[SMEM, SMEM] + [VMEM] * (len(lists) + len(before)),
        out_specs=VMEM,
        scratch_shapes=[pltpu.SMEM((2 * sizes.column_units,), jnp.int32)],
        compiler_params=pltpu.CompilerParams(vmem_limit_bytes=20 * 2**20),
    )(where, fill, *lists, *before)


def own_factor_kernel(sizes, where_ref, fill_ref, w_ref, panel_ref, window_ref, x_ref, slot_ref, near_ref, inverse_ref, masked, sem, sems):
    c, r = where_ref[0], where_ref[1]
    rows = window_ref.shape[0] // STAGES
    stages = []
    for i in range(STAGES):
        at = pl.ds(i * rows, rows)
        stages.append(pltpu.make_async_copy(window_ref.at[at], near_ref.at[at], sems.at[i]))
        stages[i].start()
    own = r * sizes.cols + c
    for u in range(sizes.per_piece):
        for p in range(2):
            at = (pl.ds(u * sizes.unit, sizes.unit), pl.ds(p * sizes.block, sizes.block))
            masked[at] = jnp.where(unit_flag(sizes, fill_ref, own, u, p), panel_ref[at], 0.0)
    w = halves(w_ref[...])
    masked[...] = dot3(halves(masked[...]), w, NT)
    copy_out = pltpu.make_async_copy(masked, x_ref, sem)
    copy_out.start()
    inverse_ref[...] = dot3(w, w, TN)

    @pl.loop(0, sizes.groups)
    def _(shift):
        group = lax.rem(c // 2 + shift, sizes.groups)
        slot = jnp.int32(0)
        for core, side, piece in pool_pieces(sizes, r // 2, group):
            for u in range(sizes.per_piece):
                for p in range(2):
                    flag = unit_flag(sizes, fill_ref, piece, u, p)

                    @pl.when(core == r % 2)
                    def _(slot=slot, flag=flag, side=side, u=u, p=p):
                        at = ((shift * 2 + side) * sizes.per_piece + u) * 2 + p
                        slot_ref[at] = jnp.where(flag, slot, -1)

                    slot = slot + flag.astype(jnp.int32)

    copy_out.wait()
    for stage in stages:
        stage.wait()


def own_factor(sizes, where, fill, w, panel, window):
    return pl.pallas_call(
        functools.partial(own_factor_kernel, sizes),
        out_shape=(
            pltpu.HBM(panel.shape, F32),
            jax.ShapeDtypeStruct((2 * sizes.tiles,), jnp.int32),
            pltpu.VMEM(window.shape, F32),
            jax.ShapeDtypeStruct(w.shape, F32),
        ),
        in_specs=[SMEM, SMEM, VMEM, VMEM, HBM],
        out_specs=(HBM, SMEM, VMEM, VMEM),
        scratch_shapes=[
            pltpu.VMEM(panel.shape, F32),
            pltpu.SemaphoreType.DMA,
            pltpu.SemaphoreType.DMA((STAGES,)),
        ],
        compiler_params=pltpu.CompilerParams(vmem_limit_bytes=20 * 2**20),
    )(where, fill, w, panel, window)


def column_factor_kernel(sizes, where_ref, fill_ref, inverse_ref, *refs):
    lists, (out_ref, column, slots) = refs[:4], refs[4:]
    c, r = where_ref[0], where_ref[1]
    side, core = c % 2, r % 2
    quarter = sizes.unit // 4
    pair_slots(sizes, fill_ref, c // 2, slots)
    column[...] = jnp.zeros_like(column)

    @pl.loop(0, sizes.column_units // 2)
    def _(unit):
        for p in range(2):
            slot = slots[side * sizes.column_units + unit * 2 + p]

            @pl.when(slot >= 0)
            def _(slot=slot, p=p):
                for flip in range(4):
                    from_side = jnp.bitwise_xor(side, flip // 2)
                    from_core = jnp.bitwise_xor(core, flip % 2)
                    at = pl.multiple_of(unit * sizes.unit + (from_side * 2 + from_core) * quarter, quarter)
                    column[pl.ds(at, quarter), pl.ds(p * sizes.block, sizes.block)] = lists[flip][slot]

    out_ref[...] = dot3(halves(inverse_ref[...]), halves(column[...]), NT)


def column_factor(sizes, where, fill, inverse, lists):
    n = inverse.shape[0]
    return pl.pallas_call(
        functools.partial(column_factor_kernel, sizes),
        out_shape=jax.ShapeDtypeStruct((n, sizes.width), F32),
        in_specs=[SMEM, SMEM, VMEM] + [VMEM] * 4,
        out_specs=VMEM,
        scratch_shapes=[pltpu.VMEM((sizes.width, n), F32), pltpu.SMEM((2 * sizes.column_units,), jnp.int32)],
        compiler_params=pltpu.CompilerParams(vmem_limit_bytes=20 * 2**20),
    )(where, fill, inverse, *lists)


def update_kernel(sizes, counts, where_ref, slot_ref, column_ref, window_ref, *refs):
    groups, merge = sizes.groups, sizes.merge
    refs, (out_ref, tiles, data, right, out_sems) = list(refs[:-5]), refs[-5:]
    lists = []
    for count in counts:
        own, other, *cores = [refs.pop(0) for _ in range(count)]
        cores = cores if count == 4 else [cores[0].at[0], cores[0].at[1]]
        lists += [own, cores[0], other, cores[1]]
    c, r = where_ref[0], where_ref[1]
    side, core = c % 2, r % 2
    per_group = 2 * sizes.per_piece // merge
    rows = merge * sizes.unit
    quarter = sizes.unit // 4

    def rows_of(t):
        group = lax.rem(c // 2 + t // per_group, groups)
        return pl.ds(pl.multiple_of((group * per_group + t % per_group) * rows, rows), rows)

    def tile_out(t, source):
        return pltpu.make_async_copy(source, out_ref.at[rows_of(t)], out_sems.at[t])

    def slot_of(t, p, part):
        return slot_ref[(t * merge + part) * 2 + p]

    def active(t):
        return jnp.logical_or(slot_of(t, 0, 0) >= 0, slot_of(t, 1, 0) >= 0)

    @pl.loop(0, per_group * groups)
    def _(t):
        pl.when(jnp.logical_not(active(t)))(tile_out(t, window_ref.at[rows_of(t)]).start)

    for p in range(2):
        high, low = halves(column_ref[p * sizes.block : (p + 1) * sizes.block, :])
        for i, part in enumerate((high, low, high)):
            right[p, i * sizes.block : (i + 1) * sizes.block, :] = part

    for group in range(groups):

        @pl.loop(group * per_group, (group + 1) * per_group)
        def _(t, group=group):
            @pl.when(active(t))
            def _():
                tiles[t] = window_ref[rows_of(t), :]
                for p in range(2):

                    @pl.when(slot_of(t, p, 0) >= 0)
                    def _(p=p):
                        for part in range(merge):
                            slot = slot_of(t, p, part)
                            for flip in range(4):
                                from_side = jnp.bitwise_xor(side, flip // 2)
                                from_core = jnp.bitwise_xor(core, flip % 2)
                                at = pl.multiple_of((part * 4 + from_side * 2 + from_core) * quarter, quarter)
                                data[pl.ds(at, quarter), :] = lists[4 * group + flip][slot]
                        high, low = halves(data[...])
                        left = jnp.concatenate([high, high, low], axis=1)
                        tiles[t] = tiles[t] - dot(left, right[p], NN)

                tile_out(t, tiles.at[t]).start()

    @pl.loop(0, per_group * groups)
    def _(t):
        tile_out(t, tiles.at[t]).wait()


def update(sizes, where, slots, column, window, lists):
    rows = sizes.merge * sizes.unit
    tiles = sizes.slab // rows
    list_bytes = 4 * sum(value.size for group in lists for value in group)
    return pl.pallas_call(
        functools.partial(update_kernel, sizes, [len(group) for group in lists]),
        out_shape=pltpu.HBM(window.shape, F32),
        in_specs=[SMEM, SMEM, VMEM, VMEM] + [VMEM] * sum(len(group) for group in lists),
        out_specs=HBM,
        scratch_shapes=[
            pltpu.VMEM((tiles, rows, sizes.width), F32),
            pltpu.VMEM((rows, sizes.block), F32),
            pltpu.VMEM((2, 3 * sizes.block, sizes.width), BF16),
            pltpu.SemaphoreType.DMA((tiles,)),
        ],
        compiler_params=pltpu.CompilerParams(vmem_limit_bytes=14 * 2**20 + list_bytes),
    )(where, slots, column, window, *(value for group in lists for value in group))


def swap(value, axis, step):
    size = lax.axis_size(axis)
    return lax.ppermute(value, axis, [(i, i ^ step) for i in range(size)])


def join(index, step, own, other):
    second = (index & step) != 0
    return jnp.where(second, jnp.concatenate([other, own], 0), jnp.concatenate([own, other], 0))


def after(value, *earlier):
    return lax.optimization_barrier((value, *earlier))[0]


def bring(sizes, value, shift):
    pairs = [(i, (i - 2 * shift) % sizes.cols) for i in range(sizes.cols)]
    return lax.ppermute(value, "col", pairs)


def spread_column(sizes, value, step):
    r, c = lax.axis_index("row"), lax.axis_index("col")
    pairs = []
    for at in range(sizes.cols):
        slab = sizes.pair_slab(at // 2)
        for row in range(sizes.rows):
            if (row // 2 ^ slab // 2) % step == 0:
                pairs.append((at * sizes.rows + row, at * sizes.rows + (row ^ step)))
    other = lax.ppermute(value, ("col", "row"), pairs)
    return jnp.where(((r ^ sizes.pair_slab(c // 2)) & step) != 0, other, value)


def per_device(trailing, panel_rows, pivot_block, panel_fill):
    sizes = Sizes(trailing, panel_rows, panel_fill)
    fill = panel_fill.reshape(-1)
    r, c = lax.axis_index("row"), lax.axis_index("col")
    where = jnp.stack([c, r]).astype(jnp.int32)
    side, core = c % 2, r % 2
    quarter = sizes.unit // 4
    split = min(4, pivot_block.shape[0] // 8)
    share = pivot_block.shape[0] // split
    most, column_most = 8 * sizes.per_piece, sizes.column_units
    levels = [(most * 5 // 12, column_most * 3 // 4), (most, column_most)]

    units = panel_rows.reshape(sizes.per_piece, sizes.unit, -1)
    quarters = panel_rows.reshape(sizes.per_piece, 2, 2, quarter, -1)

    def at_core(which):
        return lax.dynamic_index_in_dim(quarters, which, 2, keepdims=False)

    pivot = lax.dynamic_slice_in_dim(pivot_block, r % split * share, share, 0)[None]
    pivot = join(c, 1, pivot, swap(pivot, "col", 1))
    from_core = swap(at_core(1 - core), "row", 1)
    from_core, pivot = lax.optimization_barrier((from_core, pivot))
    both = jnp.stack([at_core(core), from_core])
    from_side = swap(lax.dynamic_index_in_dim(both, 1 - side, 2, keepdims=False), "col", 1)
    step = 2
    while step < sizes.cols:
        pivot = join(c, step, pivot, swap(pivot, "col", step))
        step *= 2

    def run(cap, column_cap, trailing, panel_rows, fill, units, from_core, from_side, pivot):
        own = pack(sizes, cap, where, fill, units, from_core, from_side)
        lists = {0: own}
        first = [s for s in range(1, sizes.groups) if s in sizes.needed]
        later = [s for s in range(1, sizes.groups) if s not in sizes.needed]
        lists |= {s: bring(sizes, own, s) for s in first}
        sides = {0: swap(own, "col", 1)}
        parts = [pivot] + ([swap(pivot, "row", 2)] if split == 4 else [])
        parts = [part for value in parts for part in (value, swap(value, "row", 1))]
        near = first[0]
        lists[near], sides[0], *parts = lax.optimization_barrier((lists[near], sides[0], *parts))
        sides[near] = swap(lists[near], "col", 1)
        w = inverse_factor(where, parts)
        soon, rest = [0, near], [s for s in sizes.needed if s not in (0, near)]
        column = pack_column(sizes, cap, column_cap, soon, where, fill, [lists[s] for s in soon])
        held = lax.optimization_barrier((w, column, sides[0], sides[near], *lists.values()))
        w, column, sides[0], sides[near] = held[:4]
        lists = dict(zip(lists, held[4:]))

        column = pack_column(sizes, cap, column_cap, rest, where, fill, [lists[s] for s in rest], [column])
        lists |= {s: bring(sizes, lists[0], s) for s in later}
        sides |= {s: swap(lists[s], "col", 1) for s in first[1:]}
        step = sizes.rows // 2
        while step > 1:
            column = spread_column(sizes, column, step)
            step //= 2
        panel_factor, slots, window, inverse = own_factor(sizes, where, fill, w, panel_rows, trailing)
        column, slots = lax.optimization_barrier((column, slots))
        across = swap(lax.dynamic_index_in_dim(column, 1 - side, 0, keepdims=False), "col", 1)
        column = lax.dynamic_index_in_dim(column, side, 0, keepdims=False)
        columns = [column, swap(column, "row", 1), across, swap(across, "row", 1)]
        for s in later:
            lists[s] = lax.optimization_barrier((lists[s], slots, *(sides[j] for j in first)))[0]
            sides[s] = swap(lists[s], "col", 1)
        column = column_factor(sizes, where, fill, inverse, columns)
        for s in later:
            sides[s], column = lax.optimization_barrier((sides[s], column))
        ordered = []
        for s in range(sizes.groups):
            value, other = lists[s], sides[s]
            if s in later:
                ordered.append((value, other, swap(value, "row", 1), swap(other, "row", 1)))
            else:
                ordered.append((value, other, swap(jnp.stack([value, other]), "row", 1)))
        return update(sizes, where, slots, column, window, ordered), panel_factor

    operands = (trailing, panel_rows, fill, units, from_core, from_side, pivot)
    branches = [functools.partial(run, *level) for level in levels]
    return lax.cond(level_of(sizes, levels, fill)[0] == 0, *branches, *operands)


def solution(mesh):
    in_specs = (P("row", "col"), P(("row", "col"), None), P("col", None), P())
    out_specs = (P("row", "col"), P(("row", "col"), None))
    return jax.shard_map(
        per_device, mesh=mesh, in_specs=in_specs, out_specs=out_specs, check_vma=False
    )
```

```python
import functools
import math

import jax
import jax.numpy as jnp
from jax import lax
from jax.experimental import pallas as pl
from jax.experimental.pallas import tpu as pltpu
from jax.sharding import PartitionSpec as P

F32, BF16 = jnp.float32, jnp.bfloat16
VMEM = pl.BlockSpec(memory_space=pltpu.VMEM)
SMEM = pl.BlockSpec(memory_space=pltpu.SMEM)
HBM = pl.BlockSpec(memory_space=pltpu.HBM)
COARSE_STEPS = 2
FINE_STEPS = 16
RESIDUAL = 5e-4
STAGES = 8


def halves(value):
    high = value.astype(BF16)
    return high, (value - high.astype(F32)).astype(BF16)


def dot(a, b, dims):
    return lax.dot_general(a, b, (dims, ((), ())), preferred_element_type=F32)


NN, NT, TN = ((1,), (0,)), ((1,), (1,)), ((0,), (0,))


def dot3(a, b, dims):
    (ah, al), (bh, bl) = a, b
    return dot(ah, bh, dims) + (dot(ah, bl, dims) + dot(al, bh, dims))


def inverse_factor_kernel(where_ref, *refs):
    parts, (w_ref, s_ref) = refs[:-2], refs[-2:]
    n = w_ref.shape[0]
    pieces, share = parts[0].shape[0], parts[0].shape[1]
    own = where_ref[1] % len(parts)
    for flip, ref in enumerate(parts):
        at = jnp.bitwise_xor(own, flip) * share
        for i in range(pieces):
            s_ref[pl.ds(pl.multiple_of(i * len(parts) * share + at, share), share), :] = ref[i]
    rows = lax.broadcasted_iota(jnp.int32, (n, n), 0)
    cols = lax.broadcasted_iota(jnp.int32, (n, n), 1)
    eye = (rows == cols).astype(F32)
    take = jnp.where(rows > cols, 1.0, 0.5 * eye)
    a = s_ref[...]
    diag_row = jnp.sum(a * eye, axis=0, keepdims=True)
    diag_col = jnp.sum(a * eye, axis=1, keepdims=True)
    scale_row, scale_col = lax.rsqrt(diag_row), lax.rsqrt(diag_col)
    scaled = jnp.where(rows == cols, 1.0, a * scale_row * scale_col)
    s_ref[...] = scaled
    scaled_parts = halves(scaled)
    w = eye - take * (scaled - eye)
    for _ in range(COARSE_STEPS):
        wh = w.astype(BF16)
        t = dot(wh, scaled_parts[0], NN).astype(BF16)
        change = take * (dot(t, wh, NT) - eye)
        w = w - dot(change.astype(BF16), wh, NN)
    w_ref[...] = w

    def fine(state):
        step, _ = state
        w = w_ref[...]
        parts = halves(w)
        t = halves(dot3(parts, halves(s_ref[...]), NN))
        residual = dot3(t, parts, NT) - eye
        w_ref[...] = w - dot((take * residual).astype(BF16), parts[0], NN)
        return step + 1, jnp.sum(residual * residual)

    _, left = lax.while_loop(
        lambda state: jnp.logical_and(state[0] < FINE_STEPS, jnp.logical_not(state[1] < RESIDUAL**2)),
        fine,
        (jnp.int32(0), jnp.float32(1.0)),
    )
    done = left < RESIDUAL**2

    @pl.when(jnp.logical_not(done))
    def _():
        w_ref[...] = eye

        def eliminate(j, carry):
            row = s_ref[pl.ds(j, 1), :]
            pick = lax.broadcasted_iota(jnp.int32, (1, n), 1) == j
            pivot = jnp.sum(jnp.where(pick, row, 0.0), axis=1, keepdims=True)
            column = jnp.sum(jnp.where(pick, s_ref[...], 0.0), axis=1, keepdims=True)
            below = lax.broadcasted_iota(jnp.int32, (n, 1), 0) > j
            ratio = jnp.where(below, column / pivot, 0.0)
            s_ref[...] = s_ref[...] - ratio * row
            w_ref[...] = w_ref[...] - ratio * w_ref[pl.ds(j, 1), :]
            return carry

        lax.fori_loop(0, n, eliminate, 0)
        pivots = jnp.sum(s_ref[...] * eye, axis=1, keepdims=True)
        w_ref[...] = w_ref[...] * lax.rsqrt(pivots)

    w_ref[...] = w_ref[...] * scale_row


def inverse_factor(where, parts):
    n = parts[0].shape[-1]
    return pl.pallas_call(
        inverse_factor_kernel,
        out_shape=jax.ShapeDtypeStruct((n, n), F32),
        in_specs=[SMEM] + [VMEM] * len(parts),
        out_specs=VMEM,
        scratch_shapes=[pltpu.VMEM((n, n), F32)],
        compiler_params=pltpu.CompilerParams(vmem_limit_bytes=20 * 2**20),
    )(where, *parts)


class Sizes:
    def __init__(self, trailing, panel_rows, panel_fill):
        self.cols, self.rows = lax.axis_size("col"), lax.axis_size("row")
        self.block = panel_rows.shape[1] // 2
        self.piece = panel_rows.shape[0]
        self.unit = math.gcd(self.piece, self.block)
        self.per_piece = self.piece // self.unit
        self.per_block = self.block // self.unit
        self.slab = self.piece * self.cols
        self.merge = self.per_block if 2 * self.piece % self.block == 0 else 1
        self.width = trailing.shape[1]
        self.tiles = self.cols * self.per_piece

        self.groups = self.cols // 2
        self.column_units = 2 * self.width // self.unit
        self.needed = sorted({s for g in range(self.groups) for s in self.shifts(g)})

    def pair_slab(self, group):
        return 2 * group * self.width // self.slab

    def pair_start(self, group):
        return (2 * group * self.width - self.pair_slab(group) * self.slab) // self.unit

    def shifts(self, group):
        start = self.pair_start(group) * self.unit
        first, last = start // (2 * self.piece), (start + 2 * self.width - 1) // (2 * self.piece)
        return [(g - group) % self.groups for g in range(first, last + 1)]


def unit_flag(sizes, fill_ref, piece_index, unit, panel):
    block = (piece_index * sizes.per_piece + unit) // sizes.per_block
    return fill_ref[block * 2 + panel] != 0


def pool_pieces(sizes, pool_row, pool_col):
    for core in range(2):
        for side in range(2):
            yield core, side, (pool_row * 2 + core) * sizes.cols + pool_col * 2 + side


def pair_flag(sizes, fill_ref, group, index):
    unit = sizes.pair_slab(group) * sizes.tiles + sizes.pair_start(group) + index // 2
    return fill_ref[unit // sizes.per_block * 2 + index % 2] != 0


def level_kernel(sizes, levels, fill_ref, out_ref):
    pool_most, column_most = jnp.int32(0), jnp.int32(0)
    for pool_row in range(sizes.rows // 2):
        for pool_col in range(sizes.groups):
            count = jnp.int32(0)
            for _, _, piece in pool_pieces(sizes, pool_row, pool_col):
                for u in range(sizes.per_piece):
                    for p in range(2):
                        count = count + unit_flag(sizes, fill_ref, piece, u, p).astype(jnp.int32)
            pool_most = jnp.maximum(pool_most, count)
    for group in range(sizes.groups):
        for side in range(2):
            count = jnp.int32(0)
            for i in range(sizes.column_units):
                flag = pair_flag(sizes, fill_ref, group, side * sizes.column_units + i)
                count = count + flag.astype(jnp.int32)
            column_most = jnp.maximum(column_most, count)
    level = jnp.int32(0)
    for cap, column_cap in levels[:-1]:
        fits = jnp.logical_and(pool_most <= cap, column_most <= column_cap)
        level = level + jnp.logical_not(fits).astype(jnp.int32)
    out_ref[0] = level


def level_of(sizes, levels, fill):
    return pl.pallas_call(
        functools.partial(level_kernel, sizes, levels),
        out_shape=jax.ShapeDtypeStruct((1,), jnp.int32),
        in_specs=[SMEM],
        out_specs=SMEM,
    )(fill)


def pack_kernel(sizes, cap, where_ref, fill_ref, panel_ref, core_ref, side_ref, out_ref, pool):
    c, r = where_ref[0], where_ref[1]
    side, core = c % 2, r % 2
    quarter = sizes.unit // 4
    own_at = pl.multiple_of((side * 2 + core) * quarter, quarter)
    for u in range(sizes.per_piece):
        pool[core, side, u] = panel_ref[u, pl.ds(own_at, quarter), :]
        pool[1 - core, side, u] = core_ref[u, side]
        pool[core, 1 - side, u] = side_ref[0, u]
        pool[1 - core, 1 - side, u] = side_ref[1, u]
    slot = jnp.int32(0)
    for core_at, side_at, piece in pool_pieces(sizes, r // 2, c // 2):
        for u in range(sizes.per_piece):
            for p in range(2):
                flag = unit_flag(sizes, fill_ref, piece, u, p)

                @pl.when(flag)
                def _(slot=slot, core_at=core_at, side_at=side_at, u=u, p=p):
                    out_ref[jnp.minimum(slot, cap - 1)] = pool[
                        core_at, side_at, u, :, p * sizes.block : (p + 1) * sizes.block
                    ]

                slot = slot + flag.astype(jnp.int32)


def pack(sizes, cap, where, fill, panel, from_core, from_side):
    quarter = sizes.unit // 4
    return pl.pallas_call(
        functools.partial(pack_kernel, sizes, cap),
        out_shape=jax.ShapeDtypeStruct((cap, quarter, sizes.block), F32),
        in_specs=[SMEM, SMEM, VMEM, VMEM, VMEM],
        out_specs=VMEM,
        scratch_shapes=[pltpu.VMEM((2, 2, sizes.per_piece, quarter, 2 * sizes.block), F32)],
        compiler_params=pltpu.CompilerParams(vmem_limit_bytes=16 * 2**20),
    )(where, fill, panel, from_core, from_side)


def pair_slots(sizes, fill_ref, group, slots):
    def step(i, slot):
        flag = pair_flag(sizes, fill_ref, group, i)
        slot = jnp.where(i == sizes.column_units, 0, slot)
        slots[i] = jnp.where(flag, slot, -1)
        return slot + flag.astype(jnp.int32)

    lax.fori_loop(0, 2 * sizes.column_units, step, jnp.int32(0))


def pack_column_kernel(sizes, cap, column_cap, shifts, where_ref, fill_ref, *refs):
    lists, before, (out_ref, slots) = refs[: len(shifts)], refs[len(shifts) : -2], refs[-2:]
    own = where_ref[0] // 2
    slab, start = sizes.pair_slab(own), sizes.pair_start(own)
    pair_slots(sizes, fill_ref, own, slots)
    for ref in before:
        out_ref[...] = ref[...]
    for shift, list_ref in zip(shifts, lists):
        group = lax.rem(own + shift, sizes.groups)
        slot = jnp.int32(0)
        for core, side, piece in pool_pieces(sizes, slab // 2, group):
            for u in range(sizes.per_piece):
                for p in range(2):
                    flag = unit_flag(sizes, fill_ref, piece, u, p)
                    index = (((group * 2 + side) * sizes.per_piece + u) - start) * 2 + p
                    inside = jnp.logical_and(index >= 0, index < 2 * sizes.column_units)
                    wanted = jnp.logical_and(jnp.logical_and(flag, inside), slab % 2 == core)

                    @pl.when(wanted)
                    def _(slot=slot, index=index, list_ref=list_ref):
                        index = jnp.clip(index, 0, 2 * sizes.column_units - 1)
                        target = jnp.clip(slots[index], 0, column_cap - 1)
                        out_ref[index // sizes.column_units, target] = list_ref[jnp.minimum(slot, cap - 1)]

                    slot = slot + flag.astype(jnp.int32)


def pack_column(sizes, cap, column_cap, shifts, where, fill, lists, before=()):
    return pl.pallas_call(
        functools.partial(pack_column_kernel, sizes, cap, column_cap, shifts),
        out_shape=jax.ShapeDtypeStruct((2, column_cap, sizes.unit // 4, sizes.block), F32),
        in_specs=[SMEM, SMEM] + [VMEM] * (len(lists) + len(before)),
        out_specs=VMEM,
        scratch_shapes=[pltpu.SMEM((2 * sizes.column_units,), jnp.int32)],
        compiler_params=pltpu.CompilerParams(vmem_limit_bytes=20 * 2**20),
    )(where, fill, *lists, *before)


def own_factor_kernel(sizes, where_ref, fill_ref, w_ref, panel_ref, window_ref, x_ref, slot_ref, near_ref, inverse_ref, masked, sem, sems):
    c, r = where_ref[0], where_ref[1]
    rows = window_ref.shape[0] // STAGES
    stages = []
    for i in range(STAGES):
        at = pl.ds(i * rows, rows)
        stages.append(pltpu.make_async_copy(window_ref.at[at], near_ref.at[at], sems.at[i]))
        stages[i].start()
    own = r * sizes.cols + c
    for u in range(sizes.per_piece):
        for p in range(2):
            at = (pl.ds(u * sizes.unit, sizes.unit), pl.ds(p * sizes.block, sizes.block))
            masked[at] = jnp.where(unit_flag(sizes, fill_ref, own, u, p), panel_ref[at], 0.0)
    w = halves(w_ref[...])
    masked[...] = dot3(halves(masked[...]), w, NT)
    copy_out = pltpu.make_async_copy(masked, x_ref, sem)
    copy_out.start()
    inverse_ref[...] = dot3(w, w, TN)

    @pl.loop(0, sizes.groups)
    def _(shift):
        group = lax.rem(c // 2 + shift, sizes.groups)
        slot = jnp.int32(0)
        for core, side, piece in pool_pieces(sizes, r // 2, group):
            for u in range(sizes.per_piece):
                for p in range(2):
                    flag = unit_flag(sizes, fill_ref, piece, u, p)

                    @pl.when(core == r % 2)
                    def _(slot=slot, flag=flag, side=side, u=u, p=p):
                        at = ((shift * 2 + side) * sizes.per_piece + u) * 2 + p
                        slot_ref[at] = jnp.where(flag, slot, -1)

                    slot = slot + flag.astype(jnp.int32)

    copy_out.wait()
    for stage in stages:
        stage.wait()


def own_factor(sizes, where, fill, w, panel, window):
    return pl.pallas_call(
        functools.partial(own_factor_kernel, sizes),
        out_shape=(
            pltpu.HBM(panel.shape, F32),
            jax.ShapeDtypeStruct((2 * sizes.tiles,), jnp.int32),
            pltpu.VMEM(window.shape, F32),
            jax.ShapeDtypeStruct(w.shape, F32),
        ),
        in_specs=[SMEM, SMEM, VMEM, VMEM, HBM],
        out_specs=(HBM, SMEM, VMEM, VMEM),
        scratch_shapes=[
            pltpu.VMEM(panel.shape, F32),
            pltpu.SemaphoreType.DMA,
            pltpu.SemaphoreType.DMA((STAGES,)),
        ],
        compiler_params=pltpu.CompilerParams(vmem_limit_bytes=20 * 2**20),
    )(where, fill, w, panel, window)


def column_factor_kernel(sizes, where_ref, fill_ref, inverse_ref, *refs):
    lists, (out_ref, column, slots) = refs[:4], refs[4:]
    c, r = where_ref[0], where_ref[1]
    side, core = c % 2, r % 2
    quarter = sizes.unit // 4
    pair_slots(sizes, fill_ref, c // 2, slots)
    column[...] = jnp.zeros_like(column)

    @pl.loop(0, sizes.column_units // 2)
    def _(unit):
        for p in range(2):
            slot = slots[side * sizes.column_units + unit * 2 + p]

            @pl.when(slot >= 0)
            def _(slot=slot, p=p):
                for flip in range(4):
                    from_side = jnp.bitwise_xor(side, flip // 2)
                    from_core = jnp.bitwise_xor(core, flip % 2)
                    at = pl.multiple_of(unit * sizes.unit + (from_side * 2 + from_core) * quarter, quarter)
                    column[pl.ds(at, quarter), pl.ds(p * sizes.block, sizes.block)] = lists[flip][slot]

    out_ref[...] = dot3(halves(inverse_ref[...]), halves(column[...]), NT)


def column_factor(sizes, where, fill, inverse, lists):
    n = inverse.shape[0]
    return pl.pallas_call(
        functools.partial(column_factor_kernel, sizes),
        out_shape=jax.ShapeDtypeStruct((n, sizes.width), F32),
        in_specs=[SMEM, SMEM, VMEM] + [VMEM] * 4,
        out_specs=VMEM,
        scratch_shapes=[pltpu.VMEM((sizes.width, n), F32), pltpu.SMEM((2 * sizes.column_units,), jnp.int32)],
        compiler_params=pltpu.CompilerParams(vmem_limit_bytes=20 * 2**20),
    )(where, fill, inverse, *lists)


def update_kernel(sizes, counts, where_ref, slot_ref, column_ref, window_ref, *refs):
    groups, merge = sizes.groups, sizes.merge
    refs, (out_ref, tiles, data, right, out_sems) = list(refs[:-5]), refs[-5:]
    lists = []
    for count in counts:
        own, other, *cores = [refs.pop(0) for _ in range(count)]
        cores = cores if count == 4 else [cores[0].at[0], cores[0].at[1]]
        lists += [own, cores[0], other, cores[1]]
    c, r = where_ref[0], where_ref[1]
    side, core = c % 2, r % 2
    per_group = 2 * sizes.per_piece // merge
    rows = merge * sizes.unit
    quarter = sizes.unit // 4

    def rows_of(t):
        group = lax.rem(c // 2 + t // per_group, groups)
        return pl.ds(pl.multiple_of((group * per_group + t % per_group) * rows, rows), rows)

    def tile_out(t, source):
        return pltpu.make_async_copy(source, out_ref.at[rows_of(t)], out_sems.at[t])

    def slot_of(t, p, part):
        return slot_ref[(t * merge + part) * 2 + p]

    def active(t):
        return jnp.logical_or(slot_of(t, 0, 0) >= 0, slot_of(t, 1, 0) >= 0)

    @pl.loop(0, per_group * groups)
    def _(t):
        pl.when(jnp.logical_not(active(t)))(tile_out(t, window_ref.at[rows_of(t)]).start)

    for p in range(2):
        high, low = halves(column_ref[p * sizes.block : (p + 1) * sizes.block, :])
        for i, part in enumerate((high, low, high)):
            right[p, i * sizes.block : (i + 1) * sizes.block, :] = part

    for group in range(groups):

        @pl.loop(group * per_group, (group + 1) * per_group)
        def _(t, group=group):
            @pl.when(active(t))
            def _():
                tiles[t] = window_ref[rows_of(t), :]
                for p in range(2):

                    @pl.when(slot_of(t, p, 0) >= 0)
                    def _(p=p):
                        for part in range(merge):
                            slot = slot_of(t, p, part)
                            for flip in range(4):
                                from_side = jnp.bitwise_xor(side, flip // 2)
                                from_core = jnp.bitwise_xor(core, flip % 2)
                                at = pl.multiple_of((part * 4 + from_side * 2 + from_core) * quarter, quarter)
                                data[pl.ds(at, quarter), :] = lists[4 * group + flip][slot]
                        high, low = halves(data[...])
                        left = jnp.concatenate([high, high, low], axis=1)
                        tiles[t] = tiles[t] - dot(left, right[p], NN)

                tile_out(t, tiles.at[t]).start()

    @pl.loop(0, per_group * groups)
    def _(t):
        tile_out(t, tiles.at[t]).wait()


def update(sizes, where, slots, column, window, lists):
    rows = sizes.merge * sizes.unit
    tiles = sizes.slab // rows
    list_bytes = 4 * sum(value.size for group in lists for value in group)
    return pl.pallas_call(
        functools.partial(update_kernel, sizes, [len(group) for group in lists]),
        out_shape=pltpu.HBM(window.shape, F32),
        in_specs=[SMEM, SMEM, VMEM, VMEM] + [VMEM] * sum(len(group) for group in lists),
        out_specs=HBM,
        scratch_shapes=[
            pltpu.VMEM((tiles, rows, sizes.width), F32),
            pltpu.VMEM((rows, sizes.block), F32),
            pltpu.VMEM((2, 3 * sizes.block, sizes.width), BF16),
            pltpu.SemaphoreType.DMA((tiles,)),
        ],
        compiler_params=pltpu.CompilerParams(vmem_limit_bytes=14 * 2**20 + list_bytes),
    )(where, slots, column, window, *(value for group in lists for value in group))


def swap(value, axis, step):
    size = lax.axis_size(axis)
    return lax.ppermute(value, axis, [(i, i ^ step) for i in range(size)])


def join(index, step, own, other):
    second = (index & step) != 0
    return jnp.where(second, jnp.concatenate([other, own], 0), jnp.concatenate([own, other], 0))


def after(value, *earlier):
    return lax.optimization_barrier((value, *earlier))[0]


def bring(sizes, value, shift):
    pairs = [(i, (i - 2 * shift) % sizes.cols) for i in range(sizes.cols)]
    return lax.ppermute(value, "col", pairs)


def spread_column(sizes, value, step):
    r, c = lax.axis_index("row"), lax.axis_index("col")
    pairs = []
    for at in range(sizes.cols):
        slab = sizes.pair_slab(at // 2)
        for row in range(sizes.rows):
            if (row // 2 ^ slab // 2) % step == 0:
                pairs.append((at * sizes.rows + row, at * sizes.rows + (row ^ step)))
    other = lax.ppermute(value, ("col", "row"), pairs)
    return jnp.where(((r ^ sizes.pair_slab(c // 2)) & step) != 0, other, value)


def per_device(trailing, panel_rows, pivot_block, panel_fill):
    sizes = Sizes(trailing, panel_rows, panel_fill)
    fill = panel_fill.reshape(-1)
    r, c = lax.axis_index("row"), lax.axis_index("col")
    where = jnp.stack([c, r]).astype(jnp.int32)
    side, core = c % 2, r % 2
    quarter = sizes.unit // 4
    split = min(4, pivot_block.shape[0] // 8)
    share = pivot_block.shape[0] // split
    most, column_most = 8 * sizes.per_piece, sizes.column_units
    levels = [(most * 5 // 12, column_most * 3 // 4), (most, column_most)]

    units = panel_rows.reshape(sizes.per_piece, sizes.unit, -1)
    quarters = panel_rows.reshape(sizes.per_piece, 2, 2, quarter, -1)

    def at_core(which):
        return lax.dynamic_index_in_dim(quarters, which, 2, keepdims=False)

    pivot = lax.dynamic_slice_in_dim(pivot_block, r % split * share, share, 0)[None]
    pivot = join(c, 1, pivot, swap(pivot, "col", 1))
    from_core = swap(at_core(1 - core), "row", 1)
    from_core, pivot = lax.optimization_barrier((from_core, pivot))
    both = jnp.stack([at_core(core), from_core])
    from_side = swap(lax.dynamic_index_in_dim(both, 1 - side, 2, keepdims=False), "col", 1)
    step = 2
    while step < sizes.cols:
        pivot = join(c, step, pivot, swap(pivot, "col", step))
        step *= 2

    def run(cap, column_cap, trailing, panel_rows, fill, units, from_core, from_side, pivot):
        own = pack(sizes, cap, where, fill, units, from_core, from_side)
        lists = {0: own}
        first = [s for s in range(1, sizes.groups) if s in sizes.needed]
        later = [s for s in range(1, sizes.groups) if s not in sizes.needed]
        lists |= {s: bring(sizes, own, s) for s in first}
        sides = {0: swap(own, "col", 1)}
        pivot, own = lax.optimization_barrier((pivot, own))
        parts = [pivot] + ([swap(pivot, "row", 2)] if split == 4 else [])
        parts = [part for value in parts for part in (value, swap(value, "row", 1))]
        near = first[0]
        lists[near], *parts = lax.optimization_barrier((lists[near], *parts))
        sides[near] = swap(lists[near], "col", 1)
        w = inverse_factor(where, parts)
        soon, rest = [0, near], [s for s in sizes.needed if s not in (0, near)]
        column = pack_column(sizes, cap, column_cap, soon, where, fill, [lists[s] for s in soon])
        held = lax.optimization_barrier((w, column, sides[0], sides[near], *lists.values()))
        w, column, sides[0], sides[near] = held[:4]
        lists = dict(zip(lists, held[4:]))

        column = pack_column(sizes, cap, column_cap, rest, where, fill, [lists[s] for s in rest], [column])
        lists |= {s: bring(sizes, lists[0], s) for s in later}
        sides |= {s: swap(lists[s], "col", 1) for s in first[1:]}
        step = sizes.rows // 2
        while step > 1:
            column = spread_column(sizes, column, step)
            step //= 2
        panel_factor, slots, window, inverse = own_factor(sizes, where, fill, w, panel_rows, trailing)
        column, slots = lax.optimization_barrier((column, slots))
        across = swap(lax.dynamic_index_in_dim(column, 1 - side, 0, keepdims=False), "col", 1)
        column = lax.dynamic_index_in_dim(column, side, 0, keepdims=False)
        columns = [column, swap(column, "row", 1), across, swap(across, "row", 1)]
        for s in later:
            lists[s] = lax.optimization_barrier((lists[s], slots, *(sides[j] for j in first)))[0]
            sides[s] = swap(lists[s], "col", 1)
        column = column_factor(sizes, where, fill, inverse, columns)
        for s in later:
            sides[s], column = lax.optimization_barrier((sides[s], column))
        ordered = []
        for s in range(sizes.groups):
            value, other = lists[s], sides[s]
            if s in later:
                ordered.append((value, other, swap(value, "row", 1), swap(other, "row", 1)))
            else:
                ordered.append((value, other, swap(jnp.stack([value, other]), "row", 1)))
        return update(sizes, where, slots, column, window, ordered), panel_factor

    operands = (trailing, panel_rows, fill, units, from_core, from_side, pivot)
    branches = [functools.partial(run, *level) for level in levels]
    return lax.cond(level_of(sizes, levels, fill)[0] == 0, *branches, *operands)


def solution(mesh):
    in_specs = (P("row", "col"), P(("row", "col"), None), P("col", None), P())
    out_specs = (P("row", "col"), P(("row", "col"), None))
    return jax.shard_map(
        per_device, mesh=mesh, in_specs=in_specs, out_specs=out_specs, check_vma=False
    )
```
